32 devices in a mesh: group: 2 (over x), inst: 4 (over z), tp: 4 (over y, core).
Axes of the slice: x: 2, y: 2, z: 4, core: 2. Of those that a mesh axis runs over, the one named last changes fastest.
Arguments:
- queries: bfloat16 [2048, 2048], P(('group', 'inst'), 'tp'), parts along dimension 0, may hold values from -12 to 12
- new_kv: bfloat16 [4, 2048, 256], P('tp', ('group', 'inst')), parts along dimension 1, may hold values from -12 to 12
- kv_pool: bfloat16 [4, 1024, 128, 256], P('tp', ('group', 'inst')), parts along dimension 1, may hold values from -4 to 4
- out_weight: bfloat16 [2048, 8192], P('tp'), may hold values from -0.5 to 0.5
- lengths: int32 [256], P('group'), parts along dimension 0, may hold values from 1 to 4, as said below
- page_table: int32 [256, 4], P(('group', 'inst')), parts along dimension 0, may hold values from 0 to 127, as said below
- migration: int32 [24, 4], P('group'), parts along dimension 0, may hold values from 0 to 31, as said below
Outputs:
- mixed: bfloat16 [2048, 8192], P(('group', 'inst'), 'tp'), parts along dimension 0
The draws below stay inside these ranges and needn't reach their ends.
There are 2 independent parts, one for each index of `group`. The reference program is written for one: setup_inputs(seed, part) draws one part's arguments, and reference() takes and returns one part's arrays. A program takes and returns all parts, laid end to end along the dimension named above; an argument that names none is the same for every part. Nothing has to cross between parts.
Inputs may be any that keep to these rules, and one draw needn't show every extreme that they name: context lengths in whole pages of 128 tokens; some request has 4 pages in every draw. `page_table`: row g lists the pages of request g in the pool of its home instance g // 32; the entries of one instance's requests are all different. `migration`: each row moves one request; each instance hands exactly 3 of its requests to other instances and takes exactly 3 in, into the slots that its own departing requests leave; at most one request goes from one instance to another.
All inputs are finite; a program needn't handle non-finite values.
Results may differ from the reference program's by a relative error of at most 0.0057.
Values may be sent and summed in bfloat16 or wider, within the bound.
No kernel may reach another device: no remote copies, remote signals or barrier semaphores. Data moves between devices by JAX's collectives and lax.ppermute only.
A program may use at most 128 MiB of HBM per device.

```python
import jax
import jax.numpy as jnp
from jax import lax

D = 8192
HD = 128
QH_DEV = 4
PAGE = 128
MAXP = 4
STEPS = 8
MIG = 3
SLOTS = 32
Q_HEADS = 16
KVH = 1
COPIES = 4
INSTANCES = 4
PAGES = 128
REQUESTS = 128


def common_draws(key):
    row_count = REQUESTS * STEPS
    base_key = jax.random.fold_in(key, 0)
    shared = jnp.clip(jax.random.normal(base_key, (row_count, KVH, HD), jnp.float32), -4.0, 4.0)
    return shared


def draw_queries(key, part):
    shared = common_draws(key)
    key = jax.random.fold_in(key, 11)
    row_count = REQUESTS * STEPS
    group_size = Q_HEADS // KVH
    own = jnp.clip(jax.random.normal(key, (row_count, KVH, group_size, HD), jnp.float32), -4.0, 4.0)
    values = 2.0 * (0.5 * shared[:, :, None, :] + own)
    return values.reshape(row_count, Q_HEADS * HD).astype(jnp.bfloat16)


def draw_new_kv(key, part):
    shared = common_draws(key)
    key = jax.random.fold_in(key, 12)
    key_part, value_part = jax.random.split(key)
    row_count = REQUESTS * STEPS
    own = jnp.clip(jax.random.normal(key_part, (row_count, KVH, HD), jnp.float32), -4.0, 4.0)
    values = jnp.clip(jax.random.normal(value_part, (row_count, KVH, HD), jnp.float32), -4.0, 4.0)
    keys_now = 0.5 * shared + own
    stacked = jnp.concatenate([keys_now, values], axis=-1)
    stacked = jnp.transpose(stacked, (1, 0, 2)).astype(jnp.bfloat16)
    return jnp.repeat(stacked, COPIES // KVH, axis=0)


def draw_kv_pool(key, part):
    key = jax.random.fold_in(key, 13)
    shape = (KVH, INSTANCES * PAGES, PAGE, 2 * HD)
    values = jnp.clip(jax.random.normal(key, shape, jnp.float32), -4.0, 4.0)
    return jnp.repeat(values.astype(jnp.bfloat16), COPIES // KVH, axis=0)


def draw_lengths(key, part):
    key = jax.random.fold_in(key, 21)
    level_key, raw_key, forced_key = jax.random.split(key, 3)
    level = jax.random.randint(level_key, (INSTANCES,), 1, MAXP + 1)
    raw_values = jax.random.randint(raw_key, (INSTANCES, SLOTS), 0, MAXP)
    values = (1 + raw_values % level[:, None]).reshape(REQUESTS)
    forced = jax.random.randint(forced_key, (), 0, REQUESTS)
    values = jnp.where(jnp.arange(REQUESTS) == forced, MAXP, values)
    return values.astype(jnp.int32)


def draw_page_table(key, part):
    key = jax.random.fold_in(key, 22)
    keys = jax.random.split(key, INSTANCES)
    orders = jax.vmap(lambda single: jax.random.permutation(single, PAGES))(keys)
    return orders.reshape(REQUESTS, MAXP).astype(jnp.int32)


def draw_migration(key, part):
    key = jax.random.fold_in(key, 23)
    label_key, offset_key, slot_key = jax.random.split(key, 3)
    labels = jax.random.permutation(label_key, INSTANCES).astype(jnp.int32)
    inverse = jnp.argsort(labels).astype(jnp.int32)
    offsets = (jax.random.permutation(offset_key, INSTANCES - 1)[:MIG] + 1).astype(jnp.int32)
    slot_keys = jax.random.split(slot_key, INSTANCES)
    vacated = jax.vmap(lambda single: jax.random.permutation(single, SLOTS)[:MIG])(slot_keys).astype(jnp.int32)
    marked = labels[0]
    shift_by = SLOTS - 1 - vacated[marked, 0]
    is_marked = jnp.arange(INSTANCES, dtype=jnp.int32)[:, None] == marked
    vacated = jnp.where(is_marked, (vacated + shift_by) % SLOTS, vacated).astype(jnp.int32)
    sources = jnp.broadcast_to(jnp.arange(INSTANCES, dtype=jnp.int32)[:, None], (INSTANCES, MIG))
    targets = labels[(inverse[sources] + offsets[None, :]) % INSTANCES]
    target_slots = vacated[targets, jnp.arange(MIG, dtype=jnp.int32)[None, :]]
    rows = jnp.stack([sources, vacated, targets, target_slots], axis=-1)
    return rows.reshape(INSTANCES * MIG, 4).astype(jnp.int32)


def level_of(rng, extent, pieces, smallest, top_value):
    loudness, own = 1.0, jax.random.fold_in(rng, 6)
    for position, shards_of in pieces:
        heights = jnp.exp(jax.random.uniform(jax.random.fold_in(own, position), (shards_of,), jnp.float32, smallest / len(pieces), top_value / len(pieces)))
        loudness = loudness * jnp.repeat(heights, extent[position] // shards_of).reshape([-1 if axis == position else 1 for axis in range(len(extent))])
    return loudness


def gaussian(rng, dims, scale, bound, cuts=(), kind=jnp.bfloat16):
    values = scale * jax.random.normal(rng, dims, jnp.float32)
    if cuts:
        values = values * level_of(rng, dims, cuts, -0.22, 0.18)
    return jnp.clip(values, -bound, bound).astype(kind)


def setup_inputs(seed: int = 0, part: int = 0) -> dict:
    streams_of = jax.random.split(jax.random.key(seed), 8)
    part_splits = jax.random.split(jax.random.fold_in(streams_of[7], part), 8)
    return {
        "queries": draw_queries(jax.random.fold_in(jax.random.fold_in(streams_of[7], part), 71), part),
        "new_kv": draw_new_kv(jax.random.fold_in(jax.random.fold_in(streams_of[7], part), 71), part),
        "kv_pool": draw_kv_pool(jax.random.fold_in(jax.random.fold_in(streams_of[7], part), 71), part),
        "out_weight": gaussian(streams_of[3], (Q_HEADS * HD, D), (Q_HEADS * HD // 16) ** -0.5, 0.5, ((0, 4),)),
        "lengths": draw_lengths(jax.random.fold_in(jax.random.fold_in(streams_of[7], part), 71), part),
        "page_table": draw_page_table(jax.random.fold_in(jax.random.fold_in(streams_of[7], part), 71), part),
        "migration": draw_migration(jax.random.fold_in(jax.random.fold_in(streams_of[7], part), 71), part),
    }


def reference(queries, new_kv, kv_pool, out_weight, lengths, page_table, migration):
    served = jnp.arange(REQUESTS, dtype=jnp.int32)
    source = migration[:, 0]
    home_slot = migration[:, 1]
    target = migration[:, 2]
    target_slot = migration[:, 3]
    served = served.at[target * SLOTS + target_slot].set(source * SLOTS + home_slot)
    copy_count = kv_pool.shape[0]
    scale = 1.0 / (HD ** 0.5)
    positions = jnp.arange(MAXP * PAGE, dtype=jnp.int32)
    causal = jnp.arange(STEPS, dtype=jnp.int32)[None, :] <= jnp.arange(STEPS, dtype=jnp.int32)[:, None]

    def one_request(row):
        request = served[row]
        home = request // SLOTS
        pages = (page_table[request] + home * PAGES).astype(jnp.int32)
        context = kv_pool[:, pages].reshape(copy_count, MAXP * PAGE, 2 * HD).astype(jnp.float32)
        start = (row * STEPS).astype(jnp.int32)
        query_rows = lax.dynamic_slice_in_dim(queries, start, STEPS, 0)
        query_rows = query_rows.reshape(STEPS, copy_count, QH_DEV, HD).astype(jnp.float32)
        new_rows = lax.dynamic_slice_in_dim(new_kv, start, STEPS, 1).astype(jnp.float32)
        score_ctx = jnp.einsum("tcqd,ckd->ctqk", query_rows, context[:, :, :HD]) * scale
        live = positions < lengths[request] * PAGE
        score_ctx = jnp.where(live[None, None, None, :], score_ctx, jnp.float32(-1e30))
        score_new = jnp.einsum("tcqd,cud->ctqu", query_rows, new_rows[:, :, :HD]) * scale
        score_new = jnp.where(causal[None, :, None, :], score_new, jnp.float32(-1e30))
        row_max = jnp.maximum(jnp.max(score_ctx, axis=-1), jnp.max(score_new, axis=-1))
        exp_ctx = jnp.exp(score_ctx - row_max[..., None])
        exp_new = jnp.exp(score_new - row_max[..., None])
        row_total = jnp.sum(exp_ctx, axis=-1) + jnp.sum(exp_new, axis=-1)
        weight_ctx = lax.optimization_barrier((exp_ctx / row_total[..., None]).astype(jnp.bfloat16)).astype(jnp.float32)
        weight_new = lax.optimization_barrier((exp_new / row_total[..., None]).astype(jnp.bfloat16)).astype(jnp.float32)
        result = jnp.einsum("ctqk,ckd->tcqd", weight_ctx, context[:, :, HD:])
        result = result + jnp.einsum("ctqu,cud->tcqd", weight_new, new_rows[:, :, HD:])
        return result.astype(jnp.bfloat16).reshape(STEPS, copy_count * QH_DEV * HD)

    attended = lax.map(one_request, jnp.arange(REQUESTS, dtype=jnp.int32))
    attended = attended.reshape(REQUESTS * STEPS, copy_count * QH_DEV * HD)
    return jnp.dot(attended, out_weight, preferred_element_type=jnp.float32).astype(jnp.bfloat16)
```

```python
import functools

import jax
import jax.numpy as jnp
from jax import lax
from jax.experimental import pallas as pl
from jax.experimental.pallas import tpu as pltpu
from jax.sharding import PartitionSpec as P

LOG2E = 1.4426950408889634
MASKED = -1e30
GROUP = 4

VMEM = pl.BlockSpec(memory_space=pltpu.VMEM)
SMEM = pl.BlockSpec(memory_space=pltpu.SMEM)
HBM = pl.BlockSpec(memory_space=pl.ANY)


def contract_last(a, b):
    return lax.dot_general(a, b, (((1,), (1,)), ((), ())), preferred_element_type=jnp.float32)


def attend_group(queries, tokens, contexts, live_lengths, step_count):
    head_dim = tokens.shape[1] // 2
    head_count = queries.shape[1] // head_dim
    count = len(contexts)
    rows = head_count * step_count
    gain = LOG2E / head_dim**0.5
    stacked = jnp.concatenate(
        [
            queries[g * step_count : (g + 1) * step_count, h * head_dim : (h + 1) * head_dim]
            for g in range(count)
            for h in range(head_count)
        ],
        axis=0,
    ).astype(jnp.bfloat16)
    score_new = contract_last(stacked, tokens[:, :head_dim])
    row_ids = lax.broadcasted_iota(jnp.int32, score_new.shape, 0)
    column_ids = lax.broadcasted_iota(jnp.int32, score_new.shape, 1)
    allowed = (row_ids // rows == column_ids // step_count) & (
        column_ids % step_count <= row_ids % step_count
    )
    score_new = jnp.where(allowed, score_new, MASKED)
    new_max = jnp.max(score_new, axis=1, keepdims=True)
    maxima, scores = [], []
    for g in range(count):
        pages, page_len, _ = contexts[g].shape
        keys = contexts[g][:, :, :head_dim].reshape(pages * page_len, head_dim)
        score = contract_last(stacked[g * rows : (g + 1) * rows], keys)
        position = lax.broadcasted_iota(jnp.int32, score.shape, 1)
        score = jnp.where(position < live_lengths[g], score, MASKED)
        scores.append(score)
        maxima.append(
            jnp.maximum(
                jnp.max(score, axis=1, keepdims=True), new_max[g * rows : (g + 1) * rows]
            )
        )
    exp_new = jnp.exp2((score_new - jnp.concatenate(maxima, axis=0)) * gain)
    new_total = jnp.sum(exp_new, axis=1, keepdims=True)
    results, inverses = [], []
    for g in range(count):
        pages, page_len, _ = contexts[g].shape
        exp_ctx = jnp.exp2((scores[g] - maxima[g]) * gain)
        total = jnp.sum(exp_ctx, axis=1, keepdims=True) + new_total[g * rows : (g + 1) * rows]
        inverse = 1.0 / total
        inverses.append(inverse)
        values = contexts[g][:, :, head_dim:].reshape(pages * page_len, head_dim)
        results.append(
            jnp.dot(
                (exp_ctx * inverse).astype(jnp.bfloat16),
                values,
                preferred_element_type=jnp.float32,
            )
        )
    weight_new = (exp_new * jnp.concatenate(inverses, axis=0)).astype(jnp.bfloat16)
    result = jnp.concatenate(results, axis=0) + jnp.dot(
        weight_new, tokens[:, head_dim:], preferred_element_type=jnp.float32
    )
    return jnp.concatenate(
        [
            jnp.concatenate(
                [
                    result[g * rows + h * step_count : g * rows + (h + 1) * step_count]
                    for h in range(head_count)
                ],
                axis=1,
            )
            for g in range(count)
        ],
        axis=0,
    )


def route_of(migration, own_index, peer, arriving):
    ours, theirs, slot_row = (2, 0, 3) if arriving else (0, 2, 1)
    slot = jnp.int32(-1)
    for row in range(migration.shape[1]):
        match = (migration[ours, row] == own_index) & (migration[theirs, row] == peer)
        slot = jnp.where(match, migration[slot_row, row], slot)
    return slot


def pick_rows(ref, slot, step_count):
    pair = 2 * step_count
    start = pl.multiple_of((slot // 2) * pair, pair)
    both = ref[pl.ds(start, pair), :].astype(jnp.float32)
    return jnp.where(slot % 2 == 0, both[:step_count], both[step_count:])


def pack_kernel(inst_count, step_count, migration, queries, new_tokens, *outs):
    me = lax.axis_index("inst")
    width = queries.shape[1]
    for shift in range(1, inst_count):
        peer = lax.rem(me + shift, inst_count)
        slot = jnp.maximum(route_of(migration, me, peer, True), 0)
        for source, lo in ((queries, 0), (new_tokens, width)):
            rows = pick_rows(source, slot, step_count)
            outs[shift - 1][:, lo : lo + source.shape[1]] = jnp.concatenate(
                [rows, rows], axis=0
            ).astype(jnp.bfloat16)


def start_pages(pool, buffer, sems, page_of, item, live):
    for j in range(buffer.shape[1]):

        @pl.when(j < live)
        def _():
            pltpu.make_async_copy(pool.at[page_of(j)], buffer.at[item, j], sems.at[item, j]).start()

        @pl.when(j >= live)
        def _():
            buffer[item, j] = jnp.zeros(buffer.shape[2:], buffer.dtype)


def wait_pages(pool, buffer, sems, item, live):
    for j in range(buffer.shape[1]):

        @pl.when(j < live)
        def _():
            pltpu.make_async_copy(pool.at[0], buffer.at[item, j], sems.at[item, j]).wait()


def local_kernel(step_count, lengths, page_table, queries, new_tokens, pool, out, buffer, sems):
    slot_count, _, page_len, _ = buffer.shape
    first = lax.axis_index("inst") * slot_count

    @pl.loop(0, slot_count)
    def _(slot):
        start_pages(
            pool, buffer, sems, lambda j: page_table[j, slot], slot, lengths[first + slot]
        )

    @pl.loop(0, slot_count // GROUP)
    def _(group):
        slots = [group * GROUP + g for g in range(GROUP)]
        live = [lengths[first + slot] for slot in slots]
        for slot, pages in zip(slots, live):
            wait_pages(pool, buffer, sems, slot, pages)
        size = GROUP * step_count
        rows = pl.ds(pl.multiple_of(group * size, size), size)
        out[rows, :] = attend_group(
            queries[rows, :].astype(jnp.float32),
            new_tokens[rows, :],
            [buffer.at[slot] for slot in slots],
            [pages * page_len for pages in live],
            step_count,
        ).astype(jnp.bfloat16)


def away_kernel(inst_count, slot_count, step_count, lengths, page_table, migration, *refs):
    count = inst_count - 1
    received, pool, outs = refs[:count], refs[count], refs[count + 1 : 2 * count + 1]
    buffer, sems = refs[2 * count + 1 :]
    page_len = buffer.shape[2]
    me = lax.axis_index("inst")
    width = outs[0].shape[1]
    live = []
    for k in range(count):
        peer = lax.rem(me + inst_count - (k + 1), inst_count)
        slot = jnp.maximum(route_of(migration, me, peer, False), 0)
        live.append(lengths[me * slot_count + slot])
        start_pages(pool, buffer, sems, lambda j: page_table[j, slot], k, live[k])
    for k in range(count):
        wait_pages(pool, buffer, sems, k, live[k])
    items = [ref[...].astype(jnp.float32)[:step_count] for ref in received]
    result = attend_group(
        jnp.concatenate([item[:, :width] for item in items], axis=0),
        jnp.concatenate([item[:, width:] for item in items], axis=0).astype(jnp.bfloat16),
        [buffer.at[k] for k in range(count)],
        [pages * page_len for pages in live],
        step_count,
    )
    for k in range(count):
        rows = result[k * step_count : (k + 1) * step_count]
        outs[k][...] = jnp.concatenate([rows, rows], axis=0).astype(jnp.bfloat16)


def merge_kernel(inst_count, step_count, migration, attended, *refs):
    answers, out = refs[:-1], refs[-1]
    me = lax.axis_index("inst")
    pair = 2 * step_count
    out[...] = attended[...]
    for k in range(inst_count - 1):
        peer = lax.rem(me + k + 1, inst_count)
        slot = route_of(migration, me, peer, True)

        @pl.when(slot >= 0)
        def _():
            rows = pl.ds(pl.multiple_of((slot // 2) * pair, pair), pair)
            upper = lax.broadcasted_iota(jnp.int32, (pair, out.shape[1]), 0) >= step_count
            mine = upper == (slot % 2 == 1)
            out[rows, :] = jnp.where(
                mine, answers[k][...].astype(jnp.float32), out[rows, :].astype(jnp.float32)
            ).astype(jnp.bfloat16)


def project_kernel(start, own, mate, own_weight, mate_weight, out):
    out[...] = (
        jnp.dot(own[...], own_weight[...], preferred_element_type=jnp.float32)
        + jnp.dot(mate[...], mate_weight[...], preferred_element_type=jnp.float32)
    ).astype(out.dtype)


def project(own, mate, out_weight, mate_weight, column_start, dtype):
    row_count, depth = own.shape
    columns = mate_weight.shape[1]
    tile = min(512, columns)
    whole = pl.BlockSpec((row_count, depth), lambda j, start: (0, 0))
    return pl.pallas_call(
        project_kernel,
        out_shape=jax.ShapeDtypeStruct((row_count, columns), dtype),
        grid_spec=pltpu.PrefetchScalarGridSpec(
            num_scalar_prefetch=1,
            grid=(columns // tile,),
            in_specs=[
                whole,
                whole,
                pl.BlockSpec((depth, tile), lambda j, start: (0, start[0] // tile + j)),
                pl.BlockSpec((depth, tile), lambda j, start: (0, j)),
            ],
            out_specs=pl.BlockSpec((row_count, tile), lambda j, start: (0, j)),
        ),
        compiler_params=pltpu.CompilerParams(vmem_limit_bytes=32 * 2**20),
        cost_estimate=pl.CostEstimate(
            flops=4 * row_count * depth * columns,
            bytes_accessed=4 * depth * columns + 2 * row_count * columns,
            transcendentals=0,
        ),
        name="project",
    )(column_start.reshape(1), own, mate, out_weight, mate_weight)


def on_device(queries, new_kv, kv_pool, out_weight, lengths, page_table, migration):
    inst_count = lax.axis_size("inst")
    tp_count = lax.axis_size("tp")
    chips = tp_count // 2
    own_tp = lax.axis_index("tp")
    own_chip, own_core = own_tp // 2, own_tp % 2
    slot_count, page_count = page_table.shape
    row_count, width = queries.shape
    step_count = row_count // slot_count
    new_tokens = new_kv[0]
    pool = kv_pool[0]
    page_shape = pool.shape[1:]
    columns = out_weight.shape[1] // tp_count
    page_table = page_table.T
    migration = migration.T
    others = inst_count - 1
    limit = pltpu.CompilerParams(vmem_limit_bytes=40 * 2**20)
    bf16 = jnp.bfloat16

    packs = pl.pallas_call(
        functools.partial(pack_kernel, inst_count, step_count),
        out_shape=[
            jax.ShapeDtypeStruct((2 * step_count, width + new_tokens.shape[1]), bf16)
        ] * others,
        in_specs=[SMEM, VMEM, VMEM],
        out_specs=[VMEM] * others,
        compiler_params=limit,
        name="pack",
    )(migration, queries, new_tokens)
    forward = [[(i, (i + k) % inst_count) for i in range(inst_count)] for k in range(inst_count)]
    received = [lax.ppermute(packs[k - 1], "inst", forward[k]) for k in range(1, inst_count)]

    swap = [(t, t ^ 1) for t in range(tp_count)]
    mate_weights = []
    for d in range(chips):
        block = 2 * ((own_chip + d) % chips) + 1 - own_core
        mate_weights.append(lax.dynamic_slice_in_dim(out_weight, block * columns, columns, 1))
    mate_weights = [lax.ppermute(mate_weights[d], "tp", swap) for d in [*range(1, chips), 0]]
    mate_weights = mate_weights[-1:] + mate_weights[:-1]

    attended = pl.pallas_call(
        functools.partial(local_kernel, step_count),
        out_shape=jax.ShapeDtypeStruct((row_count, width), bf16),
        in_specs=[SMEM, SMEM, VMEM, VMEM, HBM],
        out_specs=VMEM,
        scratch_shapes=[
            pltpu.VMEM((slot_count, page_count, *page_shape), bf16),
            pltpu.SemaphoreType.DMA((slot_count, page_count)),
        ],
        compiler_params=limit,
        cost_estimate=pl.CostEstimate(
            flops=2**29, bytes_accessed=pool.size * 2, transcendentals=2**19
        ),
        name="attend_local",
    )(lengths, page_table, queries, new_tokens, pool)
    answers = pl.pallas_call(
        functools.partial(away_kernel, inst_count, slot_count, step_count),
        out_shape=[jax.ShapeDtypeStruct((2 * step_count, width), bf16)] * others,
        in_specs=[SMEM, SMEM, SMEM] + [VMEM] * others + [HBM],
        out_specs=[VMEM] * others,
        scratch_shapes=[
            pltpu.VMEM((others, page_count, *page_shape), bf16),
            pltpu.SemaphoreType.DMA((others, page_count)),
        ],
        compiler_params=limit,
        cost_estimate=pl.CostEstimate(
            flops=2**26, bytes_accessed=2**20, transcendentals=2**16
        ),
        name="attend_away",
    )(lengths, page_table, migration, *received, pool)
    answers = [
        lax.ppermute(answers[k - 1], "inst", [(b, a) for a, b in forward[k]])
        for k in range(1, inst_count)
    ]
    own = pl.pallas_call(
        functools.partial(merge_kernel, inst_count, step_count),
        out_shape=jax.ShapeDtypeStruct((row_count, width), bf16),
        in_specs=[SMEM, VMEM] + [VMEM] * others,
        out_specs=VMEM,
        compiler_params=limit,
        name="merge",
    )(migration, attended, *answers)
    mate = lax.ppermute(own, "tp", swap)

    arrived = []
    for d in range(1, chips):
        block = 2 * ((own_chip + d) % chips) + own_core
        partial_sum = project(own, mate, out_weight, mate_weights[d], block * columns, bf16)
        arrived.append(
            lax.ppermute(
                partial_sum, "tp", [(t, (t + 2 * d) % tp_count) for t in range(tp_count)]
            )
        )
    total = project(own, mate, out_weight, mate_weights[0], own_tp * columns, jnp.float32)
    for part in arrived:
        total = total + part.astype(jnp.float32)
    return total.astype(bf16)


def solution(mesh):
    placed = (
        P(("group", "inst"), "tp"),
        P("tp", ("group", "inst"), None),
        P("tp", ("group", "inst"), None, None),
        P("tp", None),
        P("group"),
        P(("group", "inst"), None),
        P("group", None),
    )
    return jax.shard_map(
        on_device, mesh=mesh, in_specs=placed, out_specs=P(("group", "inst"), "tp"), check_vma=False
    )
```

```python
import functools

import jax
import jax.numpy as jnp
from jax import lax
from jax.experimental import pallas as pl
from jax.experimental.pallas import tpu as pltpu
from jax.sharding import PartitionSpec as P

LOG2E = 1.4426950408889634
MASKED = -1e30
GROUP = 8

VMEM = pl.BlockSpec(memory_space=pltpu.VMEM)
SMEM = pl.BlockSpec(memory_space=pltpu.SMEM)
HBM = pl.BlockSpec(memory_space=pltpu.HBM)


def contract_last(a, b):
    return lax.dot_general(a, b, (((1,), (1,)), ((), ())), preferred_element_type=jnp.float32)


def attend_group(queries, tokens, contexts, live_lengths, step_count):
    count = len(queries)
    head_dim = tokens[0].shape[1] // 2
    head_count = queries[0].shape[1] // head_dim
    rows = head_count * step_count
    gain = LOG2E / head_dim**0.5
    stacked = jnp.concatenate(
        [
            query[:, h * head_dim : (h + 1) * head_dim]
            for query in queries
            for h in range(head_count)
        ],
        axis=0,
    ).astype(jnp.bfloat16)
    tokens = jnp.concatenate(tokens, axis=0).astype(jnp.bfloat16)
    score_new = contract_last(stacked, tokens[:, :head_dim])
    row_ids = lax.broadcasted_iota(jnp.int32, score_new.shape, 0)
    column_ids = lax.broadcasted_iota(jnp.int32, score_new.shape, 1)
    allowed = (row_ids // rows == column_ids // step_count) & (
        column_ids % step_count <= row_ids % step_count
    )
    score_new = jnp.where(allowed, score_new, MASKED)
    new_max = jnp.max(score_new, axis=1, keepdims=True)
    maxima, scores = [], []
    for g in range(count):
        keys = jnp.concatenate([page[:, :head_dim] for page in contexts[g]], axis=0)
        score = contract_last(stacked[g * rows : (g + 1) * rows], keys)
        position = lax.broadcasted_iota(jnp.int32, score.shape, 1)
        score = jnp.where(position < live_lengths[g], score, MASKED)
        scores.append(score)
        maxima.append(
            jnp.maximum(
                jnp.max(score, axis=1, keepdims=True), new_max[g * rows : (g + 1) * rows]
            )
        )
    exp_new = jnp.exp2((score_new - jnp.concatenate(maxima, axis=0)) * gain)
    new_total = jnp.sum(exp_new, axis=1, keepdims=True)
    results, inverses = [], []
    for g in range(count):
        exp_ctx = jnp.exp2((scores[g] - maxima[g]) * gain)
        total = jnp.sum(exp_ctx, axis=1, keepdims=True) + new_total[g * rows : (g + 1) * rows]
        inverse = 1.0 / total
        inverses.append(inverse)
        values = jnp.concatenate([page[:, head_dim:] for page in contexts[g]], axis=0)
        results.append(
            jnp.dot(
                (exp_ctx * inverse).astype(jnp.bfloat16),
                values,
                preferred_element_type=jnp.float32,
            )
        )
    weight_new = (exp_new * jnp.concatenate(inverses, axis=0)).astype(jnp.bfloat16)
    result = jnp.concatenate(results, axis=0) + jnp.dot(
        weight_new, tokens[:, head_dim:], preferred_element_type=jnp.float32
    )
    return [
        jnp.concatenate(
            [
                result[g * rows + h * step_count : g * rows + (h + 1) * step_count]
                for h in range(head_count)
            ],
            axis=1,
        )
        for g in range(count)
    ]


def route_of(migration, own_index, peer, arriving):
    ours, theirs, slot_row = (2, 0, 3) if arriving else (0, 2, 1)
    slot = jnp.int32(-1)
    for row in range(migration.shape[1]):
        match = (migration[ours, row] == own_index) & (migration[theirs, row] == peer)
        slot = jnp.where(match, migration[slot_row, row], slot)
    return slot


def arrivals_of(migration, inst_count):
    me = lax.axis_index("inst")
    return [
        route_of(migration, me, lax.rem(me + shift, inst_count), True)
        for shift in range(1, inst_count)
    ]


def write_order(migration, inst_count, slot_count, order):
    incoming = migration.shape[1] // inst_count
    kept = slot_count - incoming
    arrivals = arrivals_of(migration, inst_count)
    found = jnp.int32(0)
    for shift, slot in enumerate(arrivals):

        @pl.when((slot >= 0) & (found < incoming))
        def _():
            order[kept + found] = slot
            order[slot_count + found] = shift

        found = found + (slot >= 0).astype(jnp.int32)
    position = jnp.int32(0)
    for slot in range(slot_count):
        moved = jnp.bool_(False)
        for arrival in arrivals:
            moved = moved | (arrival == slot)
        stays = jnp.logical_not(moved) & (position < kept)

        @pl.when(stays)
        def _():
            order[position] = slot

        position = position + stays.astype(jnp.int32)


def pack_kernel(inst_count, migration, queries, new_tokens, after, *outs):
    width = queries.shape[2]
    for out, slot in zip(outs, arrivals_of(migration, inst_count)):
        safe = jnp.maximum(slot, 0)
        out[:, :width] = queries[safe]
        out[:, width:] = new_tokens[safe]


def away_kernel(inst_count, lengths, page_table, migration, after, *refs):
    count = inst_count - 1
    received, pool, outs = refs[:count], refs[count], refs[count + 1 :]
    page_count, slot_count = page_table.shape
    page_len = pool.shape[1]
    me = lax.axis_index("inst")
    step_count, width = outs[0].shape
    live, contexts = [], []
    for k in range(count):
        peer = lax.rem(me + inst_count - (k + 1), inst_count)
        slot = jnp.maximum(route_of(migration, me, peer, False), 0)
        live.append(lengths[me * slot_count + slot] * page_len)
        contexts.append([pool.at[page_table[j, slot]] for j in range(page_count)])
    result = attend_group(
        [ref[:, :width].astype(jnp.float32) for ref in received],
        [ref[:, width:].astype(jnp.float32) for ref in received],
        contexts,
        live,
        step_count,
    )
    for k in range(count):
        outs[k][...] = result[k].astype(jnp.bfloat16)


def attend_positions(positions, order, lengths, page_table, queries, new_tokens, pool):
    page_count, slot_count = page_table.shape
    page_len = pool.shape[1]
    own_first = lax.axis_index("inst") * slot_count
    slots = [order[position] for position in positions]
    return attend_group(
        [queries[slot].astype(jnp.float32) for slot in slots],
        [new_tokens[slot].astype(jnp.float32) for slot in slots],
        [[pool.at[page_table[j, slot]] for j in range(page_count)] for slot in slots],
        [lengths[own_first + slot] * page_len for slot in slots],
        queries.shape[1],
    )


def store_rows(rows, attended):
    step_count = rows[0].shape[0]
    for pair in range(0, len(rows), 2):
        attended[pair * step_count : (pair + 2) * step_count, :] = jnp.concatenate(
            rows[pair : pair + 2], axis=0
        ).astype(jnp.bfloat16)


def project_far(attended, far_weight, keep, send):
    core = lax.rem(lax.axis_index("tp"), 2)
    chips = lax.axis_size("tp") // 2
    columns = far_weight.shape[1] // (2 * chips - 2)
    tile = min(512, columns)
    rows = attended[...]
    for target, side in ((send, 1 - core), (keep, core)):
        for d in range(chips - 1):
            for j in range(0, columns, tile):
                start = pl.multiple_of((2 * d + side) * columns + j, tile)
                target[:, d * columns + j : d * columns + j + tile] = jnp.dot(
                    rows, far_weight[:, pl.ds(start, tile)], preferred_element_type=jnp.float32
                ).astype(target.dtype)


def first_kernel(
    inst_count, migration, lengths, page_table, queries, new_tokens, pool, weight,
    attended, keep, send, order, local_pool, far_weight, page_sems, weight_sems,
):
    page_count, slot_count = page_table.shape
    count = attended.shape[0] // queries.shape[1]
    own_tp = lax.axis_index("tp")
    chips = lax.axis_size("tp") // 2
    pair_columns = weight.shape[1] // chips
    write_order(migration, inst_count, slot_count, order)

    def start_pages(position):
        slot = order[position]
        for j in range(page_count):
            page = page_table[j, slot]
            pltpu.make_async_copy(
                pool.at[page], local_pool.at[page], page_sems.at[position]
            ).start()

    def wait_pages(position):
        pltpu.make_async_copy(
            pool.at[pl.ds(0, page_count)],
            local_pool.at[pl.ds(0, page_count)],
            page_sems.at[position],
        ).wait()

    def weight_copy(d):
        chip = lax.rem(own_tp // 2 + d, chips)
        start = pl.multiple_of(chip * pair_columns, pair_columns)
        return pltpu.make_async_copy(
            weight.at[:, pl.ds(start, pair_columns)],
            far_weight.at[:, pl.ds((d - 1) * pair_columns, pair_columns)],
            weight_sems.at[d - 1],
        )

    for position in range(count):
        start_pages(position)
    for d in range(1, chips):
        weight_copy(d).start()
    pl.loop(count, slot_count)(start_pages)
    rows = []
    for base in range(0, count, GROUP):
        positions = range(base, min(base + GROUP, count))
        for position in positions:
            wait_pages(position)
        rows += attend_positions(
            positions, order, lengths, page_table, queries, new_tokens, local_pool
        )
    store_rows(rows, attended)
    for d in range(1, chips):
        weight_copy(d).wait()
    project_far(attended, far_weight, keep, send)
    pl.loop(count, slot_count)(wait_pages)


def chunk_kernel(
    first_position, order, lengths, page_table, queries, new_tokens, pool, far_weight, after, *refs
):
    answers, (attended, keep, send) = refs[:-3], refs[-3:]
    slot_count = page_table.shape[1]
    count = attended.shape[0] // queries.shape[1]
    local = count - (order.shape[0] - slot_count if answers else 0)
    rows = []
    for base in range(0, local, GROUP):
        positions = range(first_position + base, first_position + min(base + GROUP, local))
        rows += attend_positions(positions, order, lengths, page_table, queries, new_tokens, pool)
    for m in range(count - local):
        chosen = order[slot_count + m]
        row = answers[0][...].astype(jnp.float32)
        for k in range(1, len(answers)):
            row = jnp.where(chosen == k, answers[k][...].astype(jnp.float32), row)
        rows.append(row)
    store_rows(rows, attended)
    project_far(attended, far_weight, keep, send)


def own_kernel(weight, *refs):
    attended, (keep, send, near_weight, sems) = refs[:-4], refs[-4:]
    rows = jnp.concatenate([ref[...] for ref in attended], axis=0)
    core = lax.rem(lax.axis_index("tp"), 2)
    chip = lax.axis_index("tp") // 2
    columns = keep.shape[1]
    copies = []
    for n, side in enumerate((1 - core, core)):
        start = pl.multiple_of((chip * 2 + side) * columns, columns)
        copies.append(
            pltpu.make_async_copy(
                weight.at[:, pl.ds(start, columns)], near_weight.at[n], sems.at[n]
            )
        )
        copies[n].start()
    tile = min(512, columns)
    for n, target in enumerate((send, keep)):
        copies[n].wait()
        for j in range(0, columns, tile):
            target[:, j : j + tile] = jnp.dot(
                rows, near_weight[n, :, j : j + tile], preferred_element_type=jnp.float32
            ).astype(target.dtype)


def final_kernel(step_count, part_count, order, keep, mate, *refs):
    out = refs[-1]
    pair = 2 * step_count
    at = 0
    for chunk in range(0, len(refs) - 1, part_count):
        parts = refs[chunk : chunk + part_count]
        for base in range(0, parts[0].shape[0], pair):
            total = keep[at : at + pair, :] + mate[at : at + pair, :].astype(jnp.float32)
            for part in parts:
                total = total + part[base : base + pair, :].astype(jnp.float32)
            total = total.astype(jnp.bfloat16)
            for half in range(2):
                out[order[at // step_count + half]] = total[
                    half * step_count : (half + 1) * step_count
                ]
            at += pair


def chunk_sizes(slot_count):
    large = (slot_count * 3 // 16) * 2
    return [large, large, slot_count - 2 * large]


def on_device(queries, new_kv, kv_pool, out_weight, lengths, page_table, migration):
    inst_count = lax.axis_size("inst")
    tp_count = lax.axis_size("tp")
    chips = tp_count // 2
    slot_count, page_count = page_table.shape
    row_count, width = queries.shape
    step_count = row_count // slot_count
    queries = queries.reshape(slot_count, step_count, width)
    new_tokens = new_kv[0].reshape(slot_count, step_count, new_kv.shape[2])
    pool = kv_pool[0]
    columns = out_weight.shape[1] // tp_count
    incoming = migration.shape[0] // inst_count
    page_table = page_table.T
    migration = migration.T
    others = inst_count - 1
    limit = pltpu.CompilerParams(vmem_limit_bytes=32 * 2**20)
    wide_limit = pltpu.CompilerParams(vmem_limit_bytes=40 * 2**20)
    light = pl.CostEstimate(flops=1, bytes_accessed=1, transcendentals=0)
    bf16, f32 = jnp.bfloat16, jnp.float32
    shape = jax.ShapeDtypeStruct

    swap = [(t, t ^ 1) for t in range(tp_count)]
    forward = [[(i, (i + k) % inst_count) for i in range(inst_count)] for k in range(inst_count)]
    far = (chips - 1) * columns
    arrived = []

    def chunk_shapes(count):
        rows = count * step_count
        return [shape((rows, width), bf16), shape((rows, far), f32), shape((rows, far), bf16)]

    def hold(value, until):
        return pl.pallas_call(
            lambda *refs: None,
            out_shape=shape(value.shape, value.dtype),
            in_specs=[HBM] * (1 + len(until)),
            out_specs=HBM,
            input_output_aliases={0: 0},
            cost_estimate=light,
            name="hold",
        )(value, *until)

    def exchange(keep, send):
        mate = lax.ppermute(send, "tp", swap)
        if arrived:
            keep = hold(keep, arrived[-(chips - 1) :])
        summed = (keep + mate.astype(f32)).astype(bf16)
        for d in range(1, chips):
            arrived.append(
                lax.ppermute(
                    summed[:, (d - 1) * columns : d * columns],
                    "tp",
                    [(t, (t + 2 * d) % tp_count) for t in range(tp_count)],
                )
            )
        return summed

    counts = chunk_sizes(slot_count)
    attended, keep, send, order, local_pool, far_weight = pl.pallas_call(
        functools.partial(first_kernel, inst_count),
        out_shape=chunk_shapes(counts[0])
        + [
            shape((slot_count + incoming,), jnp.int32),
            shape(pool.shape, bf16),
            shape((width, 2 * far), bf16),
        ],
        in_specs=[SMEM, SMEM, SMEM, VMEM, VMEM, HBM, HBM],
        out_specs=[VMEM] * 3 + [SMEM, VMEM, VMEM],
        scratch_shapes=[
            pltpu.SemaphoreType.DMA((slot_count,)),
            pltpu.SemaphoreType.DMA((chips - 1,)),
        ],
        compiler_params=wide_limit,
        cost_estimate=light,
        name="attend_first",
    )(migration, lengths, page_table, queries, new_tokens, pool, out_weight)
    chunks = [attended]
    summed = exchange(keep, send)
    packs = pl.pallas_call(
        functools.partial(pack_kernel, inst_count),
        out_shape=[shape((step_count, width + new_tokens.shape[2]), bf16)] * others,
        in_specs=[SMEM, VMEM, VMEM, HBM],
        out_specs=[VMEM] * others,
        compiler_params=limit,
        cost_estimate=light,
        name="pack",
    )(migration, queries, new_tokens, summed)
    received = [lax.ppermute(packs[k - 1], "inst", forward[k]) for k in range(1, inst_count)]
    first = counts[0]
    after = packs[0]
    answers = []
    for count in counts[1:]:
        last = first + count == slot_count
        if last:
            answers = pl.pallas_call(
                functools.partial(away_kernel, inst_count),
                out_shape=[shape((step_count, width), bf16)] * others,
                in_specs=[SMEM, SMEM, SMEM, HBM] + [VMEM] * (others + 1),
                out_specs=[VMEM] * others,
                compiler_params=limit,
                cost_estimate=light,
                name="attend_away",
            )(lengths, page_table, migration, chunks[-1], *received, local_pool)
            answers = [
                lax.ppermute(answers[k - 1], "inst", [(b, a) for a, b in forward[k]])
                for k in range(1, inst_count)
            ]
        attended, keep, send = pl.pallas_call(
            functools.partial(chunk_kernel, first),
            out_shape=chunk_shapes(count),
            in_specs=[SMEM, SMEM, SMEM] + [VMEM] * 4 + [HBM] + [VMEM] * len(answers),
            out_specs=[VMEM] * 3,
            compiler_params=limit,
            cost_estimate=light,
            name="attend_chunk",
        )(order, lengths, page_table, queries, new_tokens, local_pool, far_weight, after, *answers)
        chunks.append(attended)
        after = exchange(keep, send)
        first += count
    keep, send = pl.pallas_call(
        own_kernel,
        out_shape=[shape((row_count, columns), f32), shape((row_count, columns), bf16)],
        in_specs=[HBM] + [VMEM] * len(counts),
        out_specs=[VMEM] * 2,
        scratch_shapes=[
            pltpu.VMEM((2, width, columns), bf16),
            pltpu.SemaphoreType.DMA((2,)),
        ],
        compiler_params=pltpu.CompilerParams(vmem_limit_bytes=54 * 2**20),
        cost_estimate=light,
        name="own_columns",
    )(out_weight, *chunks)
    mate = lax.ppermute(send, "tp", swap)
    out = pl.pallas_call(
        functools.partial(final_kernel, step_count, chips - 1),
        out_shape=shape((slot_count, step_count, columns), bf16),
        in_specs=[SMEM] + [VMEM] * (2 + len(arrived)),
        out_specs=VMEM,
        compiler_params=limit,
        name="final_sum",
    )(order, keep, mate, *arrived)
    return out.reshape(row_count, columns)


def solution(mesh):
    placed = (
        P(("group", "inst"), "tp"),
        P("tp", ("group", "inst"), None),
        P("tp", ("group", "inst"), None, None),
        P("tp", None),
        P("group"),
        P(("group", "inst"), None),
        P("group", None),
    )
    return jax.shard_map(
        on_device, mesh=mesh, in_specs=placed, out_specs=P(("group", "inst"), "tp"), check_vma=False
    )
```

```python
import functools

import jax
import jax.numpy as jnp
from jax import lax
from jax.experimental import pallas as pl
from jax.experimental.pallas import tpu as pltpu
from jax.sharding import PartitionSpec as P

LOG2E = 1.4426950408889634
MASKED = -1e30
GROUP = 6
NEVER = 2**30

VMEM = pl.BlockSpec(memory_space=pltpu.VMEM)
SMEM = pl.BlockSpec(memory_space=pltpu.SMEM)
ANY = pl.BlockSpec(memory_space=pl.ANY)


def attend_group(queries, tokens, contexts, live_lengths, step_count):
    count = len(queries)
    head_dim = tokens[0].shape[1] // 2
    head_count = queries[0].shape[1] // head_dim
    rows = head_count * step_count
    gain = LOG2E / head_dim**0.5
    stacked = jnp.concatenate(
        [
            query[:, h * head_dim : (h + 1) * head_dim]
            for query in queries
            for h in range(head_count)
        ],
        axis=0,
    ).astype(jnp.bfloat16)
    tokens = jnp.concatenate(tokens, axis=0).astype(jnp.bfloat16)
    score_new = contract_last(stacked, tokens[:, :head_dim])
    row_ids = lax.broadcasted_iota(jnp.int32, score_new.shape, 0)
    column_ids = lax.broadcasted_iota(jnp.int32, score_new.shape, 1)
    allowed = (row_ids // rows == column_ids // step_count) & (
        column_ids % step_count <= row_ids % step_count
    )
    score_new = jnp.where(allowed, score_new, MASKED)
    new_max = jnp.max(score_new, axis=1, keepdims=True)
    maxima, scores = [], []
    for g in range(count):
        keys = jnp.concatenate([page[:, :head_dim] for page in contexts[g]], axis=0)
        score = contract_last(stacked[g * rows : (g + 1) * rows], keys)
        position = lax.broadcasted_iota(jnp.int32, score.shape, 1)
        score = jnp.where(position < live_lengths[g], score, MASKED)
        scores.append(score)
        maxima.append(
            jnp.maximum(
                jnp.max(score, axis=1, keepdims=True), new_max[g * rows : (g + 1) * rows]
            )
        )
    exp_new = jnp.exp2((score_new - jnp.concatenate(maxima, axis=0)) * gain)
    new_total = jnp.sum(exp_new, axis=1, keepdims=True)
    results, inverses = [], []
    for g in range(count):
        exp_ctx = jnp.exp2((scores[g] - maxima[g]) * gain)
        total = jnp.sum(exp_ctx, axis=1, keepdims=True) + new_total[g * rows : (g + 1) * rows]
        inverse = 1.0 / total
        inverses.append(inverse)
        values = jnp.concatenate([page[:, head_dim:] for page in contexts[g]], axis=0)
        results.append(
            jnp.dot(
                (exp_ctx * inverse).astype(jnp.bfloat16),
                values,
                preferred_element_type=jnp.float32,
            )
        )
    weight_new = (exp_new * jnp.concatenate(inverses, axis=0)).astype(jnp.bfloat16)
    result = jnp.concatenate(results, axis=0) + jnp.dot(
        weight_new, tokens[:, head_dim:], preferred_element_type=jnp.float32
    )
    return [
        jnp.concatenate(
            [
                result[g * rows + h * step_count : g * rows + (h + 1) * step_count]
                for h in range(head_count)
            ],
            axis=1,
        )
        for g in range(count)
    ]


def contract_last(a, b):
    return lax.dot_general(a, b, (((1,), (1,)), ((), ())), preferred_element_type=jnp.float32)


def route_of(migration, own_index, peer, arriving):
    ours, theirs, slot_row = (2, 0, 3) if arriving else (0, 2, 1)
    slot = jnp.int32(0)
    for row in range(migration.shape[1]):
        match = (migration[ours, row] == own_index) & (migration[theirs, row] == peer)
        slot = jnp.where(match, migration[slot_row, row], slot)
    return slot


def arrivals_of(migration, inst_count):
    me = lax.axis_index("inst")
    incoming = migration.shape[1] // inst_count
    slots = [jnp.int32(NEVER)] * incoming
    sources = [jnp.int32(0)] * incoming
    for row in range(migration.shape[1]):
        slot = jnp.where(migration[2, row] == me, migration[3, row], NEVER)
        source = migration[0, row]
        for i in range(incoming):
            before = slot < slots[i]
            slots[i], slot = jnp.where(before, slot, slots[i]), jnp.where(before, slots[i], slot)
            sources[i], source = (
                jnp.where(before, source, sources[i]),
                jnp.where(before, sources[i], source),
            )
    return slots, sources


def slot_at(position, arrivals, slot_count):
    kept = slot_count - len(arrivals)
    if position >= kept:
        return jnp.minimum(arrivals[position - kept], slot_count - 1)
    slot = jnp.int32(position)
    for arrival in arrivals:
        slot = slot + (slot >= arrival).astype(jnp.int32)
    return slot


def pack_kernel(inst_count, migration, queries, new_tokens, after, *outs):
    me = lax.axis_index("inst")
    width = queries.shape[2]
    for shift, out in enumerate(outs):
        slot = route_of(migration, me, lax.rem(me + shift + 1, inst_count), True)
        out[:, :width] = queries[slot]
        out[:, width:] = new_tokens[slot]


def page_copies(pool, buffer, sems, page_table, item, slot):
    page_count = page_table.shape[0]
    for j in range(page_count):
        pltpu.make_async_copy(
            pool.at[page_table[j, slot]], buffer.at[item, j], sems.at[item]
        ).start()


def wait_copies(pool, buffer, sems, item):
    pltpu.make_async_copy(
        pool.at[pl.ds(0, buffer.shape[1])], buffer.at[item], sems.at[item]
    ).wait()


def away_kernel(inst_count, lengths, page_table, migration, after, *refs):
    count = inst_count - 1
    received, pool, outs = refs[:count], refs[count], refs[count + 1 : 2 * count + 1]
    buffer, sems = refs[2 * count + 1 :]
    page_count, slot_count = page_table.shape
    page_len = pool.shape[1]
    me = lax.axis_index("inst")
    step_count, width = outs[0].shape
    live = []
    for k in range(count):
        peer = lax.rem(me + inst_count - (k + 1), inst_count)
        slot = route_of(migration, me, peer, False)
        page_copies(pool, buffer, sems, page_table, k, slot)
        live.append(lengths[me * slot_count + slot] * page_len)
    for k in range(count):
        wait_copies(pool, buffer, sems, k)
    result = attend_group(
        [ref[:, :width].astype(jnp.float32) for ref in received],
        [ref[:, width:].astype(jnp.float32) for ref in received],
        [[buffer.at[k, j] for j in range(page_count)] for k in range(count)],
        live,
        step_count,
    )
    for k in range(count):
        outs[k][...] = result[k].astype(jnp.bfloat16)


def project(attended, weight, first, columns, target, offset):
    tile = min(512, columns)
    rows = attended[...]
    for j in range(0, columns, tile):
        start = pl.multiple_of(first + j, tile)
        target[:, offset + j : offset + j + tile] = jnp.dot(
            rows, weight[:, pl.ds(start, tile)], preferred_element_type=jnp.float32
        ).astype(target.dtype)


def project_far(attended, far_weight, keep, send):
    core = lax.rem(lax.axis_index("tp"), 2)
    chips = lax.axis_size("tp") // 2
    columns = far_weight.shape[1] // (2 * chips - 2)
    for target, side in ((send, 1 - core), (keep, core)):
        for d in range(chips - 1):
            project(
                attended, far_weight, (2 * d + side) * columns, columns, target, d * columns
            )


def attend_chunk(
    inst_count, first, migration, lengths, page_table, queries, new_tokens, pool, answers,
    attended, buffer, sems,
    between=lambda: None,
):
    page_count, slot_count = page_table.shape
    page_len = pool.shape[1]
    step_count = queries.shape[1]
    count = attended.shape[0] // step_count
    me = lax.axis_index("inst")
    arrivals, sources = arrivals_of(migration, inst_count)
    local = min(count, slot_count - len(arrivals) - first)
    slots = [slot_at(first + i, arrivals, slot_count) for i in range(local)]
    for i, slot in enumerate(slots):
        page_copies(pool, buffer, sems, page_table, i, slot)
    between()
    rows = []
    for base in range(0, local, GROUP):
        items = range(base, min(base + GROUP, local))
        for i in items:
            wait_copies(pool, buffer, sems, i)
        rows += attend_group(
            [queries[slots[i]].astype(jnp.float32) for i in items],
            [new_tokens[slots[i]].astype(jnp.float32) for i in items],
            [[buffer.at[i, j] for j in range(page_count)] for i in items],
            [lengths[me * slot_count + slots[i]] * page_len for i in items],
            step_count,
        )
    for m in range(count - local):
        chosen = lax.rem(sources[m] - me + inst_count, inst_count) - 1
        row = answers[0][...].astype(jnp.float32)
        for k in range(1, len(answers)):
            row = jnp.where(chosen == k, answers[k][...].astype(jnp.float32), row)
        rows.append(row)
    for pair in range(0, count, 2):
        attended[pair * step_count : (pair + 2) * step_count, :] = jnp.concatenate(
            rows[pair : pair + 2], axis=0
        ).astype(jnp.bfloat16)


def first_kernel(
    inst_count, migration, lengths, page_table, queries, new_tokens, pool, weight,
    attended, keep, send, far_weight, buffer, page_sems, weight_sems,
):
    own_tp = lax.axis_index("tp")
    chips = lax.axis_size("tp") // 2
    pair_columns = weight.shape[1] // chips

    def weight_copy(d):
        chip = lax.rem(own_tp // 2 + d, chips)
        start = pl.multiple_of(chip * pair_columns, pair_columns)
        return pltpu.make_async_copy(
            weight.at[:, pl.ds(start, pair_columns)],
            far_weight.at[:, pl.ds((d - 1) * pair_columns, pair_columns)],
            weight_sems.at[d - 1],
        )

    def start_weight():
        for d in range(1, chips):
            weight_copy(d).start()

    attend_chunk(
        inst_count, 0, migration, lengths, page_table, queries, new_tokens, pool, (),
        attended, buffer, page_sems, start_weight,
    )
    for d in range(1, chips):
        weight_copy(d).wait()
    project_far(attended, far_weight, keep, send)


def chunk_kernel(
    inst_count, first, migration, lengths, page_table, queries, new_tokens, pool, far_weight,
    after, *refs
):
    answers, (attended, keep, send, buffer, sems) = refs[:-5], refs[-5:]
    attend_chunk(
        inst_count, first, migration, lengths, page_table, queries, new_tokens, pool, answers,
        attended, buffer, sems,
    )
    project_far(attended, far_weight, keep, send)


def own_kernel(weight, *refs):
    attended, (keep, send, rows, near_weight, sems) = refs[:-5], refs[-5:]
    core = lax.rem(lax.axis_index("tp"), 2)
    chip = lax.axis_index("tp") // 2
    columns = keep.shape[1]
    copies = []
    for n, side in enumerate((1 - core, core)):
        start = pl.multiple_of((chip * 2 + side) * columns, columns)
        copies.append(
            pltpu.make_async_copy(
                weight.at[:, pl.ds(start, columns)], near_weight.at[n], sems.at[n]
            )
        )
        copies[n].start()
    at = 0
    for ref in attended:
        rows[at : at + ref.shape[0], :] = ref[...]
        at += ref.shape[0]
    for n, target in enumerate((send, keep)):
        copies[n].wait()
        project(rows, near_weight.at[n], 0, columns, target, 0)


def sum_kernel(inst_count, chunks, migration, keep, mate, *refs):
    (out, last, staged, sem), parts = refs[-4:], refs[:-4]
    slot_count, step_count, _ = out.shape
    pair = 2 * step_count
    arrivals, _ = arrivals_of(migration, inst_count)
    share = len(parts) // len(chunks)
    at = 0
    for n, chunk in enumerate(chunks):
        for base in range(0, chunk, pair):
            total = keep[at : at + pair, :] + mate[at : at + pair, :].astype(jnp.float32)
            for part in parts[n * share : (n + 1) * share]:
                total = total + part[base : base + pair, :].astype(jnp.float32)
            total = total.astype(jnp.bfloat16)
            for half in range(2):
                staged[at // step_count + half] = total[half * step_count : (half + 1) * step_count]
            at += pair
    scatter_rows(staged, out, arrivals, 0, sem)
    last[...] = keep[at:, :] + mate[at:, :].astype(jnp.float32)


def scatter_rows(staged, out, arrivals, first, sem):
    slot_count = out.shape[0]
    for i in range(staged.shape[0]):
        slot = slot_at(first + i, arrivals, slot_count)
        pltpu.make_async_copy(staged.at[i], out.at[slot], sem.at[0]).start()
    pltpu.make_async_copy(staged, out.at[pl.ds(0, staged.shape[0])], sem.at[0]).wait()


def last_kernel(inst_count, first, migration, last, *refs):
    parts, (out, staged, sem) = refs[:-4], refs[-3:]
    step_count = out.shape[1]
    pair = 2 * step_count
    arrivals, _ = arrivals_of(migration, inst_count)
    for at in range(0, last.shape[0], pair):
        total = last[at : at + pair, :]
        for part in parts:
            total = total + part[at : at + pair, :].astype(jnp.float32)
        total = total.astype(jnp.bfloat16)
        for half in range(2):
            staged[at // step_count + half] = total[half * step_count : (half + 1) * step_count]
    scatter_rows(staged, out, arrivals, first, sem)


def chunk_sizes(slot_count):
    large = (slot_count * 3 // 16) * 2
    return [large, large, slot_count - 2 * large]


def in_hbm(value):
    return pltpu.with_memory_space_constraint(value, pltpu.HBM)


def in_vmem(value):
    return pltpu.with_memory_space_constraint(value, pltpu.VMEM)


def on_device(queries, new_kv, kv_pool, out_weight, lengths, page_table, migration):
    inst_count = lax.axis_size("inst")
    tp_count = lax.axis_size("tp")
    chips = tp_count // 2
    slot_count, page_count = page_table.shape
    row_count, width = queries.shape
    step_count = row_count // slot_count
    queries = in_hbm(queries.reshape(slot_count, step_count, width))
    new_tokens = in_hbm(new_kv[0].reshape(slot_count, step_count, new_kv.shape[2]))
    pool = in_hbm(kv_pool[0])
    page_shape = pool.shape[1:]
    columns = out_weight.shape[1] // tp_count
    weight = in_hbm(out_weight)
    lengths = in_hbm(lengths)
    page_table = in_hbm(page_table.T)
    migration = in_hbm(migration.T)
    others = inst_count - 1
    limit = pltpu.CompilerParams(vmem_limit_bytes=32 * 2**20)
    light = pl.CostEstimate(flops=1, bytes_accessed=1, transcendentals=0)
    bf16, f32 = jnp.bfloat16, jnp.float32
    shape = jax.ShapeDtypeStruct
    swap = [(t, t ^ 1) for t in range(tp_count)]
    forward = [[(i, (i + k) % inst_count) for i in range(inst_count)] for k in range(inst_count)]
    far = (chips - 1) * columns
    arrived = []

    def hold(value, until):
        return pl.pallas_call(
            lambda *refs: None,
            out_shape=shape(value.shape, value.dtype),
            in_specs=[ANY] * (1 + len(until)),
            out_specs=ANY,
            input_output_aliases={0: 0},
            cost_estimate=light,
            name="hold",
        )(value, *until)

    def exchange(keep, send, gate=()):
        mate = lax.ppermute(send, "tp", swap)
        if arrived:
            keep = hold(keep, [*arrived[-(chips - 1) :], *gate])
        summed = (keep + mate.astype(f32)).astype(bf16)
        for d in range(1, chips):
            arrived.append(
                lax.ppermute(
                    summed[:, (d - 1) * columns : d * columns],
                    "tp",
                    [(t, (t + 2 * d) % tp_count) for t in range(tp_count)],
                )
            )
        return summed

    def chunk_shapes(count):
        rows = count * step_count
        return [
            pltpu.VMEM((rows, width), bf16),
            pltpu.VMEM((rows, far), f32),
            pltpu.VMEM((rows, far), bf16),
        ]

    def page_scratch(count):
        return [
            pltpu.VMEM((count, page_count, *page_shape), bf16),
            pltpu.SemaphoreType.DMA((count,)),
        ]

    counts = chunk_sizes(slot_count)
    attended, keep, send, far_weight = pl.pallas_call(
        functools.partial(first_kernel, inst_count),
        out_shape=chunk_shapes(counts[0]) + [pltpu.VMEM((width, 2 * far), bf16)],
        in_specs=[SMEM, SMEM, SMEM, VMEM, VMEM, ANY, ANY],
        out_specs=[VMEM] * 4,
        scratch_shapes=page_scratch(counts[0]) + [pltpu.SemaphoreType.DMA((chips - 1,))],
        compiler_params=limit,
        cost_estimate=light,
        name="attend_first",
    )(migration, lengths, page_table, queries, new_tokens, pool, weight)
    chunks = [attended]
    after = exchange(keep, send)
    packs = pl.pallas_call(
        functools.partial(pack_kernel, inst_count),
        out_shape=[shape((step_count, width + new_tokens.shape[2]), bf16)] * others,
        in_specs=[SMEM, VMEM, VMEM, ANY],
        out_specs=[VMEM] * others,
        compiler_params=limit,
        cost_estimate=light,
        name="pack",
    )(migration, queries, new_tokens, after)
    received = [lax.ppermute(packs[k - 1], "inst", forward[k]) for k in range(1, inst_count)]
    first = counts[0]
    after = packs[0]
    answers = []
    for count in counts[1:]:
        given = answers if first + count == slot_count else []
        attended, keep, send = pl.pallas_call(
            functools.partial(chunk_kernel, inst_count, first),
            out_shape=chunk_shapes(count),
            in_specs=[SMEM, SMEM, SMEM, VMEM, VMEM, ANY, VMEM, ANY] + [VMEM] * len(given),
            out_specs=[VMEM] * 3,
            scratch_shapes=page_scratch(count),
            compiler_params=limit,
            cost_estimate=light,
            name="attend_chunk",
        )(
            migration, lengths, page_table, queries, new_tokens, pool, in_vmem(far_weight),
            after, *given,
        )
        chunks.append(attended)
        gate = []
        if first + count == slot_count - counts[-1]:
            answers = pl.pallas_call(
                functools.partial(away_kernel, inst_count),
                out_shape=[shape((step_count, width), bf16)] * others,
                in_specs=[SMEM, SMEM, SMEM, ANY] + [VMEM] * others + [ANY],
                out_specs=[VMEM] * others,
                scratch_shapes=page_scratch(others),
                compiler_params=limit,
                cost_estimate=light,
                name="attend_away",
            )(lengths, page_table, migration, chunks[-1], *received, pool)
            gate = answers[:1]
            answers = [
                lax.ppermute(answers[k - 1], "inst", [(b, a) for a, b in forward[k]])
                for k in range(1, inst_count)
            ]
        after = exchange(keep, send, gate)
        first += count
    keep, send = pl.pallas_call(
        own_kernel,
        out_shape=[pltpu.VMEM((row_count, columns), f32), pltpu.VMEM((row_count, columns), bf16)],
        in_specs=[ANY] + [VMEM] * len(counts),
        out_specs=[VMEM] * 2,
        scratch_shapes=[
            pltpu.VMEM((row_count, width), bf16),
            pltpu.VMEM((2, width, columns), bf16),
            pltpu.SemaphoreType.DMA((2,)),
        ],
        compiler_params=limit,
        cost_estimate=light,
        name="own_columns",
    )(weight, *[in_vmem(chunk) for chunk in chunks])
    mate = lax.ppermute(send, "tp", swap)
    early = slot_count - counts[-1]
    out_shape = (slot_count, step_count, columns)
    out, last = pl.pallas_call(
        functools.partial(
            sum_kernel, inst_count, [count * step_count for count in counts[:-1]]
        ),
        out_shape=[pltpu.HBM(out_shape, bf16), pltpu.VMEM((counts[-1] * step_count, columns), f32)],
        in_specs=[SMEM] + [VMEM] * (2 + len(arrived) - chips + 1),
        out_specs=[ANY, VMEM],
        scratch_shapes=[
            pltpu.VMEM((early, step_count, columns), bf16),
            pltpu.SemaphoreType.DMA((1,)),
        ],
        compiler_params=limit,
        cost_estimate=light,
        name="sum_early",
    )(migration, in_vmem(keep), mate, *arrived[: 1 - chips])
    out = pl.pallas_call(
        functools.partial(last_kernel, inst_count, early),
        out_shape=pltpu.HBM(out_shape, bf16),
        in_specs=[SMEM] + [VMEM] * chips + [ANY],
        out_specs=ANY,
        scratch_shapes=[
            pltpu.VMEM((counts[-1], step_count, columns), bf16),
            pltpu.SemaphoreType.DMA((1,)),
        ],
        input_output_aliases={1 + chips: 0},
        compiler_params=limit,
        cost_estimate=light,
        name="sum_last",
    )(migration, in_vmem(last), *arrived[1 - chips :], out)
    return out.reshape(row_count, columns)


def solution(mesh):
    placed = (
        P(("group", "inst"), "tp"),
        P("tp", ("group", "inst"), None),
        P("tp", ("group", "inst"), None, None),
        P("tp", None),
        P("group"),
        P(("group", "inst"), None),
        P("group", None),
    )
    return jax.shard_map(
        on_device, mesh=mesh, in_specs=placed, out_specs=P(("group", "inst"), "tp"), check_vma=False
    )
```

```python
import functools

import jax
import jax.numpy as jnp
from jax import lax
from jax.experimental import pallas as pl
from jax.experimental.pallas import tpu as pltpu
from jax.sharding import PartitionSpec as P

LOG2E = 1.4426950408889634
MASKED = -1e30
GROUP = 6
NEVER = 2**30

VMEM = pl.BlockSpec(memory_space=pltpu.VMEM)
SMEM = pl.BlockSpec(memory_space=pltpu.SMEM)
ANY = pl.BlockSpec(memory_space=pl.ANY)


def attend_group(queries, tokens, contexts, live_lengths, step_count):
    count = len(queries)
    head_dim = tokens[0].shape[1] // 2
    head_count = queries[0].shape[1] // head_dim
    rows = head_count * step_count
    gain = LOG2E / head_dim**0.5
    stacked = jnp.concatenate(
        [
            query[:, h * head_dim : (h + 1) * head_dim]
            for query in queries
            for h in range(head_count)
        ],
        axis=0,
    ).astype(jnp.bfloat16)
    tokens = jnp.concatenate(tokens, axis=0).astype(jnp.bfloat16)
    score_new = contract_last(stacked, tokens[:, :head_dim])
    row_ids = lax.broadcasted_iota(jnp.int32, score_new.shape, 0)
    column_ids = lax.broadcasted_iota(jnp.int32, score_new.shape, 1)
    allowed = (row_ids // rows == column_ids // step_count) & (
        column_ids % step_count <= row_ids % step_count
    )
    score_new = jnp.where(allowed, score_new, MASKED)
    new_max = jnp.max(score_new, axis=1, keepdims=True)
    maxima, scores = [], []
    for g in range(count):
        keys = jnp.concatenate([page[:, :head_dim] for page in contexts[g]], axis=0)
        score = contract_last(stacked[g * rows : (g + 1) * rows], keys)
        position = lax.broadcasted_iota(jnp.int32, score.shape, 1)
        score = jnp.where(position < live_lengths[g], score, MASKED)
        scores.append(score)
        maxima.append(
            jnp.maximum(
                jnp.max(score, axis=1, keepdims=True), new_max[g * rows : (g + 1) * rows]
            )
        )
    exp_new = jnp.exp2((score_new - jnp.concatenate(maxima, axis=0)) * gain)
    new_total = jnp.sum(exp_new, axis=1, keepdims=True)
    results, inverses = [], []
    for g in range(count):
        exp_ctx = jnp.exp2((scores[g] - maxima[g]) * gain)
        total = jnp.sum(exp_ctx, axis=1, keepdims=True) + new_total[g * rows : (g + 1) * rows]
        inverse = 1.0 / total
        inverses.append(inverse)
        values = jnp.concatenate([page[:, head_dim:] for page in contexts[g]], axis=0)
        results.append(
            jnp.dot(
                (exp_ctx * inverse).astype(jnp.bfloat16),
                values,
                preferred_element_type=jnp.float32,
            )
        )
    weight_new = (exp_new * jnp.concatenate(inverses, axis=0)).astype(jnp.bfloat16)
    result = jnp.concatenate(results, axis=0) + jnp.dot(
        weight_new, tokens[:, head_dim:], preferred_element_type=jnp.float32
    )
    return [
        jnp.concatenate(
            [
                result[g * rows + h * step_count : g * rows + (h + 1) * step_count]
                for h in range(head_count)
            ],
            axis=1,
        )
        for g in range(count)
    ]


def contract_last(a, b):
    return lax.dot_general(a, b, (((1,), (1,)), ((), ())), preferred_element_type=jnp.float32)


def route_of(migration, own_index, peer, arriving):
    ours, theirs, slot_row = (2, 0, 3) if arriving else (0, 2, 1)
    slot = jnp.int32(0)
    for row in range(migration.shape[1]):
        match = (migration[ours, row] == own_index) & (migration[theirs, row] == peer)
        slot = jnp.where(match, migration[slot_row, row], slot)
    return slot


def arrivals_of(migration, inst_count):
    me = lax.axis_index("inst")
    incoming = migration.shape[1] // inst_count
    slots = [jnp.int32(NEVER)] * incoming
    sources = [jnp.int32(0)] * incoming
    for row in range(migration.shape[1]):
        slot = jnp.where(migration[2, row] == me, migration[3, row], NEVER)
        source = migration[0, row]
        for i in range(incoming):
            before = slot < slots[i]
            slots[i], slot = jnp.where(before, slot, slots[i]), jnp.where(before, slots[i], slot)
            sources[i], source = (
                jnp.where(before, source, sources[i]),
                jnp.where(before, sources[i], source),
            )
    return slots, sources


def slot_at(position, arrivals, slot_count):
    kept = slot_count - len(arrivals)
    if position >= kept:
        return jnp.minimum(arrivals[position - kept], slot_count - 1)
    slot = jnp.int32(position)
    for arrival in arrivals:
        slot = slot + (slot >= arrival).astype(jnp.int32)
    return slot


def pack_rows(inst_count, migration, queries, new_tokens, packs):
    me = lax.axis_index("inst")
    width = queries.shape[2]
    for peer in range(inst_count):
        slot = route_of(migration, me, peer, True)
        packs[peer, :, :width] = queries[slot]
        packs[peer, :, width:] = new_tokens[slot]


def page_copies(pool, buffer, sems, page_table, item, slot):
    page_count = page_table.shape[0]
    for j in range(page_count):
        pltpu.make_async_copy(
            pool.at[page_table[j, slot]], buffer.at[item, j], sems.at[item]
        ).start()


def wait_copies(pool, buffer, sems, item):
    pltpu.make_async_copy(
        pool.at[pl.ds(0, buffer.shape[1])], buffer.at[item], sems.at[item]
    ).wait()


def away_kernel(inst_count, lengths, page_table, migration, after, received, pool, answers, buffer, sems):
    count = inst_count - 1
    page_count, slot_count = page_table.shape
    page_len = pool.shape[1]
    me = lax.axis_index("inst")
    _, step_count, width = answers.shape
    peers = [lax.rem(me + k, inst_count) for k in range(1, inst_count)]
    live = []
    for k, peer in enumerate(peers):
        slot = route_of(migration, me, peer, False)
        page_copies(pool, buffer, sems, page_table, k, slot)
        live.append(lengths[me * slot_count + slot] * page_len)
    items = [received[peer].astype(jnp.float32) for peer in peers]
    for k in range(count):
        wait_copies(pool, buffer, sems, k)
    result = attend_group(
        [item[:, :width] for item in items],
        [item[:, width:] for item in items],
        [[buffer.at[k, j] for j in range(page_count)] for k in range(count)],
        live,
        step_count,
    )
    answers[me] = jnp.zeros((step_count, width), answers.dtype)
    for peer, rows in zip(peers, result):
        answers[peer] = rows.astype(answers.dtype)


def project(rows, weight, first, columns, target, row_offset=0, offset=0):
    tile = min(512, columns)
    rows = rows[...]
    for j in range(0, columns, tile):
        start = pl.multiple_of(first + j, tile)
        target[row_offset : row_offset + rows.shape[0], offset + j : offset + j + tile] = jnp.dot(
            rows, weight[:, pl.ds(start, tile)], preferred_element_type=jnp.float32
        ).astype(target.dtype)


def project_far(attended, far_weight, keep, send):
    core = lax.rem(lax.axis_index("tp"), 2)
    chips = lax.axis_size("tp") // 2
    columns = far_weight.shape[1] // (2 * chips - 2)
    for target, side in ((send, 1 - core), (keep, core)):
        for d in range(chips - 1):
            first = (2 * d + side) * columns
            project(attended, far_weight, first, columns, target, 0, d * columns)


def attend_slots(
    inst_count, positions, migration, lengths, page_table, queries, new_tokens, pool, buffer, sems,
    between=lambda: None,
):
    page_count, slot_count = page_table.shape
    page_len = pool.shape[1]
    me = lax.axis_index("inst")
    arrivals, _ = arrivals_of(migration, inst_count)
    slots = [slot_at(position, arrivals, slot_count) for position in positions]
    for i, slot in enumerate(slots):
        page_copies(pool, buffer, sems, page_table, i, slot)
    between()
    rows = []
    for base in range(0, len(slots), GROUP):
        items = range(base, min(base + GROUP, len(slots)))
        for i in items:
            wait_copies(pool, buffer, sems, i)
        rows += attend_group(
            [queries[slots[i]].astype(jnp.float32) for i in items],
            [new_tokens[slots[i]].astype(jnp.float32) for i in items],
            [[buffer.at[i, j] for j in range(page_count)] for i in items],
            [lengths[me * slot_count + slots[i]] * page_len for i in items],
            queries.shape[1],
        )
    return rows


def store_rows(rows, target, at=0):
    step_count = rows[0].shape[0]
    for pair in range(0, len(rows), 2):
        start = at + pair * step_count
        target[start : start + 2 * step_count, :] = jnp.concatenate(
            rows[pair : pair + 2], axis=0
        ).astype(jnp.bfloat16)


def first_kernel(
    inst_count, migration, lengths, page_table, queries, new_tokens, pool, weight,
    attended, keep, send, far_weight, packs, buffer, page_sems, weight_sems,
):
    own_tp = lax.axis_index("tp")
    chips = lax.axis_size("tp") // 2
    pair_columns = weight.shape[1] // chips

    def weight_copy(d):
        chip = lax.rem(own_tp // 2 + d, chips)
        start = pl.multiple_of(chip * pair_columns, pair_columns)
        return pltpu.make_async_copy(
            weight.at[:, pl.ds(start, pair_columns)],
            far_weight.at[:, pl.ds((d - 1) * pair_columns, pair_columns)],
            weight_sems.at[d - 1],
        )

    def between():
        for d in range(1, chips):
            weight_copy(d).start()
        pack_rows(inst_count, migration, queries, new_tokens, packs)

    count = attended.shape[0] // queries.shape[1]
    store_rows(
        attend_slots(
            inst_count, range(count), migration, lengths, page_table, queries, new_tokens, pool,
            buffer, page_sems, between,
        ),
        attended,
    )
    for d in range(1, chips):
        weight_copy(d).wait()
    project_far(attended, far_weight, keep, send)


def second_kernel(
    inst_count, first, migration, lengths, page_table, queries, new_tokens, pool, far_weight,
    after, attended, extra, keep, send, buffer, sems,
):
    count = attended.shape[0] // queries.shape[1]
    rows = attend_slots(
        inst_count, range(first, first + count + extra.shape[0]), migration, lengths, page_table,
        queries, new_tokens, pool, buffer, sems,
    )
    store_rows(rows[:count], attended)
    for i, row in enumerate(rows[count:]):
        extra[i] = row.astype(extra.dtype)
    project_far(attended, far_weight, keep, send)


def own_kernel(weight, first, second, keep, send, near_weight, rows, sems):
    core = lax.rem(lax.axis_index("tp"), 2)
    chip = lax.axis_index("tp") // 2
    columns = keep.shape[1]
    copies = []
    for n, side in enumerate((1 - core, core)):
        start = pl.multiple_of((chip * 2 + side) * columns, columns)
        copies.append(
            pltpu.make_async_copy(
                weight.at[:, pl.ds(start, columns)], near_weight.at[n], sems.at[n]
            )
        )
        copies[n].start()
    rows[: first.shape[0], :] = first[...]
    rows[first.shape[0] :, :] = second[...]
    for n, target in enumerate((send, keep)):
        copies[n].wait()
        project(rows, near_weight.at[n], 0, columns, target)


def last_rows_kernel(
    inst_count, migration, near_weight, far_weight, extra, answers, keep, send, rows
):
    core = lax.rem(lax.axis_index("tp"), 2)
    chips = lax.axis_size("tp") // 2
    columns = keep.shape[1]
    _, sources = arrivals_of(migration, inst_count)
    last = [extra[i].astype(jnp.float32) for i in range(extra.shape[0])]
    last += [answers[source].astype(jnp.float32) for source in sources]
    size = rows.shape[0]
    store_rows(last, rows)
    for n, (target, side) in enumerate(((send, 1 - core), (keep, core))):
        for d in range(chips - 1):
            project(rows, far_weight, (2 * d + side) * columns, columns, target, d * size)
        project(rows, near_weight.at[n], 0, columns, target, (chips - 1) * size)


def sum_kernel(inst_count, chunks, migration, keep, mate, *refs):
    (out, staged, sem), parts = refs[-3:], refs[:-3]
    slot_count, step_count, _ = out.shape
    pair = 2 * step_count
    arrivals, _ = arrivals_of(migration, inst_count)
    share = len(parts) // len(chunks)
    at = 0
    for n, chunk in enumerate(chunks):
        for base in range(0, chunk, pair):
            total = keep[at : at + pair, :] + mate[at : at + pair, :].astype(jnp.float32)
            for part in parts[n * share : (n + 1) * share]:
                total = total + part[base : base + pair, :].astype(jnp.float32)
            total = total.astype(jnp.bfloat16)
            for half in range(2):
                staged[at // step_count + half] = total[half * step_count : (half + 1) * step_count]
            at += pair
    scatter_rows(staged, out, arrivals, 0, sem)


def scatter_rows(staged, out, arrivals, first, sem):
    slot_count = out.shape[0]
    for i in range(staged.shape[0]):
        slot = slot_at(first + i, arrivals, slot_count)
        pltpu.make_async_copy(staged.at[i], out.at[slot], sem.at[0]).start()
    pltpu.make_async_copy(staged, out.at[pl.ds(0, staged.shape[0])], sem.at[0]).wait()


def last_kernel(inst_count, first, migration, keep, mate, *refs):
    parts, (out, staged, sem) = refs[:-4], refs[-3:]
    step_count = out.shape[1]
    pair = 2 * step_count
    size = parts[0].shape[0]
    arrivals, _ = arrivals_of(migration, inst_count)
    for at in range(0, size, pair):
        own = keep.shape[0] - size + at
        total = keep[own : own + pair, :] + mate[own : own + pair, :].astype(jnp.float32)
        for part in parts:
            total = total + part[at : at + pair, :].astype(jnp.float32)
        total = total.astype(jnp.bfloat16)
        for half in range(2):
            staged[at // step_count + half] = total[half * step_count : (half + 1) * step_count]
    scatter_rows(staged, out, arrivals, first, sem)


def in_hbm(value):
    return pltpu.with_memory_space_constraint(value, pltpu.HBM)


def in_vmem(value):
    return pltpu.with_memory_space_constraint(value, pltpu.VMEM)


def on_device(queries, new_kv, kv_pool, out_weight, lengths, page_table, migration):
    inst_count = lax.axis_size("inst")
    tp_count = lax.axis_size("tp")
    chips = tp_count // 2
    slot_count, page_count = page_table.shape
    row_count, width = queries.shape
    step_count = row_count // slot_count
    queries = in_hbm(queries.reshape(slot_count, step_count, width))
    new_tokens = in_hbm(new_kv[0].reshape(slot_count, step_count, new_kv.shape[2]))
    pool = in_hbm(kv_pool[0])
    page_shape = pool.shape[1:]
    columns = out_weight.shape[1] // tp_count
    incoming = migration.shape[0] // inst_count
    weight = in_hbm(out_weight)
    lengths = in_hbm(lengths)
    page_table = in_hbm(page_table.T)
    migration = in_hbm(migration.T)
    limit = pltpu.CompilerParams(vmem_limit_bytes=32 * 2**20)
    light = pl.CostEstimate(flops=1, bytes_accessed=1, transcendentals=0)
    bf16, f32 = jnp.bfloat16, jnp.float32
    shape = jax.ShapeDtypeStruct
    swap = [(t, t ^ 1) for t in range(tp_count)]
    far = (chips - 1) * columns

    def hold(value, until):
        return pl.pallas_call(
            lambda *refs: None,
            out_shape=pltpu.VMEM(value.shape, value.dtype),
            in_specs=[ANY] * (1 + len(until)),
            out_specs=ANY,
            input_output_aliases={0: 0},
            compiler_params=pltpu.CompilerParams(vmem_limit_bytes=2**20),
            cost_estimate=light,
            name="hold",
        )(in_vmem(value), *until)

    def send_far(summed):
        return [
            lax.ppermute(
                part, "tp", [(t, (t + 2 * d) % tp_count) for t in range(tp_count)]
            )
            for d, part in enumerate(summed, 1)
        ]

    def split_far(summed):
        return [summed[:, d * columns : (d + 1) * columns] for d in range(chips - 1)]

    def chunk_shapes(count):
        rows = count * step_count
        return [pltpu.VMEM((rows, far), f32), pltpu.VMEM((rows, far), bf16)]

    def rows_shape(count):
        return pltpu.VMEM((count * step_count, width), bf16)

    def page_scratch(count):
        return [
            pltpu.VMEM((count, page_count, *page_shape), bf16),
            pltpu.SemaphoreType.DMA((count,)),
        ]

    last_count = incoming + incoming % 2
    extra_count = last_count - incoming
    first_count = slot_count // 4 * 2
    second_count = slot_count - first_count - last_count
    last_rows = last_count * step_count

    first, keep, send, far_weight, packs = pl.pallas_call(
        functools.partial(first_kernel, inst_count),
        out_shape=[
            rows_shape(first_count),
            *chunk_shapes(first_count),
            pltpu.VMEM((width, 2 * far), bf16),
            shape((inst_count, step_count, width + new_tokens.shape[2]), bf16),
        ],
        in_specs=[SMEM, SMEM, SMEM, VMEM, VMEM, ANY, ANY],
        out_specs=[VMEM] * 5,
        scratch_shapes=page_scratch(first_count) + [pltpu.SemaphoreType.DMA((chips - 1,))],
        compiler_params=limit,
        cost_estimate=light,
        name="attend_first",
    )(migration, lengths, page_table, queries, new_tokens, pool, weight)
    far_weight = in_vmem(far_weight)
    mate = lax.ppermute(send, "tp", swap)
    summed = (keep + mate.astype(f32)).astype(bf16)
    arrived_first = send_far(split_far(summed))
    received = lax.all_to_all(packs, "inst", split_axis=0, concat_axis=0, tiled=True)

    second, extra, keep, send = pl.pallas_call(
        functools.partial(second_kernel, inst_count, first_count),
        out_shape=[
            rows_shape(second_count),
            pltpu.VMEM((extra_count, step_count, width), bf16),
            *chunk_shapes(second_count),
        ],
        in_specs=[SMEM, SMEM, SMEM, VMEM, VMEM, ANY, VMEM, ANY],
        out_specs=[VMEM] * 4,
        scratch_shapes=page_scratch(second_count + extra_count),
        compiler_params=limit,
        cost_estimate=light,
        name="attend_second",
    )(migration, lengths, page_table, queries, new_tokens, pool, far_weight, summed)
    mate = lax.ppermute(send, "tp", swap)
    answers = pl.pallas_call(
        functools.partial(away_kernel, inst_count),
        out_shape=shape((inst_count, step_count, width), bf16),
        in_specs=[SMEM, SMEM, SMEM, ANY, VMEM, ANY],
        out_specs=VMEM,
        scratch_shapes=page_scratch(inst_count - 1),
        compiler_params=limit,
        cost_estimate=light,
        name="attend_away",
    )(lengths, page_table, migration, second, received, pool)
    early_rows = (first_count + second_count) * step_count
    early_keep, early_send, near_weight = pl.pallas_call(
        own_kernel,
        out_shape=[
            pltpu.VMEM((early_rows, columns), f32),
            pltpu.VMEM((early_rows, columns), bf16),
            pltpu.VMEM((2, width, columns), bf16),
        ],
        in_specs=[ANY, VMEM, VMEM],
        out_specs=[VMEM] * 3,
        scratch_shapes=[
            pltpu.VMEM((early_rows, width), bf16),
            pltpu.SemaphoreType.DMA((2,)),
        ],
        compiler_params=limit,
        cost_estimate=light,
        name="own_columns",
    )(weight, in_vmem(first), in_vmem(second))
    early_mate = lax.ppermute(early_send, "tp", swap)
    keep = hold(keep, [*arrived_first, answers, early_keep])
    summed = (keep + mate.astype(f32)).astype(bf16)
    arrived_second = send_far(split_far(summed))
    answers = lax.all_to_all(answers, "inst", split_axis=0, concat_axis=0, tiled=True)

    keep, send = pl.pallas_call(
        functools.partial(last_rows_kernel, inst_count),
        out_shape=[
            pltpu.VMEM((last_rows * chips, columns), f32),
            pltpu.VMEM((last_rows * chips, columns), bf16),
        ],
        in_specs=[SMEM] + [VMEM] * 4,
        out_specs=[VMEM] * 2,
        scratch_shapes=[pltpu.VMEM((last_rows, width), bf16)],
        compiler_params=limit,
        cost_estimate=light,
        name="last_rows",
    )(migration, in_vmem(near_weight), far_weight, in_vmem(extra), answers)
    mate = lax.ppermute(send, "tp", swap)
    keep = hold(keep, arrived_second)
    summed = (keep[:-last_rows] + mate[:-last_rows].astype(f32)).astype(bf16)
    arrived_last = send_far([summed[d * last_rows : (d + 1) * last_rows] for d in range(chips - 1)])

    early = slot_count - last_count
    out_shape = (slot_count, step_count, columns)
    out = pl.pallas_call(
        functools.partial(
            sum_kernel, inst_count, [first_count * step_count, second_count * step_count]
        ),
        out_shape=pltpu.HBM(out_shape, bf16),
        in_specs=[SMEM] + [VMEM] * (2 + 2 * (chips - 1)),
        out_specs=ANY,
        scratch_shapes=[
            pltpu.VMEM((early, step_count, columns), bf16),
            pltpu.SemaphoreType.DMA((1,)),
        ],
        compiler_params=limit,
        cost_estimate=light,
        name="sum_early",
    )(migration, in_vmem(early_keep), early_mate, *arrived_first, *arrived_second)
    out = pl.pallas_call(
        functools.partial(last_kernel, inst_count, early),
        out_shape=pltpu.HBM(out_shape, bf16),
        in_specs=[SMEM] + [VMEM] * (chips + 1) + [ANY],
        out_specs=ANY,
        scratch_shapes=[
            pltpu.VMEM((last_count, step_count, columns), bf16),
            pltpu.SemaphoreType.DMA((1,)),
        ],
        input_output_aliases={2 + chips: 0},
        compiler_params=limit,
        cost_estimate=light,
        name="sum_last",
    )(migration, in_vmem(keep), mate, *arrived_last, out)
    return out.reshape(row_count, columns)


def solution(mesh):
    placed = (
        P(("group", "inst"), "tp"),
        P("tp", ("group", "inst"), None),
        P("tp", ("group", "inst"), None, None),
        P("tp", None),
        P("group"),
        P(("group", "inst"), None),
        P("group", None),
    )
    return jax.shard_map(
        on_device, mesh=mesh, in_specs=placed, out_specs=P(("group", "inst"), "tp"), check_vma=False
    )
```

```python
import functools

import jax
import jax.numpy as jnp
from jax import lax
from jax.experimental import pallas as pl
from jax.experimental.pallas import tpu as pltpu
from jax.sharding import PartitionSpec as P

LOG2E = 1.4426950408889634
MASKED = -1e30
GROUP = 6
NEVER = 2**30

VMEM = pl.BlockSpec(memory_space=pltpu.VMEM)
SMEM = pl.BlockSpec(memory_space=pltpu.SMEM)
ANY = pl.BlockSpec(memory_space=pl.ANY)


def attend_group(queries, tokens, contexts, live_lengths, step_count):
    count = len(queries)
    head_dim = tokens[0].shape[1] // 2
    head_count = queries[0].shape[1] // head_dim
    rows = head_count * step_count
    gain = LOG2E / head_dim**0.5
    stacked = jnp.concatenate(
        [
            query[:, h * head_dim : (h + 1) * head_dim]
            for query in queries
            for h in range(head_count)
        ],
        axis=0,
    ).astype(jnp.bfloat16)
    tokens = jnp.concatenate(tokens, axis=0).astype(jnp.bfloat16)
    score_new = contract_last(stacked, tokens[:, :head_dim])
    row_ids = lax.broadcasted_iota(jnp.int32, score_new.shape, 0)
    column_ids = lax.broadcasted_iota(jnp.int32, score_new.shape, 1)
    allowed = (row_ids // rows == column_ids // step_count) & (
        column_ids % step_count <= row_ids % step_count
    )
    score_new = jnp.where(allowed, score_new, MASKED)
    new_max = jnp.max(score_new, axis=1, keepdims=True)
    maxima, scores = [], []
    for g in range(count):
        keys = jnp.concatenate([page[:, :head_dim] for page in contexts[g]], axis=0)
        score = contract_last(stacked[g * rows : (g + 1) * rows], keys)
        position = lax.broadcasted_iota(jnp.int32, score.shape, 1)
        score = jnp.where(position < live_lengths[g], score, MASKED)
        scores.append(score)
        maxima.append(
            jnp.maximum(
                jnp.max(score, axis=1, keepdims=True), new_max[g * rows : (g + 1) * rows]
            )
        )
    exp_new = jnp.exp2((score_new - jnp.concatenate(maxima, axis=0)) * gain)
    new_total = jnp.sum(exp_new, axis=1, keepdims=True)
    results, inverses = [], []
    for g in range(count):
        exp_ctx = jnp.exp2((scores[g] - maxima[g]) * gain)
        total = jnp.sum(exp_ctx, axis=1, keepdims=True) + new_total[g * rows : (g + 1) * rows]
        inverse = 1.0 / total
        inverses.append(inverse)
        values = jnp.concatenate([page[:, head_dim:] for page in contexts[g]], axis=0)
        results.append(
            jnp.dot(
                (exp_ctx * inverse).astype(jnp.bfloat16),
                values,
                preferred_element_type=jnp.float32,
            )
        )
    weight_new = (exp_new * jnp.concatenate(inverses, axis=0)).astype(jnp.bfloat16)
    result = jnp.concatenate(results, axis=0) + jnp.dot(
        weight_new, tokens[:, head_dim:], preferred_element_type=jnp.float32
    )
    return [
        jnp.concatenate(
            [
                result[g * rows + h * step_count : g * rows + (h + 1) * step_count]
                for h in range(head_count)
            ],
            axis=1,
        )
        for g in range(count)
    ]


def contract_last(a, b):
    return lax.dot_general(a, b, (((1,), (1,)), ((), ())), preferred_element_type=jnp.float32)


def route_of(migration, own_index, peer, arriving):
    ours, theirs, slot_row = (2, 0, 3) if arriving else (0, 2, 1)
    slot = jnp.int32(0)
    for row in range(migration.shape[1]):
        match = (migration[ours, row] == own_index) & (migration[theirs, row] == peer)
        slot = jnp.where(match, migration[slot_row, row], slot)
    return slot


def arrivals_of(migration, inst_count):
    me = lax.axis_index("inst")
    incoming = migration.shape[1] // inst_count
    slots = [jnp.int32(NEVER)] * incoming
    sources = [jnp.int32(0)] * incoming
    for row in range(migration.shape[1]):
        slot = jnp.where(migration[2, row] == me, migration[3, row], NEVER)
        source = migration[0, row]
        for i in range(incoming):
            before = slot < slots[i]
            slots[i], slot = jnp.where(before, slot, slots[i]), jnp.where(before, slots[i], slot)
            sources[i], source = (
                jnp.where(before, source, sources[i]),
                jnp.where(before, sources[i], source),
            )
    return slots, sources


def slot_at(position, arrivals, slot_count):
    kept = slot_count - len(arrivals)
    if position >= kept:
        return jnp.minimum(arrivals[position - kept], slot_count - 1)
    slot = jnp.int32(position)
    for arrival in arrivals:
        slot = slot + (slot >= arrival).astype(jnp.int32)
    return slot


def pack_kernel(inst_count, migration, queries, new_tokens, packs, sems):
    me = lax.axis_index("inst")
    width = queries.shape[2]
    copies = []
    for peer in range(inst_count):
        slot = route_of(migration, me, peer, True)
        for n, (source, start) in enumerate(((queries, 0), (new_tokens, width))):
            target = packs.at[peer, :, pl.ds(start, source.shape[2])]
            copies.append(pltpu.make_async_copy(source.at[slot], target, sems.at[peer, n]))
            copies[-1].start()
    for copy in copies:
        copy.wait()


def page_copies(pool, buffer, sems, page_table, item, slot):
    page_count = page_table.shape[0]
    for j in range(page_count):
        pltpu.make_async_copy(
            pool.at[page_table[j, slot]], buffer.at[item, j], sems.at[item]
        ).start()


def wait_copies(pool, buffer, sems, item):
    pltpu.make_async_copy(
        pool.at[pl.ds(0, buffer.shape[1])], buffer.at[item], sems.at[item]
    ).wait()


def away_kernel(
    inst_count, lengths, page_table, migration, received, pool, second, far_weight,
    answers, keep, send, buffer, sems,
):
    count = inst_count - 1
    page_count, slot_count = page_table.shape
    page_len = pool.shape[1]
    me = lax.axis_index("inst")
    _, step_count, width = answers.shape
    peers = [lax.rem(me + k, inst_count) for k in range(1, inst_count)]
    live = []
    for k, peer in enumerate(peers):
        slot = route_of(migration, me, peer, False)
        page_copies(pool, buffer, sems, page_table, k, slot)
        live.append(lengths[me * slot_count + slot] * page_len)
    project_far(second, far_weight, keep, send)
    items = [received[peer, me].astype(jnp.float32) for peer in peers]
    for k in range(count):
        wait_copies(pool, buffer, sems, k)
    result = attend_group(
        [item[:, :width] for item in items],
        [item[:, width:] for item in items],
        [[buffer.at[k, j] for j in range(page_count)] for k in range(count)],
        live,
        step_count,
    )
    answers[me] = jnp.zeros((step_count, width), answers.dtype)
    for peer, rows in zip(peers, result):
        answers[peer] = rows.astype(answers.dtype)


def project(rows, weight, first, columns, target, row_offset=0, offset=0):
    tile = min(512, columns)
    rows = rows[...]
    for j in range(0, columns, tile):
        start = pl.multiple_of(first + j, tile)
        target[row_offset : row_offset + rows.shape[0], offset + j : offset + j + tile] = jnp.dot(
            rows, weight[:, pl.ds(start, tile)], preferred_element_type=jnp.float32
        ).astype(target.dtype)


def project_far(attended, far_weight, keep, send):
    core = lax.rem(lax.axis_index("tp"), 2)
    chips = lax.axis_size("tp") // 2
    columns = far_weight.shape[1] // (2 * chips - 2)
    for target, side in ((send, 1 - core), (keep, core)):
        for d in range(chips - 1):
            first = (2 * d + side) * columns
            project(attended, far_weight, first, columns, target, 0, d * columns)


def attend_slots(
    inst_count, positions, migration, lengths, page_table, queries, new_tokens, pool, buffer, sems,
    between=lambda: None,
):
    page_count, slot_count = page_table.shape
    page_len = pool.shape[1]
    me = lax.axis_index("inst")
    arrivals, _ = arrivals_of(migration, inst_count)
    slots = [slot_at(position, arrivals, slot_count) for position in positions]
    for i, slot in enumerate(slots):
        page_copies(pool, buffer, sems, page_table, i, slot)
    between()
    rows = []
    for base in range(0, len(slots), GROUP):
        items = range(base, min(base + GROUP, len(slots)))
        for i in items:
            wait_copies(pool, buffer, sems, i)
        rows += attend_group(
            [queries[slots[i]].astype(jnp.float32) for i in items],
            [new_tokens[slots[i]].astype(jnp.float32) for i in items],
            [[buffer.at[i, j] for j in range(page_count)] for i in items],
            [lengths[me * slot_count + slots[i]] * page_len for i in items],
            queries.shape[1],
        )
    return rows


def store_rows(rows, target, at=0):
    step_count = rows[0].shape[0]
    for pair in range(0, len(rows), 2):
        start = at + pair * step_count
        target[start : start + 2 * step_count, :] = jnp.concatenate(
            rows[pair : pair + 2], axis=0
        ).astype(jnp.bfloat16)


def first_kernel(
    inst_count, migration, lengths, page_table, queries, new_tokens, pool, weight, after,
    attended, keep, send, far_weight, buffer, page_sems, weight_sems,
):
    own_tp = lax.axis_index("tp")
    chips = lax.axis_size("tp") // 2
    pair_columns = weight.shape[1] // chips

    def weight_copy(d):
        chip = lax.rem(own_tp // 2 + d, chips)
        start = pl.multiple_of(chip * pair_columns, pair_columns)
        return pltpu.make_async_copy(
            weight.at[:, pl.ds(start, pair_columns)],
            far_weight.at[:, pl.ds((d - 1) * pair_columns, pair_columns)],
            weight_sems.at[d - 1],
        )

    def between():
        for d in range(1, chips):
            weight_copy(d).start()

    count = attended.shape[0] // queries.shape[1]
    store_rows(
        attend_slots(
            inst_count, range(count), migration, lengths, page_table, queries, new_tokens, pool,
            buffer, page_sems, between,
        ),
        attended,
    )
    for d in range(1, chips):
        weight_copy(d).wait()
    project_far(attended, far_weight, keep, send)


def second_kernel(
    inst_count, first, migration, lengths, page_table, queries, new_tokens, pool, after,
    attended, extra, buffer, sems,
):
    count = attended.shape[0] // queries.shape[1]
    rows = attend_slots(
        inst_count, range(first, first + count + extra.shape[0]), migration, lengths, page_table,
        queries, new_tokens, pool, buffer, sems,
    )
    store_rows(rows[:count], attended)
    for i, row in enumerate(rows[count:]):
        extra[i] = row.astype(extra.dtype)


def own_kernel(weight, first, second, after, keep, *refs):
    sends, (near_weight, rows, sems) = refs[:-3], refs[-3:]
    core = lax.rem(lax.axis_index("tp"), 2)
    chip = lax.axis_index("tp") // 2
    columns = keep.shape[1]
    copies = []
    for n, side in enumerate((1 - core, core)):
        start = pl.multiple_of((chip * 2 + side) * columns, columns)
        copies.append(
            pltpu.make_async_copy(
                weight.at[:, pl.ds(start, columns)], near_weight.at[n], sems.at[n]
            )
        )
        copies[n].start()
    rows[: first.shape[0], :] = first[...]
    rows[first.shape[0] :, :] = second[...]
    copies[0].wait()
    at = 0
    for send in sends:
        project(rows, near_weight.at[0], at, send.shape[1], send)
        at += send.shape[1]
    copies[1].wait()
    project(rows, near_weight.at[1], 0, columns, keep)


def last_rows_kernel(
    inst_count, migration, near_weight, far_weight, extra, answers, keep, send, rows
):
    core = lax.rem(lax.axis_index("tp"), 2)
    chips = lax.axis_size("tp") // 2
    columns = keep.shape[1]
    _, sources = arrivals_of(migration, inst_count)
    last = [extra[i].astype(jnp.float32) for i in range(extra.shape[0])]
    me = lax.axis_index("inst")
    last += [answers[source, me].astype(jnp.float32) for source in sources]
    size = rows.shape[0]
    store_rows(last, rows)
    for n, (target, side) in enumerate(((send, 1 - core), (keep, core))):
        for d in range(chips - 1):
            project(rows, far_weight, (2 * d + side) * columns, columns, target, d * size)
        project(rows, near_weight.at[n], 0, columns, target, (chips - 1) * size)


def sum_kernel(inst_count, chunks, piece_count, migration, keep, *refs):
    mates, parts, (out, staged, sem) = refs[:piece_count], refs[piece_count:-3], refs[-3:]
    slot_count, step_count, _ = out.shape
    pair = 2 * step_count
    width = mates[0].shape[1]
    arrivals, _ = arrivals_of(migration, inst_count)
    share = len(parts) // len(chunks)
    at = 0
    for n, chunk in enumerate(chunks):
        for base in range(0, chunk, pair):
            for m, mate in enumerate(mates):
                columns = slice(m * width, (m + 1) * width)
                total = keep[at : at + pair, columns] + mate[at : at + pair, :].astype(jnp.float32)
                for part in parts[n * share : (n + 1) * share]:
                    total = total + part[base : base + pair, columns].astype(jnp.float32)
                total = total.astype(jnp.bfloat16)
                for half in range(2):
                    staged[at // step_count + half, :, columns] = total[
                        half * step_count : (half + 1) * step_count
                    ]
            at += pair
    scatter_rows(staged, out, arrivals, 0, sem)


def scatter_rows(staged, out, arrivals, first, sem):
    slot_count = out.shape[0]
    for i in range(staged.shape[0]):
        slot = slot_at(first + i, arrivals, slot_count)
        pltpu.make_async_copy(staged.at[i], out.at[slot], sem.at[0]).start()
    pltpu.make_async_copy(staged, out.at[pl.ds(0, staged.shape[0])], sem.at[0]).wait()


def last_kernel(inst_count, first, migration, keep, mate, *refs):
    parts, (out, staged, sem) = refs[:-4], refs[-3:]
    step_count = out.shape[1]
    pair = 2 * step_count
    size = parts[0].shape[0]
    arrivals, _ = arrivals_of(migration, inst_count)
    for at in range(0, size, pair):
        own = keep.shape[0] - size + at
        total = keep[own : own + pair, :] + mate[own : own + pair, :].astype(jnp.float32)
        for part in parts:
            total = total + part[at : at + pair, :].astype(jnp.float32)
        total = total.astype(jnp.bfloat16)
        for half in range(2):
            staged[at // step_count + half] = total[half * step_count : (half + 1) * step_count]
    scatter_rows(staged, out, arrivals, first, sem)


def in_hbm(value):
    return pltpu.with_memory_space_constraint(value, pltpu.HBM)


def in_vmem(value):
    return pltpu.with_memory_space_constraint(value, pltpu.VMEM)


def on_device(queries, new_kv, kv_pool, out_weight, lengths, page_table, migration):
    inst_count = lax.axis_size("inst")
    tp_count = lax.axis_size("tp")
    chips = tp_count // 2
    slot_count, page_count = page_table.shape
    row_count, width = queries.shape
    step_count = row_count // slot_count
    queries = in_hbm(queries.reshape(slot_count, step_count, width))
    new_tokens = in_hbm(new_kv[0].reshape(slot_count, step_count, new_kv.shape[2]))
    pool = in_hbm(kv_pool[0])
    page_shape = pool.shape[1:]
    columns = out_weight.shape[1] // tp_count
    incoming = migration.shape[0] // inst_count
    weight = in_hbm(out_weight)
    lengths = in_hbm(lengths)
    page_table = in_hbm(page_table.T)
    migration = in_hbm(migration.T)
    limit = pltpu.CompilerParams(vmem_limit_bytes=32 * 2**20)
    light = pl.CostEstimate(flops=1, bytes_accessed=1, transcendentals=0)
    bf16, f32 = jnp.bfloat16, jnp.float32
    shape = jax.ShapeDtypeStruct
    swap = [(t, t ^ 1) for t in range(tp_count)]
    far = (chips - 1) * columns

    def hold(value, until):
        return pl.pallas_call(
            lambda *refs: None,
            out_shape=pltpu.VMEM(value.shape, value.dtype),
            in_specs=[ANY] * (1 + len(until)),
            out_specs=ANY,
            input_output_aliases={0: 0},
            compiler_params=pltpu.CompilerParams(vmem_limit_bytes=2**20),
            cost_estimate=light,
            name="hold",
        )(in_vmem(value), *until)

    def send_far(summed):
        return [
            lax.ppermute(
                part, "tp", [(t, (t + 2 * d) % tp_count) for t in range(tp_count)]
            )
            for d, part in enumerate(summed, 1)
        ]

    def split_far(summed):
        return [summed[:, d * columns : (d + 1) * columns] for d in range(chips - 1)]

    def chunk_shapes(count):
        rows = count * step_count
        return [pltpu.VMEM((rows, far), f32), pltpu.VMEM((rows, far), bf16)]

    def rows_shape(count):
        return pltpu.VMEM((count * step_count, width), bf16)

    def page_scratch(count):
        return [
            pltpu.VMEM((count, page_count, *page_shape), bf16),
            pltpu.SemaphoreType.DMA((count,)),
        ]

    last_count = incoming + incoming % 2
    extra_count = last_count - incoming
    first_count = slot_count // 4 * 2
    second_count = slot_count - first_count - last_count
    last_rows = last_count * step_count

    packs = pl.pallas_call(
        functools.partial(pack_kernel, inst_count),
        out_shape=shape((inst_count, step_count, width + new_tokens.shape[2]), bf16),
        in_specs=[SMEM, ANY, ANY],
        out_specs=VMEM,
        scratch_shapes=[pltpu.SemaphoreType.DMA((inst_count, 2))],
        compiler_params=limit,
        cost_estimate=light,
        name="pack",
    )(migration, queries, new_tokens)
    received = lax.all_gather(packs, "inst")

    first, keep, send, far_weight = pl.pallas_call(
        functools.partial(first_kernel, inst_count),
        out_shape=[
            rows_shape(first_count),
            *chunk_shapes(first_count),
            pltpu.VMEM((width, 2 * far), bf16),
        ],
        in_specs=[SMEM, SMEM, SMEM, VMEM, VMEM, ANY, ANY, ANY],
        out_specs=[VMEM] * 4,
        scratch_shapes=page_scratch(first_count) + [pltpu.SemaphoreType.DMA((chips - 1,))],
        compiler_params=limit,
        cost_estimate=light,
        name="attend_first",
    )(migration, lengths, page_table, queries, new_tokens, pool, weight, packs)
    far_weight = in_vmem(far_weight)
    mate = lax.ppermute(send, "tp", swap)
    summed = (keep + mate.astype(f32)).astype(bf16)
    arrived_first = send_far(split_far(summed))

    second, extra = pl.pallas_call(
        functools.partial(second_kernel, inst_count, first_count),
        out_shape=[
            rows_shape(second_count),
            pltpu.VMEM((extra_count, step_count, width), bf16),
        ],
        in_specs=[SMEM, SMEM, SMEM, VMEM, VMEM, ANY, ANY],
        out_specs=[VMEM] * 2,
        scratch_shapes=page_scratch(second_count + extra_count),
        compiler_params=limit,
        cost_estimate=light,
        name="attend_second",
    )(migration, lengths, page_table, queries, new_tokens, pool, summed)
    second = in_vmem(second)
    answers, keep, send = pl.pallas_call(
        functools.partial(away_kernel, inst_count),
        out_shape=[
            shape((inst_count, step_count, width), bf16),
            *chunk_shapes(second_count),
        ],
        in_specs=[SMEM, SMEM, SMEM, VMEM, ANY, VMEM, VMEM],
        out_specs=[VMEM] * 3,
        scratch_shapes=page_scratch(inst_count - 1),
        compiler_params=limit,
        cost_estimate=light,
        name="attend_away",
    )(lengths, page_table, migration, received, pool, second, far_weight)
    mate = lax.ppermute(send, "tp", swap)
    answers = lax.all_gather(answers, "inst")
    keep = hold(keep, arrived_first)
    summed = (keep + mate.astype(f32)).astype(bf16)
    arrived_second = send_far(split_far(summed))

    early_rows = (first_count + second_count) * step_count
    pieces = 2
    early_keep, *early_sends, near_weight = pl.pallas_call(
        own_kernel,
        out_shape=[
            pltpu.VMEM((early_rows, columns), f32),
            *[pltpu.VMEM((early_rows, columns // pieces), bf16)] * pieces,
            pltpu.VMEM((2, width, columns), bf16),
        ],
        in_specs=[ANY, VMEM, VMEM, ANY],
        out_specs=[VMEM] * (2 + pieces),
        scratch_shapes=[
            pltpu.VMEM((early_rows, width), bf16),
            pltpu.SemaphoreType.DMA((2,)),
        ],
        compiler_params=limit,
        cost_estimate=light,
        name="own_columns",
    )(weight, in_vmem(first), second, summed)
    early_mates = [lax.ppermute(early_send, "tp", swap) for early_send in early_sends]

    keep, send = pl.pallas_call(
        functools.partial(last_rows_kernel, inst_count),
        out_shape=[
            pltpu.VMEM((last_rows * chips, columns), f32),
            pltpu.VMEM((last_rows * chips, columns), bf16),
        ],
        in_specs=[SMEM] + [VMEM] * 4,
        out_specs=[VMEM] * 2,
        scratch_shapes=[pltpu.VMEM((last_rows, width), bf16)],
        compiler_params=limit,
        cost_estimate=light,
        name="last_rows",
    )(migration, in_vmem(near_weight), far_weight, in_vmem(extra), answers)
    mate = lax.ppermute(send, "tp", swap)
    keep = hold(keep, arrived_second)
    summed = (keep[:-last_rows] + mate[:-last_rows].astype(f32)).astype(bf16)
    arrived_last = send_far([summed[d * last_rows : (d + 1) * last_rows] for d in range(chips - 1)])

    early = slot_count - last_count
    out_shape = (slot_count, step_count, columns)
    out = pl.pallas_call(
        functools.partial(
            sum_kernel, inst_count, [first_count * step_count, second_count * step_count], pieces
        ),
        out_shape=pltpu.HBM(out_shape, bf16),
        in_specs=[SMEM] + [VMEM] * (1 + pieces + 2 * (chips - 1)),
        out_specs=ANY,
        scratch_shapes=[
            pltpu.VMEM((early, step_count, columns), bf16),
            pltpu.SemaphoreType.DMA((1,)),
        ],
        compiler_params=limit,
        cost_estimate=light,
        name="sum_early",
    )(migration, in_vmem(early_keep), *early_mates, *arrived_first, *arrived_second)
    out = pl.pallas_call(
        functools.partial(last_kernel, inst_count, early),
        out_shape=pltpu.HBM(out_shape, bf16),
        in_specs=[SMEM] + [VMEM] * (chips + 1) + [ANY],
        out_specs=ANY,
        scratch_shapes=[
            pltpu.VMEM((last_count, step_count, columns), bf16),
            pltpu.SemaphoreType.DMA((1,)),
        ],
        input_output_aliases={2 + chips: 0},
        compiler_params=limit,
        cost_estimate=light,
        name="sum_last",
    )(migration, in_vmem(keep), mate, *arrived_last, out)
    return out.reshape(row_count, columns)


def solution(mesh):
    placed = (
        P(("group", "inst"), "tp"),
        P("tp", ("group", "inst"), None),
        P("tp", ("group", "inst"), None, None),
        P("tp", None),
        P("group"),
        P(("group", "inst"), None),
        P("group", None),
    )
    return jax.shard_map(
        on_device, mesh=mesh, in_specs=placed, out_specs=P(("group", "inst"), "tp"), check_vma=False
    )
```

```python
import functools

import jax
import jax.numpy as jnp
from jax import lax
from jax.experimental import pallas as pl
from jax.experimental.pallas import tpu as pltpu
from jax.sharding import PartitionSpec as P

LOG2E = 1.4426950408889634
MASKED = -1e30
GROUP = 6
NEVER = 2**30

VMEM = pl.BlockSpec(memory_space=pltpu.VMEM)
SMEM = pl.BlockSpec(memory_space=pltpu.SMEM)
ANY = pl.BlockSpec(memory_space=pl.ANY)


def attend_group(queries, tokens, contexts, live_lengths, step_count):
    count = len(queries)
    head_dim = tokens[0].shape[1] // 2
    head_count = queries[0].shape[1] // head_dim
    rows = head_count * step_count
    gain = LOG2E / head_dim**0.5
    stacked = jnp.concatenate(
        [
            query[:, h * head_dim : (h + 1) * head_dim]
            for query in queries
            for h in range(head_count)
        ],
        axis=0,
    ).astype(jnp.bfloat16)
    tokens = jnp.concatenate(tokens, axis=0).astype(jnp.bfloat16)
    score_new = contract_last(stacked, tokens[:, :head_dim])
    row_ids = lax.broadcasted_iota(jnp.int32, score_new.shape, 0)
    column_ids = lax.broadcasted_iota(jnp.int32, score_new.shape, 1)
    allowed = (row_ids // rows == column_ids // step_count) & (
        column_ids % step_count <= row_ids % step_count
    )
    score_new = jnp.where(allowed, score_new, MASKED)
    new_max = jnp.max(score_new, axis=1, keepdims=True)
    maxima, scores = [], []
    for g in range(count):
        keys = jnp.concatenate([page[:, :head_dim] for page in contexts[g]], axis=0)
        score = contract_last(stacked[g * rows : (g + 1) * rows], keys)
        position = lax.broadcasted_iota(jnp.int32, score.shape, 1)
        score = jnp.where(position < live_lengths[g], score, MASKED)
        scores.append(score)
        maxima.append(
            jnp.maximum(
                jnp.max(score, axis=1, keepdims=True), new_max[g * rows : (g + 1) * rows]
            )
        )
    exp_new = jnp.exp2((score_new - jnp.concatenate(maxima, axis=0)) * gain)
    new_total = jnp.sum(exp_new, axis=1, keepdims=True)
    results, inverses = [], []
    for g in range(count):
        exp_ctx = jnp.exp2((scores[g] - maxima[g]) * gain)
        total = jnp.sum(exp_ctx, axis=1, keepdims=True) + new_total[g * rows : (g + 1) * rows]
        inverse = 1.0 / total
        inverses.append(inverse)
        values = jnp.concatenate([page[:, head_dim:] for page in contexts[g]], axis=0)
        results.append(
            jnp.dot(
                (exp_ctx * inverse).astype(jnp.bfloat16),
                values,
                preferred_element_type=jnp.float32,
            )
        )
    weight_new = (exp_new * jnp.concatenate(inverses, axis=0)).astype(jnp.bfloat16)
    result = jnp.concatenate(results, axis=0) + jnp.dot(
        weight_new, tokens[:, head_dim:], preferred_element_type=jnp.float32
    )
    return [
        jnp.concatenate(
            [
                result[g * rows + h * step_count : g * rows + (h + 1) * step_count]
                for h in range(head_count)
            ],
            axis=1,
        )
        for g in range(count)
    ]


def contract_last(a, b):
    return lax.dot_general(a, b, (((1,), (1,)), ((), ())), preferred_element_type=jnp.float32)


def route_of(migration, own_index, peer, arriving):
    ours, theirs, slot_row = (2, 0, 3) if arriving else (0, 2, 1)
    slot = jnp.int32(0)
    for row in range(migration.shape[1]):
        match = (migration[ours, row] == own_index) & (migration[theirs, row] == peer)
        slot = jnp.where(match, migration[slot_row, row], slot)
    return slot


def arrivals_of(migration, inst_count):
    me = lax.axis_index("inst")
    incoming = migration.shape[1] // inst_count
    slots = [jnp.int32(NEVER)] * incoming
    sources = [jnp.int32(0)] * incoming
    for row in range(migration.shape[1]):
        slot = jnp.where(migration[2, row] == me, migration[3, row], NEVER)
        source = migration[0, row]
        for i in range(incoming):
            before = slot < slots[i]
            slots[i], slot = jnp.where(before, slot, slots[i]), jnp.where(before, slots[i], slot)
            sources[i], source = (
                jnp.where(before, source, sources[i]),
                jnp.where(before, sources[i], source),
            )
    return slots, sources


def slot_at(position, arrivals, slot_count):
    kept = slot_count - len(arrivals)
    if position >= kept:
        return jnp.minimum(arrivals[position - kept], slot_count - 1)
    slot = jnp.int32(position)
    for arrival in arrivals:
        slot = slot + (slot >= arrival).astype(jnp.int32)
    return slot


def peer_of(me, k, count):
    return me ^ k if count & (count - 1) == 0 else (count - me + k) % count


def pack_rows(inst_count, migration, queries, new_tokens, packs):
    me = lax.axis_index("inst")
    width = queries.shape[2]
    for k, pack in packs.items():
        slot = route_of(migration, me, peer_of(me, k, inst_count), True)
        pack[:, :width] = queries[slot]
        pack[:, width:] = new_tokens[slot]


def page_copies(pool, buffer, sems, page_table, item, slot):
    page_count = page_table.shape[0]
    for j in range(page_count):
        pltpu.make_async_copy(
            pool.at[page_table[j, slot]], buffer.at[item, j], sems.at[item]
        ).start()


def wait_copies(pool, buffer, sems, item):
    pltpu.make_async_copy(
        pool.at[pl.ds(0, buffer.shape[1])], buffer.at[item], sems.at[item]
    ).wait()


def away_slot(migration, inst_count, k):
    me = lax.axis_index("inst")
    return route_of(migration, me, peer_of(me, k, inst_count), False)


def away_kernel(
    inst_count, rounds, lengths, migration, pages, second, far_weight, *refs
):
    count = len(rounds)
    received, answers, (keep, send) = refs[:count], refs[count : 2 * count], refs[2 * count :]
    _, page_count, page_len, _ = pages.shape
    step_count, width = answers[0].shape
    first = lax.axis_index("inst") * (lengths.shape[0] // inst_count)
    result = attend_group(
        [ref[:, :width].astype(jnp.float32) for ref in received],
        [ref[:, width:].astype(jnp.float32) for ref in received],
        [[pages.at[i, j] for j in range(page_count)] for i in range(count)],
        [lengths[first + away_slot(migration, inst_count, k)] * page_len for k in rounds],
        step_count,
    )
    for answer, rows in zip(answers, result):
        answer[...] = rows.astype(answer.dtype)
    project_far(second, far_weight, keep, send)


def project(rows, weight, first, columns, target, row_offset=0, offset=0):
    tile = min(512, columns)
    rows = rows[...]
    for j in range(0, columns, tile):
        start = pl.multiple_of(first + j, tile)
        target[row_offset : row_offset + rows.shape[0], offset + j : offset + j + tile] = jnp.dot(
            rows, weight[:, pl.ds(start, tile)], preferred_element_type=jnp.float32
        ).astype(target.dtype)


def project_far(attended, far_weight, keep, send):
    core = lax.rem(lax.axis_index("tp"), 2)
    chips = lax.axis_size("tp") // 2
    columns = far_weight.shape[1] // (2 * chips - 2)
    for target, side in ((send, 1 - core), (keep, core)):
        for d in range(chips - 1):
            first = (2 * d + side) * columns
            project(attended, far_weight, first, columns, target, 0, d * columns)


def attend_slots(slots, lengths, queries, new_tokens, pages, wait=lambda i: None):
    page_count, page_len = pages.shape[1:3]
    first = lax.axis_index("inst") * queries.shape[0]
    rows = []
    for base in range(0, len(slots), GROUP):
        items = range(base, min(base + GROUP, len(slots)))
        for i in items:
            wait(i)
        rows += attend_group(
            [queries[slots[i]].astype(jnp.float32) for i in items],
            [new_tokens[slots[i]].astype(jnp.float32) for i in items],
            [[pages.at[i, j] for j in range(page_count)] for i in items],
            [lengths[first + slots[i]] * page_len for i in items],
            queries.shape[1],
        )
    return rows


def store_rows(rows, target, at=0):
    step_count = rows[0].shape[0]
    for pair in range(0, len(rows), 2):
        start = at + pair * step_count
        target[start : start + 2 * step_count, :] = jnp.concatenate(
            rows[pair : pair + 2], axis=0
        ).astype(jnp.bfloat16)


def first_kernel(
    inst_count, rounds, migration, lengths, page_table, queries_in, new_in, pool, weight,
    attended, keep, send, far_weight, queries, new_tokens, second_pages, away_pages, *refs,
):
    packs = dict(zip(rounds, refs))
    buffer, small_sems, first_sems, second_sems, away_sems, weight_sems = refs[len(rounds) :]
    own_tp = lax.axis_index("tp")
    chips = lax.axis_size("tp") // 2
    pair_columns = weight.shape[1] // chips
    slot_count, step_count, _ = queries.shape
    small = [
        pltpu.make_async_copy(queries_in, queries, small_sems.at[0]),
        pltpu.make_async_copy(new_in, new_tokens, small_sems.at[1]),
    ]
    for copy in small:
        copy.start()
    arrivals, _ = arrivals_of(migration, inst_count)
    count = attended.shape[0] // step_count
    total = count + second_pages.shape[0]
    slots = [slot_at(position, arrivals, slot_count) for position in range(total)]
    for i in range(count):
        page_copies(pool, buffer, first_sems, page_table, i, slots[i])

    def weight_copy(d):
        chip = lax.rem(own_tp // 2 + d, chips)
        start = pl.multiple_of(chip * pair_columns, pair_columns)
        return pltpu.make_async_copy(
            weight.at[:, pl.ds(start, pair_columns)],
            far_weight.at[:, pl.ds((d - 1) * pair_columns, pair_columns)],
            weight_sems.at[d - 1],
        )

    for d in range(1, chips):
        weight_copy(d).start()
    for i, slot in enumerate(slots[count:]):
        page_copies(pool, second_pages, second_sems, page_table, i, slot)
    for i, k in enumerate(rounds):
        slot = away_slot(migration, inst_count, k)
        page_copies(pool, away_pages, away_sems, page_table, i, slot)
    for copy in small:
        copy.wait()
    pack_rows(inst_count, migration, queries, new_tokens, packs)
    store_rows(
        attend_slots(
            slots[:count], lengths, queries, new_tokens, buffer,
            lambda i: wait_copies(pool, buffer, first_sems, i),
        ),
        attended,
    )
    for d in range(1, chips):
        weight_copy(d).wait()
    project_far(attended, far_weight, keep, send)
    for i in range(total - count):
        wait_copies(pool, second_pages, second_sems, i)
    for i in range(len(rounds)):
        wait_copies(pool, away_pages, away_sems, i)


def second_kernel(
    inst_count, first, migration, lengths, queries, new_tokens, pages, weight, after,
    attended, extra, near_weight, sems,
):
    slot_count, step_count, _ = queries.shape
    core = lax.rem(lax.axis_index("tp"), 2)
    chip = lax.axis_index("tp") // 2
    columns = near_weight.shape[2]
    copies = []
    for n, side in enumerate((1 - core, core)):
        start = pl.multiple_of((chip * 2 + side) * columns, columns)
        copies.append(
            pltpu.make_async_copy(
                weight.at[:, pl.ds(start, columns)], near_weight.at[n], sems.at[n]
            )
        )
        copies[n].start()
    arrivals, _ = arrivals_of(migration, inst_count)
    slots = [slot_at(first + i, arrivals, slot_count) for i in range(pages.shape[0])]
    rows = attend_slots(slots, lengths, queries, new_tokens, pages)
    count = attended.shape[0] // step_count
    store_rows(rows[:count], attended)
    for i, row in enumerate(rows[count:]):
        extra[i] = row.astype(extra.dtype)
    for copy in copies:
        copy.wait()


def own_kernel(near_weight, first, second, after, keep, *refs):
    sends, rows = refs[:-1], refs[-1]
    rows[: first.shape[0], :] = first[...]
    rows[first.shape[0] :, :] = second[...]
    at = 0
    for send in sends:
        project(rows, near_weight.at[0], at, send.shape[1], send)
        at += send.shape[1]
    project(rows, near_weight.at[1], 0, keep.shape[1], keep)


def last_rows_kernel(
    inst_count, rounds, migration, near_weight, far_weight, extra, after, *refs
):
    answers, (keep, send, rows) = refs[:-3], refs[-3:]
    core = lax.rem(lax.axis_index("tp"), 2)
    chips = lax.axis_size("tp") // 2
    me = lax.axis_index("inst")
    columns = keep.shape[1]
    _, sources = arrivals_of(migration, inst_count)
    last = [extra[i].astype(jnp.float32) for i in range(extra.shape[0])]
    given = [answer[...].astype(jnp.float32) for answer in answers]
    for source in sources:
        row = given[0]
        for k, answer in zip(rounds[1:], given[1:]):
            row = jnp.where(source == peer_of(me, k, inst_count), answer, row)
        last.append(row)
    size = rows.shape[0]
    store_rows(last, rows)
    for n, (target, side) in enumerate(((send, 1 - core), (keep, core))):
        for d in range(chips - 1):
            project(rows, far_weight, (2 * d + side) * columns, columns, target, d * size)
        project(rows, near_weight.at[n], 0, columns, target, (chips - 1) * size)


def sum_kernel(inst_count, chunks, piece_count, migration, keep, *refs):
    mates, parts, (out, staged, sem) = refs[:piece_count], refs[piece_count:-3], refs[-3:]
    slot_count, step_count, _ = out.shape
    pair = 2 * step_count
    width = mates[0].shape[1]
    arrivals, _ = arrivals_of(migration, inst_count)
    share = len(parts) // len(chunks)
    at = 0
    for n, chunk in enumerate(chunks):
        for base in range(0, chunk, pair):
            for m, mate in enumerate(mates):
                columns = slice(m * width, (m + 1) * width)
                total = keep[at : at + pair, columns] + mate[at : at + pair, :].astype(jnp.float32)
                for part in parts[n * share : (n + 1) * share]:
                    total = total + part[base : base + pair, columns].astype(jnp.float32)
                total = total.astype(jnp.bfloat16)
                for half in range(2):
                    staged[at // step_count + half, :, columns] = total[
                        half * step_count : (half + 1) * step_count
                    ]
            at += pair
    scatter_rows(staged, out, arrivals, 0, sem)


def scatter_rows(staged, out, arrivals, first, sem):
    slot_count = out.shape[0]
    for i in range(staged.shape[0]):
        slot = slot_at(first + i, arrivals, slot_count)
        pltpu.make_async_copy(staged.at[i], out.at[slot], sem.at[0]).start()
    pltpu.make_async_copy(staged, out.at[pl.ds(0, staged.shape[0])], sem.at[0]).wait()


def last_kernel(inst_count, first, migration, keep, mate, *refs):
    parts, (out, staged, sem) = refs[:-4], refs[-3:]
    step_count = out.shape[1]
    pair = 2 * step_count
    size = parts[0].shape[0]
    arrivals, _ = arrivals_of(migration, inst_count)
    for at in range(0, size, pair):
        own = keep.shape[0] - size + at
        total = keep[own : own + pair, :] + mate[own : own + pair, :].astype(jnp.float32)
        for part in parts:
            total = total + part[at : at + pair, :].astype(jnp.float32)
        total = total.astype(jnp.bfloat16)
        for half in range(2):
            staged[at // step_count + half] = total[half * step_count : (half + 1) * step_count]
    scatter_rows(staged, out, arrivals, first, sem)


def in_hbm(value):
    return pltpu.with_memory_space_constraint(value, pltpu.HBM)


def in_vmem(value):
    return pltpu.with_memory_space_constraint(value, pltpu.VMEM)


def on_device(queries, new_kv, kv_pool, out_weight, lengths, page_table, migration):
    inst_count = lax.axis_size("inst")
    tp_count = lax.axis_size("tp")
    chips = tp_count // 2
    slot_count, page_count = page_table.shape
    row_count, width = queries.shape
    step_count = row_count // slot_count
    queries = in_hbm(queries.reshape(slot_count, step_count, width))
    new_tokens = in_hbm(new_kv[0].reshape(slot_count, step_count, new_kv.shape[2]))
    pool = in_hbm(kv_pool[0])
    columns = out_weight.shape[1] // tp_count
    incoming = migration.shape[0] // inst_count
    weight = in_hbm(out_weight)
    lengths = in_hbm(lengths)
    page_table = in_hbm(page_table.T)
    migration = in_hbm(migration.T)
    limit = pltpu.CompilerParams(vmem_limit_bytes=32 * 2**20)
    light = pl.CostEstimate(flops=1, bytes_accessed=1, transcendentals=0)
    bf16, f32 = jnp.bfloat16, jnp.float32
    shape = jax.ShapeDtypeStruct
    swap = [(t, t ^ 1) for t in range(tp_count)]
    far = (chips - 1) * columns

    def hold(value, until):
        return pl.pallas_call(
            lambda *refs: None,
            out_shape=pltpu.VMEM(value.shape, value.dtype),
            in_specs=[ANY] * (1 + len(until)),
            out_specs=ANY,
            input_output_aliases={0: 0},
            compiler_params=pltpu.CompilerParams(vmem_limit_bytes=2**20),
            cost_estimate=light,
            name="hold",
        )(in_vmem(value), *until)

    def send_far(summed):
        return [
            lax.ppermute(
                part, "tp", [(t, (t + 2 * d) % tp_count) for t in range(tp_count)]
            )
            for d, part in enumerate(summed, 1)
        ]

    def split_far(summed):
        return [summed[:, d * columns : (d + 1) * columns] for d in range(chips - 1)]

    def chunk_shapes(count):
        rows = count * step_count
        return [pltpu.VMEM((rows, far), f32), pltpu.VMEM((rows, far), bf16)]

    def rows_shape(count):
        return pltpu.VMEM((count * step_count, width), bf16)

    last_count = incoming + incoming % 2
    extra_count = last_count - incoming
    first_count = slot_count // 4 * 2
    second_count = slot_count - first_count - last_count
    last_rows = last_count * step_count

    def page_shape(count):
        return pltpu.VMEM((count, page_count, *pool.shape[1:]), bf16)

    dma = pltpu.SemaphoreType.DMA
    rounds = [
        k
        for k in range(inst_count)
        if any(peer_of(i, k, inst_count) != i for i in range(inst_count))
    ]
    pairs = {k: [(i, peer_of(i, k, inst_count)) for i in range(inst_count)] for k in rounds}
    rest_count = second_count + extra_count
    (
        first, keep, send, far_weight, queries, new_tokens, second_pages, away_pages, *packs
    ) = pl.pallas_call(
        functools.partial(first_kernel, inst_count, rounds),
        out_shape=[
            rows_shape(first_count),
            *chunk_shapes(first_count),
            pltpu.VMEM((width, 2 * far), bf16),
            pltpu.VMEM(queries.shape, bf16),
            pltpu.VMEM(new_tokens.shape, bf16),
            page_shape(rest_count),
            page_shape(len(rounds)),
        ]
        + [shape((step_count, width + new_tokens.shape[2]), bf16)] * len(rounds),
        in_specs=[SMEM, SMEM, SMEM, ANY, ANY, ANY, ANY],
        out_specs=[VMEM] * (8 + len(rounds)),
        scratch_shapes=[
            page_shape(first_count),
            dma((2,)),
            dma((first_count,)),
            dma((rest_count,)),
            dma((len(rounds),)),
            dma((chips - 1,)),
        ],
        compiler_params=limit,
        cost_estimate=light,
        name="attend_first",
    )(migration, lengths, page_table, queries, new_tokens, pool, weight)
    far_weight = in_vmem(far_weight)
    mate = lax.ppermute(send, "tp", swap)
    summed = (keep + mate.astype(f32)).astype(bf16)
    arrived_first = send_far(split_far(summed))
    received = [lax.ppermute(pack, "inst", pairs[k]) for k, pack in zip(rounds, packs)]

    second, extra, near_weight = pl.pallas_call(
        functools.partial(second_kernel, inst_count, first_count),
        out_shape=[
            rows_shape(second_count),
            pltpu.VMEM((extra_count, step_count, width), bf16),
            pltpu.VMEM((2, width, columns), bf16),
        ],
        in_specs=[SMEM, SMEM, VMEM, VMEM, VMEM, ANY, ANY],
        out_specs=[VMEM] * 3,
        scratch_shapes=[dma((2,))],
        compiler_params=limit,
        cost_estimate=light,
        name="attend_second",
    )(
        migration, lengths, in_vmem(queries), in_vmem(new_tokens), in_vmem(second_pages), weight,
        summed,
    )
    second, near_weight = in_vmem(second), in_vmem(near_weight)
    *answers, keep, send = pl.pallas_call(
        functools.partial(away_kernel, inst_count, rounds),
        out_shape=[shape((step_count, width), bf16)] * len(rounds) + chunk_shapes(second_count),
        in_specs=[SMEM, SMEM] + [VMEM] * (3 + len(rounds)),
        out_specs=[VMEM] * (2 + len(rounds)),
        compiler_params=limit,
        cost_estimate=light,
        name="attend_away",
    )(lengths, migration, in_vmem(away_pages), second, far_weight, *received)
    mate = lax.ppermute(send, "tp", swap)
    answers = [lax.ppermute(answer, "inst", pairs[k]) for k, answer in zip(rounds, answers)]
    keep = hold(keep, arrived_first)
    summed = (keep + mate.astype(f32)).astype(bf16)
    arrived_second = send_far(split_far(summed))

    early_rows = (first_count + second_count) * step_count
    pieces = 2
    early_keep, *early_sends = pl.pallas_call(
        own_kernel,
        out_shape=[
            pltpu.VMEM((early_rows, columns), f32),
            *[pltpu.VMEM((early_rows, columns // pieces), bf16)] * pieces,
        ],
        in_specs=[VMEM, VMEM, VMEM, ANY],
        out_specs=[VMEM] * (1 + pieces),
        scratch_shapes=[pltpu.VMEM((early_rows, width), bf16)],
        compiler_params=limit,
        cost_estimate=light,
        name="own_columns",
    )(near_weight, in_vmem(first), second, summed)
    early_mates = [lax.ppermute(early_send, "tp", swap) for early_send in early_sends]

    keep, send = pl.pallas_call(
        functools.partial(last_rows_kernel, inst_count, rounds),
        out_shape=[
            pltpu.VMEM((last_rows * chips, columns), f32),
            pltpu.VMEM((last_rows * chips, columns), bf16),
        ],
        in_specs=[SMEM] + [VMEM] * 3 + [ANY] + [VMEM] * len(rounds),
        out_specs=[VMEM] * 2,
        scratch_shapes=[pltpu.VMEM((last_rows, width), bf16)],
        compiler_params=limit,
        cost_estimate=light,
        name="last_rows",
    )(migration, near_weight, far_weight, in_vmem(extra), early_keep, *answers)
    mate = lax.ppermute(send, "tp", swap)
    keep = hold(keep, arrived_second)
    summed = (keep[:-last_rows] + mate[:-last_rows].astype(f32)).astype(bf16)
    arrived_last = send_far([summed[d * last_rows : (d + 1) * last_rows] for d in range(chips - 1)])

    early = slot_count - last_count
    out_shape = (slot_count, step_count, columns)
    out = pl.pallas_call(
        functools.partial(
            sum_kernel, inst_count, [first_count * step_count, second_count * step_count], pieces
        ),
        out_shape=pltpu.HBM(out_shape, bf16),
        in_specs=[SMEM] + [VMEM] * (1 + pieces + 2 * (chips - 1)),
        out_specs=ANY,
        scratch_shapes=[
            pltpu.VMEM((early, step_count, columns), bf16),
            pltpu.SemaphoreType.DMA((1,)),
        ],
        compiler_params=limit,
        cost_estimate=light,
        name="sum_early",
    )(migration, in_vmem(early_keep), *early_mates, *arrived_first, *arrived_second)
    out = pl.pallas_call(
        functools.partial(last_kernel, inst_count, early),
        out_shape=pltpu.HBM(out_shape, bf16),
        in_specs=[SMEM] + [VMEM] * (chips + 1) + [ANY],
        out_specs=ANY,
        scratch_shapes=[
            pltpu.VMEM((last_count, step_count, columns), bf16),
            pltpu.SemaphoreType.DMA((1,)),
        ],
        input_output_aliases={2 + chips: 0},
        compiler_params=limit,
        cost_estimate=light,
        name="sum_last",
    )(migration, in_vmem(keep), mate, *arrived_last, out)
    return out.reshape(row_count, columns)


def solution(mesh):
    placed = (
        P(("group", "inst"), "tp"),
        P("tp", ("group", "inst"), None),
        P("tp", ("group", "inst"), None, None),
        P("tp", None),
        P("group"),
        P(("group", "inst"), None),
        P("group", None),
    )
    return jax.shard_map(
        on_device, mesh=mesh, in_specs=placed, out_specs=P(("group", "inst"), "tp"), check_vma=False
    )
```

```python
import functools

import jax
import jax.numpy as jnp
from jax import lax
from jax.experimental import pallas as pl
from jax.experimental.pallas import tpu as pltpu
from jax.sharding import PartitionSpec as P

LOG2E = 1.4426950408889634
MASKED = -1e30
GROUP = 8
NEVER = 2**30
PIECES = 2

VMEM = pl.BlockSpec(memory_space=pltpu.VMEM)
SMEM = pl.BlockSpec(memory_space=pltpu.SMEM)
ANY = pl.BlockSpec(memory_space=pl.ANY)


def attend_group(queries, tokens, contexts, live_lengths, step_count):
    count = len(queries)
    head_dim = tokens[0].shape[1] // 2
    head_count = queries[0].shape[1] // head_dim
    rows = head_count * step_count
    gain = LOG2E / head_dim**0.5
    stacked = jnp.concatenate(
        [
            query[:, h * head_dim : (h + 1) * head_dim]
            for query in queries
            for h in range(head_count)
        ],
        axis=0,
    ).astype(jnp.bfloat16)
    tokens = jnp.concatenate(tokens, axis=0).astype(jnp.bfloat16)
    score_new = contract_last(stacked, tokens[:, :head_dim])
    row_ids = lax.broadcasted_iota(jnp.int32, score_new.shape, 0)
    column_ids = lax.broadcasted_iota(jnp.int32, score_new.shape, 1)
    allowed = (row_ids // rows == column_ids // step_count) & (
        column_ids % step_count <= row_ids % step_count
    )
    score_new = jnp.where(allowed, score_new, MASKED)
    new_max = jnp.max(score_new, axis=1, keepdims=True)
    maxima, scores = [], []
    for g in range(count):
        keys = jnp.concatenate([page[:, :head_dim] for page in contexts[g]], axis=0)
        score = contract_last(stacked[g * rows : (g + 1) * rows], keys)
        position = lax.broadcasted_iota(jnp.int32, score.shape, 1)
        score = jnp.where(position < live_lengths[g], score, MASKED)
        scores.append(score)
        maxima.append(
            jnp.maximum(
                jnp.max(score, axis=1, keepdims=True), new_max[g * rows : (g + 1) * rows]
            )
        )
    exp_new = jnp.exp2((score_new - jnp.concatenate(maxima, axis=0)) * gain)
    new_total = jnp.sum(exp_new, axis=1, keepdims=True)
    results, inverses = [], []
    for g in range(count):
        exp_ctx = jnp.exp2((scores[g] - maxima[g]) * gain)
        total = jnp.sum(exp_ctx, axis=1, keepdims=True) + new_total[g * rows : (g + 1) * rows]
        inverse = 1.0 / total
        inverses.append(inverse)
        values = jnp.concatenate([page[:, head_dim:] for page in contexts[g]], axis=0)
        results.append(
            jnp.dot(
                (exp_ctx * inverse).astype(jnp.bfloat16),
                values,
                preferred_element_type=jnp.float32,
            )
        )
    weight_new = (exp_new * jnp.concatenate(inverses, axis=0)).astype(jnp.bfloat16)
    result = jnp.concatenate(results, axis=0) + jnp.dot(
        weight_new, tokens[:, head_dim:], preferred_element_type=jnp.float32
    )
    return [
        jnp.concatenate(
            [
                result[g * rows + h * step_count : g * rows + (h + 1) * step_count]
                for h in range(head_count)
            ],
            axis=1,
        )
        for g in range(count)
    ]


def contract_last(a, b):
    return lax.dot_general(a, b, (((1,), (1,)), ((), ())), preferred_element_type=jnp.float32)


def route_of(migration, own_index, peer, arriving):
    ours, theirs, slot_row = (2, 0, 3) if arriving else (0, 2, 1)
    slot = jnp.int32(0)
    for row in range(migration.shape[1]):
        match = (migration[ours, row] == own_index) & (migration[theirs, row] == peer)
        slot = jnp.where(match, migration[slot_row, row], slot)
    return slot


def arrivals_of(migration, inst_count):
    me = lax.axis_index("inst")
    incoming = migration.shape[1] // inst_count
    slots = [jnp.int32(NEVER)] * incoming
    sources = [jnp.int32(0)] * incoming
    for row in range(migration.shape[1]):
        slot = jnp.where(migration[2, row] == me, migration[3, row], NEVER)
        source = migration[0, row]
        for i in range(incoming):
            before = slot < slots[i]
            slots[i], slot = jnp.where(before, slot, slots[i]), jnp.where(before, slots[i], slot)
            sources[i], source = (
                jnp.where(before, source, sources[i]),
                jnp.where(before, sources[i], source),
            )
    return slots, sources


def slot_at(position, arrivals, slot_count):
    kept = slot_count - len(arrivals)
    if position >= kept:
        return jnp.minimum(arrivals[position - kept], slot_count - 1)
    slot = jnp.int32(position)
    for arrival in arrivals:
        slot = slot + (slot >= arrival).astype(jnp.int32)
    return slot


def peer_of(me, k, count):
    return me ^ k if count & (count - 1) == 0 else (count - me + k) % count


def pack_rows(inst_count, migration, queries, new_tokens, packs):
    me = lax.axis_index("inst")
    width = queries.shape[2]
    for k, pack in packs.items():
        slot = route_of(migration, me, peer_of(me, k, inst_count), True)
        pack[:, :width] = queries[slot]
        pack[:, width:] = new_tokens[slot]


def page_copies(pool, buffer, sems, page_table, item, slot):
    page_count = page_table.shape[0]
    for j in range(page_count):
        pltpu.make_async_copy(
            pool.at[page_table[j, slot]], buffer.at[item, j], sems.at[item]
        ).start()


def wait_copies(pool, buffer, sems, item):
    pltpu.make_async_copy(
        pool.at[pl.ds(0, buffer.shape[1])], buffer.at[item], sems.at[item]
    ).wait()


def away_slot(migration, inst_count, k):
    me = lax.axis_index("inst")
    return route_of(migration, me, peer_of(me, k, inst_count), False)


def away_kernel(
    inst_count, rounds, lengths, page_table, migration, pool, second, weight, *refs
):
    count = len(rounds)
    received, answers = refs[:count], refs[count : 2 * count]
    keep, send, buffer, sems = refs[2 * count :]
    page_count, slot_count = page_table.shape
    step_count, width = answers[0].shape
    first = lax.axis_index("inst") * slot_count
    slots = [away_slot(migration, inst_count, k) for k in rounds]
    for i, slot in enumerate(slots):
        page_copies(pool, buffer, sems, page_table, i, slot)
    project_far(second, weight, keep, send)
    for i in range(count):
        wait_copies(pool, buffer, sems, i)
    result = attend_group(
        [ref[:, :width].astype(jnp.float32) for ref in received],
        [ref[:, width:].astype(jnp.float32) for ref in received],
        [[buffer.at[i, j] for j in range(page_count)] for i in range(count)],
        [lengths[first + slot] * pool.shape[1] for slot in slots],
        step_count,
    )
    for answer, rows in zip(answers, result):
        answer[...] = rows.astype(answer.dtype)


def project(rows, weight, first, columns, target, row_offset=0, offset=0):
    tile = min(512, columns)
    rows = rows[...]
    for j in range(0, columns, tile):
        start = pl.multiple_of(first + j, tile)
        target[row_offset : row_offset + rows.shape[0], offset + j : offset + j + tile] = jnp.dot(
            rows, weight[:, pl.ds(start, tile)], preferred_element_type=jnp.float32
        ).astype(target.dtype)


def project_far(attended, weight, keep, send, stacked=False):
    core = lax.rem(lax.axis_index("tp"), 2)
    chip = lax.axis_index("tp") // 2
    chips = lax.axis_size("tp") // 2
    columns = weight.shape[1] // (2 * chips)
    for target, side in ((send, 1 - core), (keep, core)):
        for d in range(1, chips):
            first = (2 * lax.rem(chip + d, chips) + side) * columns
            row, column = ((d - 1) * attended.shape[0], 0) if stacked else (0, (d - 1) * columns)
            project(attended, weight, first, columns, target, row, column)


def attend_slots(slots, lengths, queries, new_tokens, pages_of, page_len, wait=lambda i: None):
    first = lax.axis_index("inst") * queries.shape[0]
    rows = []
    for base in range(0, len(slots), GROUP):
        items = range(base, min(base + GROUP, len(slots)))
        for i in items:
            wait(i)
        rows += attend_group(
            [queries[slots[i]].astype(jnp.float32) for i in items],
            [new_tokens[slots[i]].astype(jnp.float32) for i in items],
            [pages_of(i) for i in items],
            [lengths[first + slots[i]] * page_len for i in items],
            queries.shape[1],
        )
    return rows


def store_rows(rows, target, at=0):
    step_count = rows[0].shape[0]
    for pair in range(0, len(rows), 2):
        start = at + pair * step_count
        target[start : start + 2 * step_count, :] = jnp.concatenate(
            rows[pair : pair + 2], axis=0
        ).astype(jnp.bfloat16)


def first_kernel(
    inst_count, rounds, migration, lengths, page_table, queries_in, new_in, pool,
    attended, queries, new_tokens, *refs,
):
    packs = dict(zip(rounds, refs))
    buffer, small_sems, page_sems = refs[len(rounds) :]
    slot_count, step_count, _ = queries.shape
    small = [
        pltpu.make_async_copy(queries_in, queries, small_sems.at[0]),
        pltpu.make_async_copy(new_in, new_tokens, small_sems.at[1]),
    ]
    for copy in small:
        copy.start()
    arrivals, _ = arrivals_of(migration, inst_count)
    slots = [
        slot_at(position, arrivals, slot_count)
        for position in range(attended.shape[0] // step_count)
    ]
    for i, slot in enumerate(slots):
        page_copies(pool, buffer, page_sems, page_table, i, slot)
    for copy in small:
        copy.wait()
    pack_rows(inst_count, migration, queries, new_tokens, packs)
    rows = attend_slots(
        slots, lengths, queries, new_tokens,
        lambda i: [buffer.at[i, j] for j in range(buffer.shape[1])],
        buffer.shape[2],
        lambda i: wait_copies(pool, buffer, page_sems, i),
    )
    store_rows(rows, attended)


def far_kernel(attended, weight, keep, send):
    project_far(attended, weight, keep, send)


def second_kernel(
    inst_count, first, migration, lengths, page_table, queries, new_tokens, pool, after,
    attended, extra,
):
    slot_count, step_count, _ = queries.shape
    count = attended.shape[0] // step_count
    arrivals, _ = arrivals_of(migration, inst_count)
    slots = [
        slot_at(first + i, arrivals, slot_count) for i in range(count + extra.shape[0])
    ]
    rows = attend_slots(
        slots, lengths, queries, new_tokens,
        lambda i: [pool.at[page_table[j, slots[i]]] for j in range(page_table.shape[0])],
        pool.shape[1],
    )
    store_rows(rows[:count], attended)
    for i, row in enumerate(rows[count:]):
        extra[i] = row.astype(extra.dtype)


def last_rows_kernel(inst_count, rounds, migration, weight, extra, *refs):
    answers, (rows, keep, send) = refs[:-3], refs[-3:]
    me = lax.axis_index("inst")
    _, sources = arrivals_of(migration, inst_count)
    last = [extra[i].astype(jnp.float32) for i in range(extra.shape[0])]
    given = [answer[...].astype(jnp.float32) for answer in answers]
    for source in sources:
        row = given[0]
        for k, answer in zip(rounds[1:], given[1:]):
            row = jnp.where(source == peer_of(me, k, inst_count), answer, row)
        last.append(row)
    store_rows(last, rows)
    project_far(rows, weight, keep, send, stacked=True)


def own_kernel(weight, first, second, last, after, keep, *refs):
    sends, rows = refs[:-1], refs[-1]
    core = lax.rem(lax.axis_index("tp"), 2)
    pair = lax.axis_index("tp") // 2 * 2
    columns = keep.shape[1]
    at = 0
    for part in (first, second, last):
        rows[at : at + part.shape[0], :] = part[...]
        at += part.shape[0]
    at = 0
    for send in sends:
        project(rows, weight, (pair + 1 - core) * columns + at, send.shape[1], send)
        at += send.shape[1]
    project(rows, weight, (pair + core) * columns, columns, keep)


def sum_kernel(inst_count, chunks, piece_count, migration, keep, *refs):
    mates, parts, (out, staged, sem) = refs[:piece_count], refs[piece_count:-3], refs[-3:]
    slot_count, step_count, _ = out.shape
    pair = 2 * step_count
    width = mates[0].shape[1]
    arrivals, _ = arrivals_of(migration, inst_count)
    share = len(parts) // len(chunks)
    at = 0
    for n, chunk in enumerate(chunks):
        for base in range(0, chunk, pair):
            for m, mate in enumerate(mates):
                columns = slice(m * width, (m + 1) * width)
                total = keep[at : at + pair, columns] + mate[at : at + pair, :].astype(jnp.float32)
                for part in parts[n * share : (n + 1) * share]:
                    total = total + part[base : base + pair, columns].astype(jnp.float32)
                total = total.astype(jnp.bfloat16)
                for half in range(2):
                    staged[at // step_count + half, :, columns] = total[
                        half * step_count : (half + 1) * step_count
                    ]
            at += pair
    scatter_rows(staged, out, arrivals, 0, sem)


def scatter_rows(staged, out, arrivals, first, sem):
    slot_count = out.shape[0]
    for i in range(staged.shape[0]):
        slot = slot_at(first + i, arrivals, slot_count)
        pltpu.make_async_copy(staged.at[i], out.at[slot], sem.at[0]).start()
    pltpu.make_async_copy(staged, out.at[pl.ds(0, staged.shape[0])], sem.at[0]).wait()


def last_kernel(inst_count, first, piece_count, migration, keep, *refs):
    mates, parts, (out, staged, sem) = refs[:piece_count], refs[piece_count:-4], refs[-3:]
    step_count = out.shape[1]
    pair = 2 * step_count
    width = mates[0].shape[1]
    size = parts[0].shape[0]
    arrivals, _ = arrivals_of(migration, inst_count)
    for at in range(0, size, pair):
        own = keep.shape[0] - size + at
        for m, mate in enumerate(mates):
            columns = slice(m * width, (m + 1) * width)
            total = keep[own : own + pair, columns] + mate[own : own + pair, :].astype(jnp.float32)
            for part in parts:
                total = total + part[at : at + pair, columns].astype(jnp.float32)
            total = total.astype(jnp.bfloat16)
            for half in range(2):
                staged[at // step_count + half, :, columns] = total[
                    half * step_count : (half + 1) * step_count
                ]
    scatter_rows(staged, out, arrivals, first, sem)


def in_hbm(value):
    return pltpu.with_memory_space_constraint(value, pltpu.HBM)


def in_vmem(value):
    return pltpu.with_memory_space_constraint(value, pltpu.VMEM)


def on_device(queries, new_kv, kv_pool, out_weight, lengths, page_table, migration):
    inst_count = lax.axis_size("inst")
    tp_count = lax.axis_size("tp")
    chips = tp_count // 2
    slot_count, page_count = page_table.shape
    row_count, width = queries.shape
    step_count = row_count // slot_count
    queries = in_hbm(queries.reshape(slot_count, step_count, width))
    new_tokens = in_hbm(new_kv[0].reshape(slot_count, step_count, new_kv.shape[2]))
    pool = kv_pool[0]
    columns = out_weight.shape[1] // tp_count
    incoming = migration.shape[0] // inst_count
    weight = in_vmem(out_weight)
    lengths = in_hbm(lengths)
    page_table = in_hbm(page_table.T)
    migration = in_hbm(migration.T)
    limit = pltpu.CompilerParams(vmem_limit_bytes=32 * 2**20)
    light = pl.CostEstimate(flops=1, bytes_accessed=1, transcendentals=0)
    bf16, f32 = jnp.bfloat16, jnp.float32
    shape = jax.ShapeDtypeStruct
    swap = [(t, t ^ 1) for t in range(tp_count)]
    far = (chips - 1) * columns

    def hold(values, until):
        return pl.pallas_call(
            lambda *refs: None,
            out_shape=[pltpu.VMEM(value.shape, value.dtype) for value in values],
            in_specs=[ANY] * (len(values) + len(until)),
            out_specs=[ANY] * len(values),
            input_output_aliases={i: i for i in range(len(values))},
            compiler_params=pltpu.CompilerParams(vmem_limit_bytes=2**20),
            cost_estimate=light,
            name="hold",
        )(*[in_vmem(value) for value in values], *until)

    def send_far(summed):
        return [
            lax.ppermute(
                part, "tp", [(t, (t + 2 * d) % tp_count) for t in range(tp_count)]
            )
            for d, part in enumerate(summed, 1)
        ]

    def split_far(summed):
        return [summed[:, d * columns : (d + 1) * columns] for d in range(chips - 1)]

    def chunk_shapes(count):
        rows = count * step_count
        return [pltpu.VMEM((rows, far), f32), pltpu.VMEM((rows, far), bf16)]

    def rows_shape(count):
        return pltpu.VMEM((count * step_count, width), bf16)

    last_count = incoming + incoming % 2
    extra_count = last_count - incoming
    first_count = slot_count // 4 * 2
    second_count = slot_count - first_count - last_count
    last_rows = last_count * step_count

    def page_shape(count):
        return pltpu.VMEM((count, page_count, *pool.shape[1:]), bf16)

    dma = pltpu.SemaphoreType.DMA
    rounds = [
        k
        for k in range(inst_count)
        if any(peer_of(i, k, inst_count) != i for i in range(inst_count))
    ]
    pairs = {k: [(i, peer_of(i, k, inst_count)) for i in range(inst_count)] for k in rounds}
    first, queries, new_tokens, *packs = pl.pallas_call(
        functools.partial(first_kernel, inst_count, rounds),
        out_shape=[
            rows_shape(first_count),
            pltpu.VMEM(queries.shape, bf16),
            pltpu.VMEM(new_tokens.shape, bf16),
        ]
        + [shape((step_count, width + new_tokens.shape[2]), bf16)] * len(rounds),
        in_specs=[SMEM, SMEM, SMEM, ANY, ANY, ANY],
        out_specs=[VMEM] * (3 + len(rounds)),
        scratch_shapes=[page_shape(first_count), dma((2,)), dma((first_count,))],
        compiler_params=limit,
        cost_estimate=light,
        name="attend_first",
    )(migration, lengths, page_table, queries, new_tokens, in_hbm(pool))
    first, queries, new_tokens = in_vmem(first), in_vmem(queries), in_vmem(new_tokens)
    keep, send = pl.pallas_call(
        far_kernel,
        out_shape=chunk_shapes(first_count),
        in_specs=[VMEM] * 2,
        out_specs=[VMEM] * 2,
        compiler_params=limit,
        cost_estimate=light,
        name="far_first",
    )(first, weight)
    mate = lax.ppermute(send, "tp", swap)
    summed = (keep + mate.astype(f32)).astype(bf16)
    arrived_first = send_far(split_far(summed))
    packs = hold(packs, [summed])
    received = [lax.ppermute(pack, "inst", pairs[k]) for k, pack in zip(rounds, packs)]

    second, extra = pl.pallas_call(
        functools.partial(second_kernel, inst_count, first_count),
        out_shape=[
            rows_shape(second_count),
            pltpu.VMEM((extra_count, step_count, width), bf16),
        ],
        in_specs=[SMEM, SMEM, SMEM, VMEM, VMEM, VMEM, ANY],
        out_specs=[VMEM] * 2,
        compiler_params=limit,
        cost_estimate=light,
        name="attend_second",
    )(migration, lengths, page_table, queries, new_tokens, in_vmem(pool), summed)
    second = in_vmem(second)
    *answers, keep, send = pl.pallas_call(
        functools.partial(away_kernel, inst_count, rounds),
        out_shape=[shape((step_count, width), bf16)] * len(rounds) + chunk_shapes(second_count),
        in_specs=[SMEM, SMEM, SMEM, ANY] + [VMEM] * (2 + len(rounds)),
        out_specs=[VMEM] * (2 + len(rounds)),
        scratch_shapes=[page_shape(len(rounds)), dma((len(rounds),))],
        compiler_params=limit,
        cost_estimate=light,
        name="attend_away",
    )(lengths, page_table, migration, in_hbm(pool), second, weight, *received)
    mate = lax.ppermute(send, "tp", swap)
    answers = [lax.ppermute(answer, "inst", pairs[k]) for k, answer in zip(rounds, answers)]
    (keep,) = hold([keep], arrived_first)
    summed = (keep + mate.astype(f32)).astype(bf16)
    arrived_second = send_far(split_far(summed))

    last, keep, send = pl.pallas_call(
        functools.partial(last_rows_kernel, inst_count, rounds),
        out_shape=[
            rows_shape(last_count),
            pltpu.VMEM((last_rows * (chips - 1), columns), f32),
            pltpu.VMEM((last_rows * (chips - 1), columns), bf16),
        ],
        in_specs=[SMEM] + [VMEM] * (2 + len(rounds)),
        out_specs=[VMEM] * 3,
        compiler_params=limit,
        cost_estimate=light,
        name="last_rows",
    )(migration, weight, in_vmem(extra), *answers)
    mate = lax.ppermute(send, "tp", swap)
    own_keep, *own_sends = pl.pallas_call(
        own_kernel,
        out_shape=[
            pltpu.VMEM((row_count, columns), f32),
            *[pltpu.VMEM((row_count, columns // PIECES), bf16)] * PIECES,
        ],
        in_specs=[VMEM] * 4 + [ANY],
        out_specs=[VMEM] * (1 + PIECES),
        scratch_shapes=[pltpu.VMEM((row_count, width), bf16)],
        compiler_params=limit,
        cost_estimate=light,
        name="own_columns",
    )(weight, first, second, in_vmem(last), summed)
    own_keep = in_vmem(own_keep)
    own_mates = [lax.ppermute(own_send, "tp", swap) for own_send in own_sends]
    (keep,) = hold([keep], [*arrived_second, own_keep])
    summed = (keep + mate.astype(f32)).astype(bf16)
    arrived_last = send_far([summed[d * last_rows : (d + 1) * last_rows] for d in range(chips - 1)])

    early = slot_count - last_count
    out_shape = (slot_count, step_count, columns)
    out = pl.pallas_call(
        functools.partial(
            sum_kernel, inst_count, [first_count * step_count, second_count * step_count], PIECES
        ),
        out_shape=pltpu.HBM(out_shape, bf16),
        in_specs=[SMEM] + [VMEM] * (1 + PIECES + 2 * (chips - 1)),
        out_specs=ANY,
        scratch_shapes=[pltpu.VMEM((early, step_count, columns), bf16), dma((1,))],
        compiler_params=limit,
        cost_estimate=light,
        name="sum_early",
    )(migration, own_keep, *own_mates, *arrived_first, *arrived_second)
    out = pl.pallas_call(
        functools.partial(last_kernel, inst_count, early, PIECES),
        out_shape=pltpu.HBM(out_shape, bf16),
        in_specs=[SMEM] + [VMEM] * (PIECES + chips) + [ANY],
        out_specs=ANY,
        scratch_shapes=[pltpu.VMEM((last_count, step_count, columns), bf16), dma((1,))],
        input_output_aliases={PIECES + chips + 1: 0},
        compiler_params=limit,
        cost_estimate=light,
        name="sum_last",
    )(migration, own_keep, *own_mates, *arrived_last, out)
    return out.reshape(row_count, columns)


def solution(mesh):
    placed = (
        P(("group", "inst"), "tp"),
        P("tp", ("group", "inst"), None),
        P("tp", ("group", "inst"), None, None),
        P("tp", None),
        P("group"),
        P(("group", "inst"), None),
        P("group", None),
    )
    return jax.shard_map(
        on_device, mesh=mesh, in_specs=placed, out_specs=P(("group", "inst"), "tp"), check_vma=False
    )
```

```python
import functools

import jax
import jax.numpy as jnp
from jax import lax
from jax.experimental import pallas as pl
from jax.experimental.pallas import tpu as pltpu
from jax.sharding import PartitionSpec as P

LOG2E = 1.4426950408889634
MASKED = -1e30
GROUP = 8
NEVER = 2**30
PIECES = 4

VMEM = pl.BlockSpec(memory_space=pltpu.VMEM)
SMEM = pl.BlockSpec(memory_space=pltpu.SMEM)
ANY = pl.BlockSpec(memory_space=pl.ANY)


def attend_group(queries, tokens, contexts, live_lengths, step_count):
    count = len(queries)
    head_dim = tokens[0].shape[1] // 2
    head_count = queries[0].shape[1] // head_dim
    rows = head_count * step_count
    gain = LOG2E / head_dim**0.5
    stacked = jnp.concatenate(
        [
            query[:, h * head_dim : (h + 1) * head_dim]
            for query in queries
            for h in range(head_count)
        ],
        axis=0,
    ).astype(jnp.bfloat16)
    tokens = jnp.concatenate(tokens, axis=0).astype(jnp.bfloat16)
    score_new = contract_last(stacked, tokens[:, :head_dim])
    row_ids = lax.broadcasted_iota(jnp.int32, score_new.shape, 0)
    column_ids = lax.broadcasted_iota(jnp.int32, score_new.shape, 1)
    allowed = (row_ids // rows == column_ids // step_count) & (
        column_ids % step_count <= row_ids % step_count
    )
    score_new = jnp.where(allowed, score_new, MASKED)
    new_max = jnp.max(score_new, axis=1, keepdims=True)
    maxima, scores = [], []
    for g in range(count):
        keys = jnp.concatenate([page[:, :head_dim] for page in contexts[g]], axis=0)
        score = contract_last(stacked[g * rows : (g + 1) * rows], keys)
        position = lax.broadcasted_iota(jnp.int32, score.shape, 1)
        score = jnp.where(position < live_lengths[g], score, MASKED)
        scores.append(score)
        maxima.append(
            jnp.maximum(
                jnp.max(score, axis=1, keepdims=True), new_max[g * rows : (g + 1) * rows]
            )
        )
    exp_new = jnp.exp2((score_new - jnp.concatenate(maxima, axis=0)) * gain)
    new_total = jnp.sum(exp_new, axis=1, keepdims=True)
    results, inverses = [], []
    for g in range(count):
        exp_ctx = jnp.exp2((scores[g] - maxima[g]) * gain)
        total = jnp.sum(exp_ctx, axis=1, keepdims=True) + new_total[g * rows : (g + 1) * rows]
        inverse = 1.0 / total
        inverses.append(inverse)
        values = jnp.concatenate([page[:, head_dim:] for page in contexts[g]], axis=0)
        results.append(
            jnp.dot(
                (exp_ctx * inverse).astype(jnp.bfloat16),
                values,
                preferred_element_type=jnp.float32,
            )
        )
    weight_new = (exp_new * jnp.concatenate(inverses, axis=0)).astype(jnp.bfloat16)
    result = jnp.concatenate(results, axis=0) + jnp.dot(
        weight_new, tokens[:, head_dim:], preferred_element_type=jnp.float32
    )
    return [
        jnp.concatenate(
            [
                result[g * rows + h * step_count : g * rows + (h + 1) * step_count]
                for h in range(head_count)
            ],
            axis=1,
        )
        for g in range(count)
    ]


def contract_last(a, b):
    return lax.dot_general(a, b, (((1,), (1,)), ((), ())), preferred_element_type=jnp.float32)


def route_of(migration, own_index, peer, arriving):
    ours, theirs, slot_row = (2, 0, 3) if arriving else (0, 2, 1)
    slot = jnp.int32(0)
    for row in range(migration.shape[1]):
        match = (migration[ours, row] == own_index) & (migration[theirs, row] == peer)
        slot = jnp.where(match, migration[slot_row, row], slot)
    return slot


def arrivals_of(migration, inst_count):
    me = lax.axis_index("inst")
    incoming = migration.shape[1] // inst_count
    slots = [jnp.int32(NEVER)] * incoming
    sources = [jnp.int32(0)] * incoming
    for row in range(migration.shape[1]):
        slot = jnp.where(migration[2, row] == me, migration[3, row], NEVER)
        source = migration[0, row]
        for i in range(incoming):
            before = slot < slots[i]
            slots[i], slot = jnp.where(before, slot, slots[i]), jnp.where(before, slots[i], slot)
            sources[i], source = (
                jnp.where(before, source, sources[i]),
                jnp.where(before, sources[i], source),
            )
    return slots, sources


def slot_at(position, arrivals, slot_count):
    kept = slot_count - len(arrivals)
    if position >= kept:
        return jnp.minimum(arrivals[position - kept], slot_count - 1)
    slot = jnp.int32(position)
    for arrival in arrivals:
        slot = slot + (slot >= arrival).astype(jnp.int32)
    return slot


def peer_of(me, k, count):
    return me ^ k if count & (count - 1) == 0 else (count - me + k) % count


def pack_rows(inst_count, migration, queries, new_tokens, packs):
    me = lax.axis_index("inst")
    width = queries.shape[2]
    for k, pack in packs.items():
        slot = route_of(migration, me, peer_of(me, k, inst_count), True)
        pack[:, :width] = queries[slot]
        pack[:, width:] = new_tokens[slot]


def page_copies(pool, buffer, sems, page_table, item, slot):
    page_count = page_table.shape[0]
    for j in range(page_count):
        pltpu.make_async_copy(
            pool.at[page_table[j, slot]], buffer.at[item, j], sems.at[item]
        ).start()


def wait_copies(pool, buffer, sems, item):
    pltpu.make_async_copy(
        pool.at[pl.ds(0, buffer.shape[1])], buffer.at[item], sems.at[item]
    ).wait()


def away_slot(migration, inst_count, k):
    me = lax.axis_index("inst")
    return route_of(migration, me, peer_of(me, k, inst_count), False)


def away_kernel(inst_count, rounds, lengths, migration, pages, *refs):
    received, answers = refs[: len(rounds)], refs[len(rounds) :]
    _, page_count, page_len, _ = pages.shape
    step_count, width = answers[0].shape
    first = lax.axis_index("inst") * (lengths.shape[0] // inst_count)
    result = attend_group(
        [ref[:, :width].astype(jnp.float32) for ref in received],
        [ref[:, width:].astype(jnp.float32) for ref in received],
        [[pages.at[i, j] for j in range(page_count)] for i in range(len(rounds))],
        [lengths[first + away_slot(migration, inst_count, k)] * page_len for k in rounds],
        step_count,
    )
    for answer, rows in zip(answers, result):
        answer[...] = rows.astype(answer.dtype)


def project(rows, weight, first, columns, target, offset=0):
    tile = min(512, columns)
    rows = rows[...]
    for j in range(0, columns, tile):
        start = pl.multiple_of(first + j, tile)
        target[:, offset + j : offset + j + tile] = jnp.dot(
            rows, weight[:, pl.ds(start, tile)], preferred_element_type=jnp.float32
        ).astype(target.dtype)


def project_far(attended, weight, keep, send):
    core = lax.rem(lax.axis_index("tp"), 2)
    chip = lax.axis_index("tp") // 2
    chips = lax.axis_size("tp") // 2
    columns = weight.shape[1] // (2 * chips)
    for target, side in ((send, 1 - core), (keep, core)):
        for d in range(1, chips):
            first = (2 * lax.rem(chip + d, chips) + side) * columns
            project(attended, weight, first, columns, target, (d - 1) * columns)


def attend_slots(slots, lengths, queries, new_tokens, pages_of, page_len, wait=lambda i: None):
    first = lax.axis_index("inst") * queries.shape[0]
    rows = []
    for base in range(0, len(slots), GROUP):
        items = range(base, min(base + GROUP, len(slots)))
        for i in items:
            wait(i)
        rows += attend_group(
            [queries[slots[i]].astype(jnp.float32) for i in items],
            [new_tokens[slots[i]].astype(jnp.float32) for i in items],
            [pages_of(i) for i in items],
            [lengths[first + slots[i]] * page_len for i in items],
            queries.shape[1],
        )
    return rows


def store_rows(rows, target, at=0):
    step_count = rows[0].shape[0]
    for pair in range(0, len(rows), 2):
        start = at + pair * step_count
        target[start : start + 2 * step_count, :] = jnp.concatenate(
            rows[pair : pair + 2], axis=0
        ).astype(jnp.bfloat16)


def first_kernel(
    inst_count, rounds, migration, lengths, page_table, queries_in, new_in, pool,
    attended, queries, new_tokens, *refs,
):
    packs = dict(zip(rounds, refs))
    buffer, small_sems, page_sems = refs[len(rounds) :]
    slot_count, step_count, _ = queries.shape
    small = [
        pltpu.make_async_copy(queries_in, queries, small_sems.at[0]),
        pltpu.make_async_copy(new_in, new_tokens, small_sems.at[1]),
    ]
    for copy in small:
        copy.start()
    arrivals, _ = arrivals_of(migration, inst_count)
    slots = [
        slot_at(position, arrivals, slot_count)
        for position in range(attended.shape[0] // step_count)
    ]
    for i, slot in enumerate(slots):
        page_copies(pool, buffer, page_sems, page_table, i, slot)
    for copy in small:
        copy.wait()
    pack_rows(inst_count, migration, queries, new_tokens, packs)
    rows = attend_slots(
        slots, lengths, queries, new_tokens,
        lambda i: [buffer.at[i, j] for j in range(buffer.shape[1])],
        buffer.shape[2],
        lambda i: wait_copies(pool, buffer, page_sems, i),
    )
    store_rows(rows, attended)


def far_kernel(attended, weight, keep, send):
    project_far(attended, weight, keep, send)


def second_kernel(
    inst_count, rounds, first, migration, lengths, page_table, queries, new_tokens, pool, after,
    attended, away_pages, sems,
):
    slot_count, step_count, _ = queries.shape
    for i, k in enumerate(rounds):
        slot = away_slot(migration, inst_count, k)
        page_copies(pool, away_pages, sems, page_table, i, slot)
    arrivals, _ = arrivals_of(migration, inst_count)
    slots = [slot_at(first + i, arrivals, slot_count) for i in range(attended.shape[0])]
    rows = attend_slots(
        slots, lengths, queries, new_tokens,
        lambda i: [pool.at[page_table[j, slots[i]]] for j in range(page_table.shape[0])],
        pool.shape[1],
    )
    for i, row in enumerate(rows):
        attended[i] = row.astype(attended.dtype)
    for i in range(len(rounds)):
        wait_copies(pool, away_pages, sems, i)


def far_second_kernel(inst_count, rounds, migration, weight, attended, *refs):
    answers, (rows, keep, send) = refs[:-3], refs[-3:]
    me = lax.axis_index("inst")
    _, sources = arrivals_of(migration, inst_count)
    parts = [attended[i].astype(jnp.float32) for i in range(attended.shape[0])]
    given = [answer[...].astype(jnp.float32) for answer in answers]
    for source in sources:
        part = given[0]
        for k, answer in zip(rounds[1:], given[1:]):
            part = jnp.where(source == peer_of(me, k, inst_count), answer, part)
        parts.append(part)
    store_rows(parts, rows)
    project_far(rows, weight, keep, send)


def own_kernel(weight, first, second, after, keep, *refs):
    sends, rows = refs[:-1], refs[-1]
    core = lax.rem(lax.axis_index("tp"), 2)
    pair = lax.axis_index("tp") // 2 * 2
    columns = keep.shape[1]
    rows[: first.shape[0], :] = first[...]
    rows[first.shape[0] :, :] = second[...]
    at = 0
    for send in sends:
        project(rows, weight, (pair + 1 - core) * columns + at, send.shape[1], send)
        at += send.shape[1]
    project(rows, weight, (pair + core) * columns, columns, keep)


def sum_kernel(inst_count, first, piece_count, migration, keep, *refs):
    mates, parts = refs[:piece_count], refs[piece_count:-3]
    out, staged, sem = refs[-3:]
    parts = parts[: lax.axis_size("tp") // 2 - 1]
    slot_count, step_count, _ = out.shape
    pair = 2 * step_count
    width = mates[0].shape[1]
    arrivals, _ = arrivals_of(migration, inst_count)
    for at in range(0, staged.shape[0] * step_count, pair):
        own = first * step_count + at
        for m, mate in enumerate(mates):
            columns = slice(m * width, (m + 1) * width)
            total = keep[own : own + pair, columns] + mate[own : own + pair, :].astype(jnp.float32)
            for part in parts:
                total = total + part[at : at + pair, columns].astype(jnp.float32)
            total = total.astype(jnp.bfloat16)
            for half in range(2):
                staged[at // step_count + half, :, columns] = total[
                    half * step_count : (half + 1) * step_count
                ]
    for i in range(staged.shape[0]):
        slot = slot_at(first + i, arrivals, slot_count)
        pltpu.make_async_copy(staged.at[i], out.at[slot], sem.at[0]).start()
    pltpu.make_async_copy(staged, out.at[pl.ds(0, staged.shape[0])], sem.at[0]).wait()


def in_hbm(value):
    return pltpu.with_memory_space_constraint(value, pltpu.HBM)


def in_vmem(value):
    return pltpu.with_memory_space_constraint(value, pltpu.VMEM)


def on_device(queries, new_kv, kv_pool, out_weight, lengths, page_table, migration):
    inst_count = lax.axis_size("inst")
    tp_count = lax.axis_size("tp")
    chips = tp_count // 2
    slot_count, page_count = page_table.shape
    row_count, width = queries.shape
    step_count = row_count // slot_count
    queries = in_hbm(queries.reshape(slot_count, step_count, width))
    new_tokens = in_hbm(new_kv[0].reshape(slot_count, step_count, new_kv.shape[2]))
    pool = kv_pool[0]
    columns = out_weight.shape[1] // tp_count
    incoming = migration.shape[0] // inst_count
    weight = in_vmem(out_weight)
    lengths = in_hbm(lengths)
    page_table = in_hbm(page_table.T)
    migration = in_hbm(migration.T)
    limit = pltpu.CompilerParams(vmem_limit_bytes=32 * 2**20)
    light = pl.CostEstimate(flops=1, bytes_accessed=1, transcendentals=0)
    bf16, f32 = jnp.bfloat16, jnp.float32
    shape = jax.ShapeDtypeStruct
    swap = [(t, t ^ 1) for t in range(tp_count)]
    far = (chips - 1) * columns

    def hold(values, until):
        return pl.pallas_call(
            lambda *refs: None,
            out_shape=[pltpu.VMEM(value.shape, value.dtype) for value in values],
            in_specs=[ANY] * (len(values) + len(until)),
            out_specs=[ANY] * len(values),
            input_output_aliases={i: i for i in range(len(values))},
            compiler_params=pltpu.CompilerParams(vmem_limit_bytes=2**20),
            cost_estimate=light,
            name="hold",
        )(*[in_vmem(value) for value in values], *until)

    def send_far(summed):
        return [
            lax.ppermute(
                part, "tp", [(t, (t + 2 * d) % tp_count) for t in range(tp_count)]
            )
            for d, part in enumerate(summed, 1)
        ]

    def split_far(summed):
        return [summed[:, d * columns : (d + 1) * columns] for d in range(chips - 1)]

    def chunk_shapes(count):
        rows = count * step_count
        return [pltpu.VMEM((rows, far), f32), pltpu.VMEM((rows, far), bf16)]

    def rows_shape(count):
        return pltpu.VMEM((count * step_count, width), bf16)

    first_count = slot_count // 16 * 10
    second_count = slot_count - first_count

    def page_shape(count):
        return pltpu.VMEM((count, page_count, *pool.shape[1:]), bf16)

    dma = pltpu.SemaphoreType.DMA
    rounds = [
        k
        for k in range(inst_count)
        if any(peer_of(i, k, inst_count) != i for i in range(inst_count))
    ]
    pairs = {k: [(i, peer_of(i, k, inst_count)) for i in range(inst_count)] for k in rounds}
    first, queries, new_tokens, *packs = pl.pallas_call(
        functools.partial(first_kernel, inst_count, rounds),
        out_shape=[
            rows_shape(first_count),
            pltpu.VMEM(queries.shape, bf16),
            pltpu.VMEM(new_tokens.shape, bf16),
        ]
        + [shape((step_count, width + new_tokens.shape[2]), bf16)] * len(rounds),
        in_specs=[SMEM, SMEM, SMEM, ANY, ANY, ANY],
        out_specs=[VMEM] * (3 + len(rounds)),
        scratch_shapes=[page_shape(first_count), dma((2,)), dma((first_count,))],
        compiler_params=limit,
        cost_estimate=light,
        name="attend_first",
    )(migration, lengths, page_table, queries, new_tokens, in_hbm(pool))
    first, queries, new_tokens = in_vmem(first), in_vmem(queries), in_vmem(new_tokens)
    keep, send = pl.pallas_call(
        far_kernel,
        out_shape=chunk_shapes(first_count),
        in_specs=[VMEM] * 2,
        out_specs=[VMEM] * 2,
        compiler_params=limit,
        cost_estimate=light,
        name="far_first",
    )(first, weight)
    mate = lax.ppermute(send, "tp", swap)
    summed = (keep + mate.astype(f32)).astype(bf16)
    arrived_first = send_far(split_far(summed))
    packs = hold(packs, [summed])
    received = [lax.ppermute(pack, "inst", pairs[k]) for k, pack in zip(rounds, packs)]

    attended, away_pages = pl.pallas_call(
        functools.partial(second_kernel, inst_count, rounds, first_count),
        out_shape=[
            pltpu.VMEM((second_count - incoming, step_count, width), bf16),
            page_shape(len(rounds)),
        ],
        in_specs=[SMEM, SMEM, SMEM, VMEM, VMEM, VMEM, ANY],
        out_specs=[VMEM] * 2,
        scratch_shapes=[dma((len(rounds),))],
        compiler_params=limit,
        cost_estimate=light,
        name="attend_second",
    )(
        migration, lengths, page_table, queries, new_tokens, in_vmem(pool), summed,
    )
    attended = in_vmem(attended)
    answers = pl.pallas_call(
        functools.partial(away_kernel, inst_count, rounds),
        out_shape=[shape((step_count, width), bf16)] * len(rounds),
        in_specs=[SMEM, SMEM] + [VMEM] * (1 + len(rounds)),
        out_specs=[VMEM] * len(rounds),
        compiler_params=limit,
        cost_estimate=light,
        name="attend_away",
    )(lengths, migration, in_vmem(away_pages), *received)
    answers = [lax.ppermute(answer, "inst", pairs[k]) for k, answer in zip(rounds, answers)]
    second, keep, send = pl.pallas_call(
        functools.partial(far_second_kernel, inst_count, rounds),
        out_shape=[rows_shape(second_count), *chunk_shapes(second_count)],
        in_specs=[SMEM] + [VMEM] * (2 + len(rounds)),
        out_specs=[VMEM] * 3,
        compiler_params=limit,
        cost_estimate=light,
        name="far_second",
    )(migration, weight, attended, *answers)
    mate = lax.ppermute(send, "tp", swap)
    (keep,) = hold([keep], arrived_first)
    summed = (keep + mate.astype(f32)).astype(bf16)
    arrived_second = send_far(split_far(summed))
    own_keep, *own_sends = pl.pallas_call(
        own_kernel,
        out_shape=[
            pltpu.VMEM((row_count, columns), f32),
            *[pltpu.VMEM((row_count, columns // PIECES), bf16)] * PIECES,
        ],
        in_specs=[VMEM] * 3 + [ANY],
        out_specs=[VMEM] * (1 + PIECES),
        scratch_shapes=[pltpu.VMEM((row_count, width), bf16)],
        compiler_params=limit,
        cost_estimate=light,
        name="own_columns",
    )(weight, first, in_vmem(second), summed)
    own_keep = in_vmem(own_keep)
    own_mates = [lax.ppermute(own_send, "tp", swap) for own_send in own_sends]

    out = []
    for start, count, arrived in (
        (0, first_count, arrived_first),
        (first_count, second_count, arrived_second),
    ):
        operands = [migration, own_keep, *own_mates, *arrived]
        out = [
            pl.pallas_call(
                functools.partial(sum_kernel, inst_count, start, PIECES),
                out_shape=pltpu.HBM((slot_count, step_count, columns), bf16),
                in_specs=[SMEM] + [VMEM] * (len(operands) - 1) + [ANY] * len(out),
                out_specs=ANY,
                scratch_shapes=[pltpu.VMEM((count, step_count, columns), bf16), dma((1,))],
                input_output_aliases={len(operands): 0} if out else {},
                compiler_params=limit,
                cost_estimate=light,
                name="sum_chunk",
            )(*operands, *out)
        ]
    (out,) = out
    return out.reshape(row_count, columns)


def solution(mesh):
    placed = (
        P(("group", "inst"), "tp"),
        P("tp", ("group", "inst"), None),
        P("tp", ("group", "inst"), None, None),
        P("tp", None),
        P("group"),
        P(("group", "inst"), None),
        P("group", None),
    )
    return jax.shard_map(
        on_device, mesh=mesh, in_specs=placed, out_specs=P(("group", "inst"), "tp"), check_vma=False
    )
```

```python
import functools

import jax
import jax.numpy as jnp
from jax import lax
from jax.experimental import pallas as pl
from jax.experimental.pallas import tpu as pltpu
from jax.sharding import PartitionSpec as P

LOG2E = 1.4426950408889634
MASKED = -1e30
GROUP = 8
NEVER = 2**30
PIECES = 2

VMEM = pl.BlockSpec(memory_space=pltpu.VMEM)
SMEM = pl.BlockSpec(memory_space=pltpu.SMEM)
ANY = pl.BlockSpec(memory_space=pl.ANY)


def attend_group(queries, tokens, contexts, live_lengths, step_count):
    count = len(queries)
    head_dim = tokens[0].shape[1] // 2
    head_count = queries[0].shape[1] // head_dim
    rows = head_count * step_count
    gain = LOG2E / head_dim**0.5
    stacked = jnp.concatenate(
        [
            query[:, h * head_dim : (h + 1) * head_dim]
            for query in queries
            for h in range(head_count)
        ],
        axis=0,
    ).astype(jnp.bfloat16)
    tokens = jnp.concatenate(tokens, axis=0).astype(jnp.bfloat16)
    score_new = contract_last(stacked, tokens[:, :head_dim])
    row_ids = lax.broadcasted_iota(jnp.int32, score_new.shape, 0)
    column_ids = lax.broadcasted_iota(jnp.int32, score_new.shape, 1)
    allowed = (row_ids // rows == column_ids // step_count) & (
        column_ids % step_count <= row_ids % step_count
    )
    score_new = jnp.where(allowed, score_new, MASKED)
    new_max = jnp.max(score_new, axis=1, keepdims=True)
    maxima, scores = [], []
    for g in range(count):
        keys = jnp.concatenate([page[:, :head_dim] for page in contexts[g]], axis=0)
        score = contract_last(stacked[g * rows : (g + 1) * rows], keys)
        position = lax.broadcasted_iota(jnp.int32, score.shape, 1)
        score = jnp.where(position < live_lengths[g], score, MASKED)
        scores.append(score)
        maxima.append(
            jnp.maximum(
                jnp.max(score, axis=1, keepdims=True), new_max[g * rows : (g + 1) * rows]
            )
        )
    exp_new = jnp.exp2((score_new - jnp.concatenate(maxima, axis=0)) * gain)
    new_total = jnp.sum(exp_new, axis=1, keepdims=True)
    results, inverses = [], []
    for g in range(count):
        exp_ctx = jnp.exp2((scores[g] - maxima[g]) * gain)
        total = jnp.sum(exp_ctx, axis=1, keepdims=True) + new_total[g * rows : (g + 1) * rows]
        inverse = 1.0 / total
        inverses.append(inverse)
        values = jnp.concatenate([page[:, head_dim:] for page in contexts[g]], axis=0)
        results.append(
            jnp.dot(
                (exp_ctx * inverse).astype(jnp.bfloat16),
                values,
                preferred_element_type=jnp.float32,
            )
        )
    weight_new = (exp_new * jnp.concatenate(inverses, axis=0)).astype(jnp.bfloat16)
    result = jnp.concatenate(results, axis=0) + jnp.dot(
        weight_new, tokens[:, head_dim:], preferred_element_type=jnp.float32
    )
    return [
        jnp.concatenate(
            [
                result[g * rows + h * step_count : g * rows + (h + 1) * step_count]
                for h in range(head_count)
            ],
            axis=1,
        )
        for g in range(count)
    ]


def contract_last(a, b):
    return lax.dot_general(a, b, (((1,), (1,)), ((), ())), preferred_element_type=jnp.float32)


def route_of(migration, own_index, peer, arriving):
    ours, theirs, slot_row = (2, 0, 3) if arriving else (0, 2, 1)
    slot = jnp.int32(0)
    for row in range(migration.shape[1]):
        match = (migration[ours, row] == own_index) & (migration[theirs, row] == peer)
        slot = jnp.where(match, migration[slot_row, row], slot)
    return slot


def arrivals_of(migration, inst_count):
    me = lax.axis_index("inst")
    incoming = migration.shape[1] // inst_count
    slots = [jnp.int32(NEVER)] * incoming
    sources = [jnp.int32(0)] * incoming
    for row in range(migration.shape[1]):
        slot = jnp.where(migration[2, row] == me, migration[3, row], NEVER)
        source = migration[0, row]
        for i in range(incoming):
            before = slot < slots[i]
            slots[i], slot = jnp.where(before, slot, slots[i]), jnp.where(before, slots[i], slot)
            sources[i], source = (
                jnp.where(before, source, sources[i]),
                jnp.where(before, sources[i], source),
            )
    return slots, sources


def slot_at(position, arrivals, slot_count):
    kept = slot_count - len(arrivals)
    if position >= kept:
        return jnp.minimum(arrivals[position - kept], slot_count - 1)
    slot = jnp.int32(position)
    for arrival in arrivals:
        slot = slot + (slot >= arrival).astype(jnp.int32)
    return slot


def peer_of(me, k, count):
    return me ^ k if count & (count - 1) == 0 else (count - me + k) % count


def pack_rows(inst_count, migration, queries, new_tokens, packs):
    me = lax.axis_index("inst")
    width = queries.shape[2]
    for k, pack in packs.items():
        slot = route_of(migration, me, peer_of(me, k, inst_count), True)
        pack[:, :width] = queries[slot]
        pack[:, width:] = new_tokens[slot]


def page_copies(pool, buffer, sems, page_table, item, slot):
    page_count = page_table.shape[0]
    for j in range(page_count):
        pltpu.make_async_copy(
            pool.at[page_table[j, slot]], buffer.at[item, j], sems.at[item]
        ).start()


def wait_copies(pool, buffer, sems, item):
    pltpu.make_async_copy(
        pool.at[pl.ds(0, buffer.shape[1])], buffer.at[item], sems.at[item]
    ).wait()


def away_slot(migration, inst_count, k):
    me = lax.axis_index("inst")
    return route_of(migration, me, peer_of(me, k, inst_count), False)


def away_kernel(
    inst_count, rounds, lengths, page_table, migration, pool, second, weight, *refs
):
    count = len(rounds)
    received, answers = refs[:count], refs[count : 2 * count]
    keep, send, buffer, sems = refs[2 * count :]
    page_count, slot_count = page_table.shape
    step_count, width = answers[0].shape
    first = lax.axis_index("inst") * slot_count
    slots = [away_slot(migration, inst_count, k) for k in rounds]
    for i, slot in enumerate(slots):
        page_copies(pool, buffer, sems, page_table, i, slot)
    project_far(second, weight, keep, send)
    for i in range(count):
        wait_copies(pool, buffer, sems, i)
    result = attend_group(
        [ref[:, :width].astype(jnp.float32) for ref in received],
        [ref[:, width:].astype(jnp.float32) for ref in received],
        [[buffer.at[i, j] for j in range(page_count)] for i in range(count)],
        [lengths[first + slot] * pool.shape[1] for slot in slots],
        step_count,
    )
    for answer, rows in zip(answers, result):
        answer[...] = rows.astype(answer.dtype)


def project(rows, weight, first, columns, target, row_offset=0, offset=0):
    tile = min(512, columns)
    rows = rows[...]
    for j in range(0, columns, tile):
        start = pl.multiple_of(first + j, tile)
        target[row_offset : row_offset + rows.shape[0], offset + j : offset + j + tile] = jnp.dot(
            rows, weight[:, pl.ds(start, tile)], preferred_element_type=jnp.float32
        ).astype(target.dtype)


def project_far(attended, weight, keep, send, stacked=False):
    core = lax.rem(lax.axis_index("tp"), 2)
    chip = lax.axis_index("tp") // 2
    chips = lax.axis_size("tp") // 2
    columns = weight.shape[1] // (2 * chips)
    for target, side in ((send, 1 - core), (keep, core)):
        for d in range(1, chips):
            first = (2 * lax.rem(chip + d, chips) + side) * columns
            row, column = ((d - 1) * attended.shape[0], 0) if stacked else (0, (d - 1) * columns)
            project(attended, weight, first, columns, target, row, column)


def attend_slots(slots, lengths, queries, new_tokens, pages_of, page_len, wait=lambda i: None):
    first = lax.axis_index("inst") * queries.shape[0]
    rows = []
    for base in range(0, len(slots), GROUP):
        items = range(base, min(base + GROUP, len(slots)))
        for i in items:
            wait(i)
        rows += attend_group(
            [queries[slots[i]].astype(jnp.float32) for i in items],
            [new_tokens[slots[i]].astype(jnp.float32) for i in items],
            [pages_of(i) for i in items],
            [lengths[first + slots[i]] * page_len for i in items],
            queries.shape[1],
        )
    return rows


def store_rows(rows, target, at=0):
    step_count = rows[0].shape[0]
    for pair in range(0, len(rows), 2):
        start = at + pair * step_count
        target[start : start + 2 * step_count, :] = jnp.concatenate(
            rows[pair : pair + 2], axis=0
        ).astype(jnp.bfloat16)


def first_kernel(
    inst_count, rounds, migration, lengths, page_table, queries_in, new_in, pool,
    attended, queries, new_tokens, *refs,
):
    packs = dict(zip(rounds, refs))
    buffer, small_sems, page_sems = refs[len(rounds) :]
    slot_count, step_count, _ = queries.shape
    small = [
        pltpu.make_async_copy(queries_in, queries, small_sems.at[0]),
        pltpu.make_async_copy(new_in, new_tokens, small_sems.at[1]),
    ]
    for copy in small:
        copy.start()
    arrivals, _ = arrivals_of(migration, inst_count)
    slots = [
        slot_at(position, arrivals, slot_count)
        for position in range(attended.shape[0] // step_count)
    ]
    for i, slot in enumerate(slots):
        page_copies(pool, buffer, page_sems, page_table, i, slot)
    for copy in small:
        copy.wait()
    pack_rows(inst_count, migration, queries, new_tokens, packs)
    rows = attend_slots(
        slots, lengths, queries, new_tokens,
        lambda i: [buffer.at[i, j] for j in range(buffer.shape[1])],
        buffer.shape[2],
        lambda i: wait_copies(pool, buffer, page_sems, i),
    )
    store_rows(rows, attended)


def far_kernel(attended, weight, keep, send):
    project_far(attended, weight, keep, send)


def second_kernel(
    inst_count, first, migration, lengths, page_table, queries, new_tokens, pool, after,
    attended, extra,
):
    slot_count, step_count, _ = queries.shape
    count = attended.shape[0] // step_count
    arrivals, _ = arrivals_of(migration, inst_count)
    slots = [
        slot_at(first + i, arrivals, slot_count) for i in range(count + extra.shape[0])
    ]
    rows = attend_slots(
        slots, lengths, queries, new_tokens,
        lambda i: [pool.at[page_table[j, slots[i]]] for j in range(page_table.shape[0])],
        pool.shape[1],
    )
    store_rows(rows[:count], attended)
    for i, row in enumerate(rows[count:]):
        extra[i] = row.astype(extra.dtype)


def last_rows_kernel(inst_count, rounds, migration, weight, extra, *refs):
    answers, (rows, keep, send) = refs[:-3], refs[-3:]
    me = lax.axis_index("inst")
    _, sources = arrivals_of(migration, inst_count)
    last = [extra[i].astype(jnp.float32) for i in range(extra.shape[0])]
    given = [answer[...].astype(jnp.float32) for answer in answers]
    for source in sources:
        row = given[0]
        for k, answer in zip(rounds[1:], given[1:]):
            row = jnp.where(source == peer_of(me, k, inst_count), answer, row)
        last.append(row)
    store_rows(last, rows)
    project_far(rows, weight, keep, send, stacked=True)


def own_kernel(weight, first, second, last, after, keep, *refs):
    sends, rows = refs[:-1], refs[-1]
    core = lax.rem(lax.axis_index("tp"), 2)
    pair = lax.axis_index("tp") // 2 * 2
    columns = keep.shape[1]
    at = 0
    for part in (first, second, last):
        rows[at : at + part.shape[0], :] = part[...]
        at += part.shape[0]
    at = 0
    for send in sends:
        project(rows, weight, (pair + 1 - core) * columns + at, send.shape[1], send)
        at += send.shape[1]
    project(rows, weight, (pair + core) * columns, columns, keep)


def sum_kernel(inst_count, chunks, piece_count, migration, keep, *refs):
    mates, parts, (out, staged, sem) = refs[:piece_count], refs[piece_count:-3], refs[-3:]
    slot_count, step_count, _ = out.shape
    pair = 2 * step_count
    width = mates[0].shape[1]
    arrivals, _ = arrivals_of(migration, inst_count)
    share = len(parts) // len(chunks)
    at = 0
    for n, chunk in enumerate(chunks):
        for base in range(0, chunk, pair):
            for m, mate in enumerate(mates):
                columns = slice(m * width, (m + 1) * width)
                total = keep[at : at + pair, columns] + mate[at : at + pair, :].astype(jnp.float32)
                for part in parts[n * share : (n + 1) * share]:
                    total = total + part[base : base + pair, columns].astype(jnp.float32)
                total = total.astype(jnp.bfloat16)
                for half in range(2):
                    staged[at // step_count + half, :, columns] = total[
                        half * step_count : (half + 1) * step_count
                    ]
            at += pair
    scatter_rows(staged, out, arrivals, 0, sem)


def scatter_rows(staged, out, arrivals, first, sem):
    slot_count = out.shape[0]
    for i in range(staged.shape[0]):
        slot = slot_at(first + i, arrivals, slot_count)
        pltpu.make_async_copy(staged.at[i], out.at[slot], sem.at[0]).start()
    pltpu.make_async_copy(staged, out.at[pl.ds(0, staged.shape[0])], sem.at[0]).wait()


def last_kernel(inst_count, first, piece_count, migration, keep, *refs):
    mates, parts, (out, staged, sem) = refs[:piece_count], refs[piece_count:-4], refs[-3:]
    step_count = out.shape[1]
    pair = 2 * step_count
    width = mates[0].shape[1]
    size = parts[0].shape[0]
    arrivals, _ = arrivals_of(migration, inst_count)
    for at in range(0, size, pair):
        own = keep.shape[0] - size + at
        for m, mate in enumerate(mates):
            columns = slice(m * width, (m + 1) * width)
            total = keep[own : own + pair, columns] + mate[own : own + pair, :].astype(jnp.float32)
            for part in parts:
                total = total + part[at : at + pair, columns].astype(jnp.float32)
            total = total.astype(jnp.bfloat16)
            for half in range(2):
                staged[at // step_count + half, :, columns] = total[
                    half * step_count : (half + 1) * step_count
                ]
    scatter_rows(staged, out, arrivals, first, sem)


def in_hbm(value):
    return pltpu.with_memory_space_constraint(value, pltpu.HBM)


def in_vmem(value):
    return pltpu.with_memory_space_constraint(value, pltpu.VMEM)


def on_device(queries, new_kv, kv_pool, out_weight, lengths, page_table, migration):
    inst_count = lax.axis_size("inst")
    tp_count = lax.axis_size("tp")
    chips = tp_count // 2
    slot_count, page_count = page_table.shape
    row_count, width = queries.shape
    step_count = row_count // slot_count
    queries = in_hbm(queries.reshape(slot_count, step_count, width))
    new_tokens = in_hbm(new_kv[0].reshape(slot_count, step_count, new_kv.shape[2]))
    pool = kv_pool[0]
    columns = out_weight.shape[1] // tp_count
    incoming = migration.shape[0] // inst_count
    weight = in_vmem(out_weight)
    lengths = in_hbm(lengths)
    page_table = in_hbm(page_table.T)
    migration = in_hbm(migration.T)
    limit = pltpu.CompilerParams(vmem_limit_bytes=32 * 2**20)
    light = pl.CostEstimate(flops=1, bytes_accessed=1, transcendentals=0)
    bf16, f32 = jnp.bfloat16, jnp.float32
    shape = jax.ShapeDtypeStruct
    swap = [(t, t ^ 1) for t in range(tp_count)]
    far = (chips - 1) * columns

    def hold(values, until):
        return pl.pallas_call(
            lambda *refs: None,
            out_shape=[pltpu.VMEM(value.shape, value.dtype) for value in values],
            in_specs=[ANY] * (len(values) + len(until)),
            out_specs=[ANY] * len(values),
            input_output_aliases={i: i for i in range(len(values))},
            compiler_params=pltpu.CompilerParams(vmem_limit_bytes=2**20),
            cost_estimate=light,
            name="hold",
        )(*[in_vmem(value) for value in values], *until)

    def send_far(summed):
        return [
            lax.ppermute(
                part, "tp", [(t, (t + 2 * d) % tp_count) for t in range(tp_count)]
            )
            for d, part in enumerate(summed, 1)
        ]

    def split_far(summed):
        return [summed[:, d * columns : (d + 1) * columns] for d in range(chips - 1)]

    def chunk_shapes(count):
        rows = count * step_count
        return [pltpu.VMEM((rows, far), f32), pltpu.VMEM((rows, far), bf16)]

    def rows_shape(count):
        return pltpu.VMEM((count * step_count, width), bf16)

    last_count = incoming + incoming % 2
    extra_count = last_count - incoming
    first_count = slot_count // 16 * 9 // 2 * 2
    second_count = slot_count - first_count - last_count
    last_rows = last_count * step_count

    def page_shape(count):
        return pltpu.VMEM((count, page_count, *pool.shape[1:]), bf16)

    dma = pltpu.SemaphoreType.DMA
    rounds = [
        k
        for k in range(inst_count)
        if any(peer_of(i, k, inst_count) != i for i in range(inst_count))
    ]
    pairs = {k: [(i, peer_of(i, k, inst_count)) for i in range(inst_count)] for k in rounds}
    first, queries, new_tokens, *packs = pl.pallas_call(
        functools.partial(first_kernel, inst_count, rounds),
        out_shape=[
            rows_shape(first_count),
            pltpu.VMEM(queries.shape, bf16),
            pltpu.VMEM(new_tokens.shape, bf16),
        ]
        + [shape((step_count, width + new_tokens.shape[2]), bf16)] * len(rounds),
        in_specs=[SMEM, SMEM, SMEM, ANY, ANY, ANY],
        out_specs=[VMEM] * (3 + len(rounds)),
        scratch_shapes=[page_shape(first_count), dma((2,)), dma((first_count,))],
        compiler_params=limit,
        cost_estimate=light,
        name="attend_first",
    )(migration, lengths, page_table, queries, new_tokens, in_hbm(pool))
    first, queries, new_tokens = in_vmem(first), in_vmem(queries), in_vmem(new_tokens)
    keep, send = pl.pallas_call(
        far_kernel,
        out_shape=chunk_shapes(first_count),
        in_specs=[VMEM] * 2,
        out_specs=[VMEM] * 2,
        compiler_params=limit,
        cost_estimate=light,
        name="far_first",
    )(first, weight)
    mate = lax.ppermute(send, "tp", swap)
    summed = (keep + mate.astype(f32)).astype(bf16)
    arrived_first = send_far(split_far(summed))
    packs = hold(packs, [summed])
    received = [lax.ppermute(pack, "inst", pairs[k]) for k, pack in zip(rounds, packs)]

    second, extra = pl.pallas_call(
        functools.partial(second_kernel, inst_count, first_count),
        out_shape=[
            rows_shape(second_count),
            pltpu.VMEM((extra_count, step_count, width), bf16),
        ],
        in_specs=[SMEM, SMEM, SMEM, VMEM, VMEM, VMEM, ANY],
        out_specs=[VMEM] * 2,
        compiler_params=limit,
        cost_estimate=light,
        name="attend_second",
    )(migration, lengths, page_table, queries, new_tokens, in_vmem(pool), summed)
    second = in_vmem(second)
    *answers, keep, send = pl.pallas_call(
        functools.partial(away_kernel, inst_count, rounds),
        out_shape=[shape((step_count, width), bf16)] * len(rounds) + chunk_shapes(second_count),
        in_specs=[SMEM, SMEM, SMEM, ANY] + [VMEM] * (2 + len(rounds)),
        out_specs=[VMEM] * (2 + len(rounds)),
        scratch_shapes=[page_shape(len(rounds)), dma((len(rounds),))],
        compiler_params=limit,
        cost_estimate=light,
        name="attend_away",
    )(lengths, page_table, migration, in_hbm(pool), second, weight, *received)
    mate = lax.ppermute(send, "tp", swap)
    answers = [lax.ppermute(answer, "inst", pairs[k]) for k, answer in zip(rounds, answers)]
    (keep,) = hold([keep], [*arrived_first, *answers])
    summed = (keep + mate.astype(f32)).astype(bf16)
    arrived_second = send_far(split_far(summed))

    last, keep, send = pl.pallas_call(
        functools.partial(last_rows_kernel, inst_count, rounds),
        out_shape=[
            rows_shape(last_count),
            pltpu.VMEM((last_rows * (chips - 1), columns), f32),
            pltpu.VMEM((last_rows * (chips - 1), columns), bf16),
        ],
        in_specs=[SMEM] + [VMEM] * (2 + len(rounds)),
        out_specs=[VMEM] * 3,
        compiler_params=limit,
        cost_estimate=light,
        name="last_rows",
    )(migration, weight, in_vmem(extra), *answers)
    mate = lax.ppermute(send, "tp", swap)
    own_keep, *own_sends = pl.pallas_call(
        own_kernel,
        out_shape=[
            pltpu.VMEM((row_count, columns), f32),
            *[pltpu.VMEM((row_count, columns // PIECES), bf16)] * PIECES,
        ],
        in_specs=[VMEM] * 4 + [ANY],
        out_specs=[VMEM] * (1 + PIECES),
        scratch_shapes=[pltpu.VMEM((row_count, width), bf16)],
        compiler_params=limit,
        cost_estimate=light,
        name="own_columns",
    )(weight, first, second, in_vmem(last), summed)
    own_keep = in_vmem(own_keep)
    own_mates = [lax.ppermute(own_send, "tp", swap) for own_send in own_sends]
    (keep,) = hold([keep], [*arrived_second, own_keep])
    summed = (keep + mate.astype(f32)).astype(bf16)
    arrived_last = send_far([summed[d * last_rows : (d + 1) * last_rows] for d in range(chips - 1)])

    early = slot_count - last_count
    out_shape = (slot_count, step_count, columns)
    out = pl.pallas_call(
        functools.partial(
            sum_kernel, inst_count, [first_count * step_count, second_count * step_count], PIECES
        ),
        out_shape=pltpu.HBM(out_shape, bf16),
        in_specs=[SMEM] + [VMEM] * (1 + PIECES + 2 * (chips - 1)),
        out_specs=ANY,
        scratch_shapes=[pltpu.VMEM((early, step_count, columns), bf16), dma((1,))],
        compiler_params=limit,
        cost_estimate=light,
        name="sum_early",
    )(migration, own_keep, *own_mates, *arrived_first, *arrived_second)
    out = pl.pallas_call(
        functools.partial(last_kernel, inst_count, early, PIECES),
        out_shape=pltpu.HBM(out_shape, bf16),
        in_specs=[SMEM] + [VMEM] * (PIECES + chips) + [ANY],
        out_specs=ANY,
        scratch_shapes=[pltpu.VMEM((last_count, step_count, columns), bf16), dma((1,))],
        input_output_aliases={PIECES + chips + 1: 0},
        compiler_params=limit,
        cost_estimate=light,
        name="sum_last",
    )(migration, own_keep, *own_mates, *arrived_last, out)
    return out.reshape(row_count, columns)


def solution(mesh):
    placed = (
        P(("group", "inst"), "tp"),
        P("tp", ("group", "inst"), None),
        P("tp", ("group", "inst"), None, None),
        P("tp", None),
        P("group"),
        P(("group", "inst"), None),
        P("group", None),
    )
    return jax.shard_map(
        on_device, mesh=mesh, in_specs=placed, out_specs=P(("group", "inst"), "tp"), check_vma=False
    )
```

```python
import functools

import jax
import jax.numpy as jnp
from jax import lax
from jax.experimental import pallas as pl
from jax.experimental.pallas import tpu as pltpu
from jax.sharding import PartitionSpec as P

LOG2E = 1.4426950408889634
MASKED = -1e30
GROUP = 16
NEVER = 2**30
PIECES = 2

VMEM = pl.BlockSpec(memory_space=pltpu.VMEM)
SMEM = pl.BlockSpec(memory_space=pltpu.SMEM)
ANY = pl.BlockSpec(memory_space=pl.ANY)


def attend_group(queries, tokens, contexts, live_lengths, step_count):
    count = len(queries)
    head_dim = tokens[0].shape[1] // 2
    head_count = queries[0].shape[1] // head_dim
    rows = head_count * step_count
    gain = LOG2E / head_dim**0.5
    stacked = jnp.concatenate(
        [
            query[:, h * head_dim : (h + 1) * head_dim]
            for query in queries
            for h in range(head_count)
        ],
        axis=0,
    ).astype(jnp.bfloat16)
    tokens = jnp.concatenate(tokens, axis=0).astype(jnp.bfloat16)
    score_new = contract_last(stacked, tokens[:, :head_dim])
    row_ids = lax.broadcasted_iota(jnp.int32, score_new.shape, 0)
    column_ids = lax.broadcasted_iota(jnp.int32, score_new.shape, 1)
    allowed = (row_ids // rows == column_ids // step_count) & (
        column_ids % step_count <= row_ids % step_count
    )
    score_new = jnp.where(allowed, score_new, MASKED)
    new_max = jnp.max(score_new, axis=1, keepdims=True)
    maxima, scores = [], []
    for g in range(count):
        keys = jnp.concatenate([page[:, :head_dim] for page in contexts[g]], axis=0)
        score = contract_last(stacked[g * rows : (g + 1) * rows], keys)
        position = lax.broadcasted_iota(jnp.int32, score.shape, 1)
        score = jnp.where(position < live_lengths[g], score, MASKED)
        scores.append(score)
        maxima.append(
            jnp.maximum(
                jnp.max(score, axis=1, keepdims=True), new_max[g * rows : (g + 1) * rows]
            )
        )
    exp_new = jnp.exp2((score_new - jnp.concatenate(maxima, axis=0)) * gain)
    new_total = jnp.sum(exp_new, axis=1, keepdims=True)
    results, inverses = [], []
    for g in range(count):
        exp_ctx = jnp.exp2((scores[g] - maxima[g]) * gain)
        total = jnp.sum(exp_ctx, axis=1, keepdims=True) + new_total[g * rows : (g + 1) * rows]
        inverse = 1.0 / total
        inverses.append(inverse)
        values = jnp.concatenate([page[:, head_dim:] for page in contexts[g]], axis=0)
        results.append(
            jnp.dot(
                (exp_ctx * inverse).astype(jnp.bfloat16),
                values,
                preferred_element_type=jnp.float32,
            )
        )
    weight_new = (exp_new * jnp.concatenate(inverses, axis=0)).astype(jnp.bfloat16)
    result = jnp.concatenate(results, axis=0) + jnp.dot(
        weight_new, tokens[:, head_dim:], preferred_element_type=jnp.float32
    )
    return [
        jnp.concatenate(
            [
                result[g * rows + h * step_count : g * rows + (h + 1) * step_count]
                for h in range(head_count)
            ],
            axis=1,
        )
        for g in range(count)
    ]


def contract_last(a, b):
    return lax.dot_general(a, b, (((1,), (1,)), ((), ())), preferred_element_type=jnp.float32)


def route_of(migration, own_index, peer, arriving):
    ours, theirs, slot_row = (2, 0, 3) if arriving else (0, 2, 1)
    slot = jnp.int32(0)
    for row in range(migration.shape[1]):
        match = (migration[ours, row] == own_index) & (migration[theirs, row] == peer)
        slot = jnp.where(match, migration[slot_row, row], slot)
    return slot


def arrivals_of(migration, inst_count):
    me = lax.axis_index("inst")
    incoming = migration.shape[1] // inst_count
    slots = [jnp.int32(NEVER)] * incoming
    sources = [jnp.int32(0)] * incoming
    for row in range(migration.shape[1]):
        slot = jnp.where(migration[2, row] == me, migration[3, row], NEVER)
        source = migration[0, row]
        for i in range(incoming):
            before = slot < slots[i]
            slots[i], slot = jnp.where(before, slot, slots[i]), jnp.where(before, slots[i], slot)
            sources[i], source = (
                jnp.where(before, source, sources[i]),
                jnp.where(before, sources[i], source),
            )
    return slots, sources


def slot_at(position, arrivals, slot_count):
    kept = slot_count - len(arrivals)
    if position >= kept:
        return jnp.minimum(arrivals[position - kept], slot_count - 1)
    slot = jnp.int32(position)
    for arrival in arrivals:
        slot = slot + (slot >= arrival).astype(jnp.int32)
    return slot


def peer_of(me, k, count):
    return me ^ k if count & (count - 1) == 0 else (count - me + k) % count


def pack_rows(inst_count, migration, queries, new_tokens, packs):
    me = lax.axis_index("inst")
    width = queries.shape[2]
    for k, pack in packs.items():
        slot = route_of(migration, me, peer_of(me, k, inst_count), True)
        pack[:, :width] = queries[slot]
        pack[:, width:] = new_tokens[slot]


def page_copies(pool, buffer, sems, page_table, item, slot):
    page_count = page_table.shape[0]
    for j in range(page_count):
        pltpu.make_async_copy(
            pool.at[page_table[j, slot]], buffer.at[item, j], sems.at[item]
        ).start()


def wait_copies(pool, buffer, sems, item):
    pltpu.make_async_copy(
        pool.at[pl.ds(0, buffer.shape[1])], buffer.at[item], sems.at[item]
    ).wait()


def away_slot(migration, inst_count, k):
    me = lax.axis_index("inst")
    return route_of(migration, me, peer_of(me, k, inst_count), False)


def away_kernel(
    inst_count, rounds, lengths, page_table, migration, pool, second, weight, *refs
):
    count = len(rounds)
    received, answers = refs[:count], refs[count : 2 * count]
    keep, send, buffer, sems = refs[2 * count :]
    page_count, slot_count = page_table.shape
    step_count, width = answers[0].shape
    first = lax.axis_index("inst") * slot_count
    slots = [away_slot(migration, inst_count, k) for k in rounds]
    for i, slot in enumerate(slots):
        page_copies(pool, buffer, sems, page_table, i, slot)
    project_far(second, weight, keep, send)
    for i in range(count):
        wait_copies(pool, buffer, sems, i)
    result = attend_group(
        [ref[:, :width].astype(jnp.float32) for ref in received],
        [ref[:, width:].astype(jnp.float32) for ref in received],
        [[buffer.at[i, j] for j in range(page_count)] for i in range(count)],
        [lengths[first + slot] * pool.shape[1] for slot in slots],
        step_count,
    )
    for answer, rows in zip(answers, result):
        answer[...] = rows.astype(answer.dtype)


def project(rows, weight, first, columns, target, row_offset=0, offset=0):
    tile = min(512, columns)
    rows = rows[...]
    for j in range(0, columns, tile):
        start = pl.multiple_of(first + j, tile)
        target[row_offset : row_offset + rows.shape[0], offset + j : offset + j + tile] = jnp.dot(
            rows, weight[:, pl.ds(start, tile)], preferred_element_type=jnp.float32
        ).astype(target.dtype)


def project_far(attended, weight, keep, send, stacked=False):
    core = lax.rem(lax.axis_index("tp"), 2)
    chip = lax.axis_index("tp") // 2
    chips = lax.axis_size("tp") // 2
    columns = weight.shape[1] // (2 * chips)
    for target, side in ((send, 1 - core), (keep, core)):
        for d in range(1, chips):
            first = (2 * lax.rem(chip + d, chips) + side) * columns
            row, column = ((d - 1) * attended.shape[0], 0) if stacked else (0, (d - 1) * columns)
            project(attended, weight, first, columns, target, row, column)


def attend_slots(slots, lengths, queries, new_tokens, pages_of, page_len, wait=lambda i: None):
    first = lax.axis_index("inst") * queries.shape[0]
    rows = []
    for base in range(0, len(slots), GROUP):
        items = range(base, min(base + GROUP, len(slots)))
        for i in items:
            wait(i)
        rows += attend_group(
            [queries[slots[i]].astype(jnp.float32) for i in items],
            [new_tokens[slots[i]].astype(jnp.float32) for i in items],
            [pages_of(i) for i in items],
            [lengths[first + slots[i]] * page_len for i in items],
            queries.shape[1],
        )
    return rows


def store_rows(rows, target, at=0):
    step_count = rows[0].shape[0]
    for pair in range(0, len(rows), 2):
        start = at + pair * step_count
        target[start : start + 2 * step_count, :] = jnp.concatenate(
            rows[pair : pair + 2], axis=0
        ).astype(jnp.bfloat16)


def first_kernel(
    inst_count, rounds, migration, lengths, page_table, queries_in, new_in, pool,
    attended, queries, new_tokens, *refs,
):
    packs = dict(zip(rounds, refs))
    buffer, small_sems, page_sems = refs[len(rounds) :]
    slot_count, step_count, _ = queries.shape
    small = [
        pltpu.make_async_copy(queries_in, queries, small_sems.at[0]),
        pltpu.make_async_copy(new_in, new_tokens, small_sems.at[1]),
    ]
    for copy in small:
        copy.start()
    arrivals, _ = arrivals_of(migration, inst_count)
    slots = [
        slot_at(position, arrivals, slot_count)
        for position in range(attended.shape[0] // step_count)
    ]
    for i, slot in enumerate(slots):
        page_copies(pool, buffer, page_sems, page_table, i, slot)
    for copy in small:
        copy.wait()
    pack_rows(inst_count, migration, queries, new_tokens, packs)
    rows = attend_slots(
        slots, lengths, queries, new_tokens,
        lambda i: [buffer.at[i, j] for j in range(buffer.shape[1])],
        buffer.shape[2],
        lambda i: wait_copies(pool, buffer, page_sems, i),
    )
    store_rows(rows, attended)


def far_kernel(attended, weight, keep, send):
    project_far(attended, weight, keep, send)


def second_kernel(
    inst_count, first, migration, lengths, page_table, queries, new_tokens, pool, after,
    attended, extra,
):
    slot_count, step_count, _ = queries.shape
    count = attended.shape[0] // step_count
    arrivals, _ = arrivals_of(migration, inst_count)
    slots = [
        slot_at(first + i, arrivals, slot_count) for i in range(count + extra.shape[0])
    ]
    rows = attend_slots(
        slots, lengths, queries, new_tokens,
        lambda i: [pool.at[page_table[j, slots[i]]] for j in range(page_table.shape[0])],
        pool.shape[1],
    )
    store_rows(rows[:count], attended)
    for i, row in enumerate(rows[count:]):
        extra[i] = row.astype(extra.dtype)


def last_rows_kernel(inst_count, rounds, migration, weight, extra, after, *refs):
    answers, (keep, send, rows) = refs[:-3], refs[-3:]
    me = lax.axis_index("inst")
    _, sources = arrivals_of(migration, inst_count)
    last = [extra[i].astype(jnp.float32) for i in range(extra.shape[0])]
    given = [answer[...].astype(jnp.float32) for answer in answers]
    for source in sources:
        row = given[0]
        for k, answer in zip(rounds[1:], given[1:]):
            row = jnp.where(source == peer_of(me, k, inst_count), answer, row)
        last.append(row)
    store_rows(last, rows)
    core = lax.rem(lax.axis_index("tp"), 2)
    chip = lax.axis_index("tp") // 2
    chips = lax.axis_size("tp") // 2
    columns = keep.shape[1]
    for target, side in ((send, 1 - core), (keep, core)):
        for d in range(1, chips + 1):
            first = (2 * lax.rem(chip + d, chips) + side) * columns
            project(rows, weight, first, columns, target, (d - 1) * rows.shape[0])


def own_kernel(weight, first, second, after, keep, *refs):
    sends, rows = refs[:-1], refs[-1]
    core = lax.rem(lax.axis_index("tp"), 2)
    pair = lax.axis_index("tp") // 2 * 2
    columns = keep.shape[1]
    rows[: first.shape[0], :] = first[...]
    rows[first.shape[0] :, :] = second[...]
    at = 0
    for send in sends:
        project(rows, weight, (pair + 1 - core) * columns + at, send.shape[1], send)
        at += send.shape[1]
    project(rows, weight, (pair + core) * columns, columns, keep)


def sum_kernel(inst_count, chunks, piece_count, migration, keep, *refs):
    mates, parts, (out, staged, sem) = refs[:piece_count], refs[piece_count:-3], refs[-3:]
    slot_count, step_count, _ = out.shape
    pair = 2 * step_count
    width = mates[0].shape[1]
    arrivals, _ = arrivals_of(migration, inst_count)
    share = len(parts) // len(chunks)
    at = 0
    for n, chunk in enumerate(chunks):
        for base in range(0, chunk, pair):
            for m, mate in enumerate(mates):
                columns = slice(m * width, (m + 1) * width)
                total = keep[at : at + pair, columns] + mate[at : at + pair, :].astype(jnp.float32)
                for part in parts[n * share : (n + 1) * share]:
                    total = total + part[base : base + pair, columns].astype(jnp.float32)
                total = total.astype(jnp.bfloat16)
                for half in range(2):
                    staged[at // step_count + half, :, columns] = total[
                        half * step_count : (half + 1) * step_count
                    ]
            at += pair
    scatter_rows(staged, out, arrivals, 0, sem)


def scatter_rows(staged, out, arrivals, first, sem):
    slot_count = out.shape[0]
    for i in range(staged.shape[0]):
        slot = slot_at(first + i, arrivals, slot_count)
        pltpu.make_async_copy(staged.at[i], out.at[slot], sem.at[0]).start()
    pltpu.make_async_copy(staged, out.at[pl.ds(0, staged.shape[0])], sem.at[0]).wait()


def last_kernel(inst_count, first, migration, keep, mate, *refs):
    parts, (out, staged, sem) = refs[:-4], refs[-3:]
    step_count = out.shape[1]
    pair = 2 * step_count
    size = parts[0].shape[0]
    arrivals, _ = arrivals_of(migration, inst_count)
    for at in range(0, size, pair):
        own = keep.shape[0] - size + at
        total = keep[own : own + pair, :] + mate[own : own + pair, :].astype(jnp.float32)
        for part in parts:
            total = total + part[at : at + pair, :].astype(jnp.float32)
        total = total.astype(jnp.bfloat16)
        for half in range(2):
            staged[at // step_count + half] = total[half * step_count : (half + 1) * step_count]
    scatter_rows(staged, out, arrivals, first, sem)


def in_hbm(value):
    return pltpu.with_memory_space_constraint(value, pltpu.HBM)


def in_vmem(value):
    return pltpu.with_memory_space_constraint(value, pltpu.VMEM)


def on_device(queries, new_kv, kv_pool, out_weight, lengths, page_table, migration):
    inst_count = lax.axis_size("inst")
    tp_count = lax.axis_size("tp")
    chips = tp_count // 2
    slot_count, page_count = page_table.shape
    row_count, width = queries.shape
    step_count = row_count // slot_count
    queries = in_hbm(queries.reshape(slot_count, step_count, width))
    new_tokens = in_hbm(new_kv[0].reshape(slot_count, step_count, new_kv.shape[2]))
    pool = kv_pool[0]
    columns = out_weight.shape[1] // tp_count
    incoming = migration.shape[0] // inst_count
    weight = in_vmem(out_weight)
    lengths = in_hbm(lengths)
    page_table = in_hbm(page_table.T)
    migration = in_hbm(migration.T)
    limit = pltpu.CompilerParams(vmem_limit_bytes=32 * 2**20)
    light = pl.CostEstimate(flops=1, bytes_accessed=1, transcendentals=0)
    bf16, f32 = jnp.bfloat16, jnp.float32
    shape = jax.ShapeDtypeStruct
    swap = [(t, t ^ 1) for t in range(tp_count)]
    far = (chips - 1) * columns

    def hold(values, until):
        return pl.pallas_call(
            lambda *refs: None,
            out_shape=[pltpu.VMEM(value.shape, value.dtype) for value in values],
            in_specs=[ANY] * (len(values) + len(until)),
            out_specs=[ANY] * len(values),
            input_output_aliases={i: i for i in range(len(values))},
            compiler_params=pltpu.CompilerParams(vmem_limit_bytes=2**20),
            cost_estimate=light,
            name="hold",
        )(*[in_vmem(value) for value in values], *until)

    def send_far(summed):
        return [
            lax.ppermute(
                part, "tp", [(t, (t + 2 * d) % tp_count) for t in range(tp_count)]
            )
            for d, part in enumerate(summed, 1)
        ]

    def split_far(summed):
        return [summed[:, d * columns : (d + 1) * columns] for d in range(chips - 1)]

    def chunk_shapes(count):
        rows = count * step_count
        return [pltpu.VMEM((rows, far), f32), pltpu.VMEM((rows, far), bf16)]

    def rows_shape(count):
        return pltpu.VMEM((count * step_count, width), bf16)

    last_count = incoming + incoming % 2
    extra_count = last_count - incoming
    first_count = slot_count // 4 * 2
    second_count = slot_count - first_count - last_count
    last_rows = last_count * step_count

    def page_shape(count):
        return pltpu.VMEM((count, page_count, *pool.shape[1:]), bf16)

    dma = pltpu.SemaphoreType.DMA
    rounds = [
        k
        for k in range(inst_count)
        if any(peer_of(i, k, inst_count) != i for i in range(inst_count))
    ]
    pairs = {k: [(i, peer_of(i, k, inst_count)) for i in range(inst_count)] for k in rounds}
    first, queries, new_tokens, *packs = pl.pallas_call(
        functools.partial(first_kernel, inst_count, rounds),
        out_shape=[
            rows_shape(first_count),
            pltpu.VMEM(queries.shape, bf16),
            pltpu.VMEM(new_tokens.shape, bf16),
        ]
        + [shape((step_count, width + new_tokens.shape[2]), bf16)] * len(rounds),
        in_specs=[SMEM, SMEM, SMEM, ANY, ANY, ANY],
        out_specs=[VMEM] * (3 + len(rounds)),
        scratch_shapes=[page_shape(first_count), dma((2,)), dma((first_count,))],
        compiler_params=limit,
        cost_estimate=light,
        name="attend_first",
    )(migration, lengths, page_table, queries, new_tokens, in_hbm(pool))
    first, queries, new_tokens = in_vmem(first), in_vmem(queries), in_vmem(new_tokens)
    keep, send = pl.pallas_call(
        far_kernel,
        out_shape=chunk_shapes(first_count),
        in_specs=[VMEM] * 2,
        out_specs=[VMEM] * 2,
        compiler_params=limit,
        cost_estimate=light,
        name="far_first",
    )(first, weight)
    mate = lax.ppermute(send, "tp", swap)
    summed = (keep + mate.astype(f32)).astype(bf16)
    arrived_first = send_far(split_far(summed))
    packs = hold(packs, [summed])
    received = [lax.ppermute(pack, "inst", pairs[k]) for k, pack in zip(rounds, packs)]

    second, extra = pl.pallas_call(
        functools.partial(second_kernel, inst_count, first_count),
        out_shape=[
            rows_shape(second_count),
            pltpu.VMEM((extra_count, step_count, width), bf16),
        ],
        in_specs=[SMEM, SMEM, SMEM, VMEM, VMEM, VMEM, ANY],
        out_specs=[VMEM] * 2,
        compiler_params=limit,
        cost_estimate=light,
        name="attend_second",
    )(migration, lengths, page_table, queries, new_tokens, in_vmem(pool), summed)
    second = in_vmem(second)
    *answers, keep, send = pl.pallas_call(
        functools.partial(away_kernel, inst_count, rounds),
        out_shape=[shape((step_count, width), bf16)] * len(rounds) + chunk_shapes(second_count),
        in_specs=[SMEM, SMEM, SMEM, ANY] + [VMEM] * (2 + len(rounds)),
        out_specs=[VMEM] * (2 + len(rounds)),
        scratch_shapes=[page_shape(len(rounds)), dma((len(rounds),))],
        compiler_params=limit,
        cost_estimate=light,
        name="attend_away",
    )(lengths, page_table, migration, in_hbm(pool), second, weight, *received)
    mate = lax.ppermute(send, "tp", swap)
    answers = [lax.ppermute(answer, "inst", pairs[k]) for k, answer in zip(rounds, answers)]
    (keep,) = hold([keep], arrived_first)
    summed = (keep + mate.astype(f32)).astype(bf16)
    arrived_second = send_far(split_far(summed))

    early_rows = (first_count + second_count) * step_count
    pieces = PIECES
    early_keep, *early_sends = pl.pallas_call(
        own_kernel,
        out_shape=[
            pltpu.VMEM((early_rows, columns), f32),
            *[pltpu.VMEM((early_rows, columns // pieces), bf16)] * pieces,
        ],
        in_specs=[VMEM, VMEM, VMEM, ANY],
        out_specs=[VMEM] * (1 + pieces),
        scratch_shapes=[pltpu.VMEM((early_rows, width), bf16)],
        compiler_params=limit,
        cost_estimate=light,
        name="own_columns",
    )(weight, first, second, summed)
    early_mates = [lax.ppermute(early_send, "tp", swap) for early_send in early_sends]

    keep, send = pl.pallas_call(
        functools.partial(last_rows_kernel, inst_count, rounds),
        out_shape=[
            pltpu.VMEM((last_rows * chips, columns), f32),
            pltpu.VMEM((last_rows * chips, columns), bf16),
        ],
        in_specs=[SMEM] + [VMEM] * 2 + [ANY] + [VMEM] * len(rounds),
        out_specs=[VMEM] * 2,
        scratch_shapes=[pltpu.VMEM((last_rows, width), bf16)],
        compiler_params=limit,
        cost_estimate=light,
        name="last_rows",
    )(migration, weight, in_vmem(extra), early_keep, *answers)
    mate = lax.ppermute(send, "tp", swap)
    (keep,) = hold([keep], arrived_second)
    summed = (keep[:-last_rows] + mate[:-last_rows].astype(f32)).astype(bf16)
    arrived_last = send_far([summed[d * last_rows : (d + 1) * last_rows] for d in range(chips - 1)])

    early = slot_count - last_count
    out_shape = (slot_count, step_count, columns)
    out = pl.pallas_call(
        functools.partial(
            sum_kernel, inst_count, [first_count * step_count, second_count * step_count], pieces
        ),
        out_shape=pltpu.HBM(out_shape, bf16),
        in_specs=[SMEM] + [VMEM] * (1 + pieces + 2 * (chips - 1)),
        out_specs=ANY,
        scratch_shapes=[
            pltpu.VMEM((early, step_count, columns), bf16),
            pltpu.SemaphoreType.DMA((1,)),
        ],
        compiler_params=limit,
        cost_estimate=light,
        name="sum_early",
    )(migration, in_vmem(early_keep), *early_mates, *arrived_first, *arrived_second)
    out = pl.pallas_call(
        functools.partial(last_kernel, inst_count, early),
        out_shape=pltpu.HBM(out_shape, bf16),
        in_specs=[SMEM] + [VMEM] * (chips + 1) + [ANY],
        out_specs=ANY,
        scratch_shapes=[
            pltpu.VMEM((last_count, step_count, columns), bf16),
            pltpu.SemaphoreType.DMA((1,)),
        ],
        input_output_aliases={2 + chips: 0},
        compiler_params=limit,
        cost_estimate=light,
        name="sum_last",
    )(migration, in_vmem(keep), mate, *arrived_last, out)
    return out.reshape(row_count, columns)


def solution(mesh):
    placed = (
        P(("group", "inst"), "tp"),
        P("tp", ("group", "inst"), None),
        P("tp", ("group", "inst"), None, None),
        P("tp", None),
        P("group"),
        P(("group", "inst"), None),
        P("group", None),
    )
    return jax.shard_map(
        on_device, mesh=mesh, in_specs=placed, out_specs=P(("group", "inst"), "tp"), check_vma=False
    )
```

```python
import functools

import jax
import jax.numpy as jnp
from jax import lax
from jax.experimental import pallas as pl
from jax.experimental.pallas import tpu as pltpu
from jax.sharding import PartitionSpec as P

LOG2E = 1.4426950408889634
MASKED = -1e30
GROUP = 16
NEVER = 2**30
PIECES = 2

VMEM = pl.BlockSpec(memory_space=pltpu.VMEM)
SMEM = pl.BlockSpec(memory_space=pltpu.SMEM)
ANY = pl.BlockSpec(memory_space=pl.ANY)


def attend_group(queries, tokens, contexts, live_lengths, step_count):
    count = len(queries)
    head_dim = tokens[0].shape[1] // 2
    head_count = queries[0].shape[1] // head_dim
    rows = head_count * step_count
    gain = LOG2E / head_dim**0.5
    stacked = jnp.concatenate(
        [
            query[:, h * head_dim : (h + 1) * head_dim]
            for query in queries
            for h in range(head_count)
        ],
        axis=0,
    ).astype(jnp.bfloat16)
    tokens = jnp.concatenate(tokens, axis=0).astype(jnp.bfloat16)
    score_new = contract_last(stacked, tokens[:, :head_dim])
    row_ids = lax.broadcasted_iota(jnp.int32, score_new.shape, 0)
    column_ids = lax.broadcasted_iota(jnp.int32, score_new.shape, 1)
    allowed = (row_ids // rows == column_ids // step_count) & (
        column_ids % step_count <= row_ids % step_count
    )
    score_new = jnp.where(allowed, score_new, MASKED)
    new_max = jnp.max(score_new, axis=1, keepdims=True)
    maxima, scores = [], []
    for g in range(count):
        keys = jnp.concatenate([page[:, :head_dim] for page in contexts[g]], axis=0)
        score = contract_last(stacked[g * rows : (g + 1) * rows], keys)
        position = lax.broadcasted_iota(jnp.int32, score.shape, 1)
        score = jnp.where(position < live_lengths[g], score, MASKED)
        scores.append(score)
        maxima.append(
            jnp.maximum(
                jnp.max(score, axis=1, keepdims=True), new_max[g * rows : (g + 1) * rows]
            )
        )
    exp_new = jnp.exp2((score_new - jnp.concatenate(maxima, axis=0)) * gain)
    new_total = jnp.sum(exp_new, axis=1, keepdims=True)
    results, inverses = [], []
    for g in range(count):
        exp_ctx = jnp.exp2((scores[g] - maxima[g]) * gain)
        total = jnp.sum(exp_ctx, axis=1, keepdims=True) + new_total[g * rows : (g + 1) * rows]
        inverse = 1.0 / total
        inverses.append(inverse)
        values = jnp.concatenate([page[:, head_dim:] for page in contexts[g]], axis=0)
        results.append(
            jnp.dot(
                (exp_ctx * inverse).astype(jnp.bfloat16),
                values,
                preferred_element_type=jnp.float32,
            )
        )
    weight_new = (exp_new * jnp.concatenate(inverses, axis=0)).astype(jnp.bfloat16)
    result = jnp.concatenate(results, axis=0) + jnp.dot(
        weight_new, tokens[:, head_dim:], preferred_element_type=jnp.float32
    )
    return [
        jnp.concatenate(
            [
                result[g * rows + h * step_count : g * rows + (h + 1) * step_count]
                for h in range(head_count)
            ],
            axis=1,
        )
        for g in range(count)
    ]


def contract_last(a, b):
    return lax.dot_general(a, b, (((1,), (1,)), ((), ())), preferred_element_type=jnp.float32)


def route_of(migration, own_index, peer, arriving):
    ours, theirs, slot_row = (2, 0, 3) if arriving else (0, 2, 1)
    slot = jnp.int32(0)
    for row in range(migration.shape[1]):
        match = (migration[ours, row] == own_index) & (migration[theirs, row] == peer)
        slot = jnp.where(match, migration[slot_row, row], slot)
    return slot


def arrivals_of(migration, inst_count):
    me = lax.axis_index("inst")
    incoming = migration.shape[1] // inst_count
    slots = [jnp.int32(NEVER)] * incoming
    sources = [jnp.int32(0)] * incoming
    for row in range(migration.shape[1]):
        slot = jnp.where(migration[2, row] == me, migration[3, row], NEVER)
        source = migration[0, row]
        for i in range(incoming):
            before = slot < slots[i]
            slots[i], slot = jnp.where(before, slot, slots[i]), jnp.where(before, slots[i], slot)
            sources[i], source = (
                jnp.where(before, source, sources[i]),
                jnp.where(before, sources[i], source),
            )
    return slots, sources


def slot_at(position, arrivals, slot_count):
    kept = slot_count - len(arrivals)
    if position >= kept:
        return jnp.minimum(arrivals[position - kept], slot_count - 1)
    slot = jnp.int32(position)
    for arrival in arrivals:
        slot = slot + (slot >= arrival).astype(jnp.int32)
    return slot


def peer_of(me, k, count):
    return me ^ k if count & (count - 1) == 0 else (count - me + k) % count


def pack_rows(inst_count, migration, queries, new_tokens, packs):
    me = lax.axis_index("inst")
    width = queries.shape[2]
    for k, pack in packs.items():
        slot = route_of(migration, me, peer_of(me, k, inst_count), True)
        pack[:, :width] = queries[slot]
        pack[:, width:] = new_tokens[slot]


def page_copies(pool, buffer, sems, page_table, item, slot):
    page_count = page_table.shape[0]
    for j in range(page_count):
        pltpu.make_async_copy(
            pool.at[page_table[j, slot]], buffer.at[item, j], sems.at[item]
        ).start()


def wait_copies(pool, buffer, sems, item):
    pltpu.make_async_copy(
        pool.at[pl.ds(0, buffer.shape[1])], buffer.at[item], sems.at[item]
    ).wait()


def away_slot(migration, inst_count, k):
    me = lax.axis_index("inst")
    return route_of(migration, me, peer_of(me, k, inst_count), False)


def away_kernel(
    inst_count, rounds, lengths, page_table, migration, pool, second, weight, *refs
):
    count = len(rounds)
    received, answers = refs[:count], refs[count : 2 * count]
    keep, send, buffer, sems = refs[2 * count :]
    page_count, slot_count = page_table.shape
    step_count, width = answers[0].shape
    first = lax.axis_index("inst") * slot_count
    slots = [away_slot(migration, inst_count, k) for k in rounds]
    for i, slot in enumerate(slots):
        page_copies(pool, buffer, sems, page_table, i, slot)
    project_far(second, weight, keep, send)
    for i in range(count):
        wait_copies(pool, buffer, sems, i)
    result = attend_group(
        [ref[:, :width].astype(jnp.float32) for ref in received],
        [ref[:, width:].astype(jnp.float32) for ref in received],
        [[buffer.at[i, j] for j in range(page_count)] for i in range(count)],
        [lengths[first + slot] * pool.shape[1] for slot in slots],
        step_count,
    )
    for answer, rows in zip(answers, result):
        answer[...] = rows.astype(answer.dtype)


def project(rows, weight, first, columns, target, row_offset=0, offset=0):
    tile = min(512, columns)
    rows = rows[...]
    for j in range(0, columns, tile):
        start = pl.multiple_of(first + j, tile)
        target[row_offset : row_offset + rows.shape[0], offset + j : offset + j + tile] = jnp.dot(
            rows, weight[:, pl.ds(start, tile)], preferred_element_type=jnp.float32
        ).astype(target.dtype)


def project_far(attended, weight, keep, send, stacked=False):
    core = lax.rem(lax.axis_index("tp"), 2)
    chip = lax.axis_index("tp") // 2
    chips = lax.axis_size("tp") // 2
    columns = weight.shape[1] // (2 * chips)
    for target, side in ((send, 1 - core), (keep, core)):
        for d in range(1, chips):
            first = (2 * lax.rem(chip + d, chips) + side) * columns
            row, column = ((d - 1) * attended.shape[0], 0) if stacked else (0, (d - 1) * columns)
            project(attended, weight, first, columns, target, row, column)


def attend_slots(slots, lengths, queries, new_tokens, pages_of, page_len, wait=lambda i: None):
    first = lax.axis_index("inst") * queries.shape[0]
    rows = []
    for base in range(0, len(slots), GROUP):
        items = range(base, min(base + GROUP, len(slots)))
        for i in items:
            wait(i)
        rows += attend_group(
            [queries[slots[i]].astype(jnp.float32) for i in items],
            [new_tokens[slots[i]].astype(jnp.float32) for i in items],
            [pages_of(i) for i in items],
            [lengths[first + slots[i]] * page_len for i in items],
            queries.shape[1],
        )
    return rows


def store_rows(rows, target, at=0):
    step_count = rows[0].shape[0]
    for pair in range(0, len(rows), 2):
        start = at + pair * step_count
        target[start : start + 2 * step_count, :] = jnp.concatenate(
            rows[pair : pair + 2], axis=0
        ).astype(jnp.bfloat16)


def first_kernel(
    inst_count, rounds, migration, lengths, page_table, queries_in, new_in, pool,
    attended, queries, new_tokens, *refs,
):
    packs = dict(zip(rounds, refs))
    buffer, small_sems, page_sems = refs[len(rounds) :]
    slot_count, step_count, _ = queries.shape
    small = [
        pltpu.make_async_copy(queries_in, queries, small_sems.at[0]),
        pltpu.make_async_copy(new_in, new_tokens, small_sems.at[1]),
    ]
    for copy in small:
        copy.start()
    arrivals, _ = arrivals_of(migration, inst_count)
    slots = [
        slot_at(position, arrivals, slot_count)
        for position in range(attended.shape[0] // step_count)
    ]
    for i, slot in enumerate(slots):
        page_copies(pool, buffer, page_sems, page_table, i, slot)
    for copy in small:
        copy.wait()
    pack_rows(inst_count, migration, queries, new_tokens, packs)
    rows = attend_slots(
        slots, lengths, queries, new_tokens,
        lambda i: [buffer.at[i, j] for j in range(buffer.shape[1])],
        buffer.shape[2],
        lambda i: wait_copies(pool, buffer, page_sems, i),
    )
    store_rows(rows, attended)


def far_kernel(attended, weight, keep, send):
    project_far(attended, weight, keep, send)


def second_kernel(
    inst_count, first, migration, lengths, page_table, queries, new_tokens, pool, after,
    attended, extra,
):
    slot_count, step_count, _ = queries.shape
    count = attended.shape[0] // step_count
    arrivals, _ = arrivals_of(migration, inst_count)
    slots = [
        slot_at(first + i, arrivals, slot_count) for i in range(count + extra.shape[0])
    ]
    rows = attend_slots(
        slots, lengths, queries, new_tokens,
        lambda i: [pool.at[page_table[j, slots[i]]] for j in range(page_table.shape[0])],
        pool.shape[1],
    )
    store_rows(rows[:count], attended)
    for i, row in enumerate(rows[count:]):
        extra[i] = row.astype(extra.dtype)


def last_rows_kernel(inst_count, rounds, migration, weight, extra, after, *refs):
    answers, (rows, keep, send) = refs[:-3], refs[-3:]
    me = lax.axis_index("inst")
    _, sources = arrivals_of(migration, inst_count)
    last = [extra[i].astype(jnp.float32) for i in range(extra.shape[0])]
    given = [answer[...].astype(jnp.float32) for answer in answers]
    for source in sources:
        row = given[0]
        for k, answer in zip(rounds[1:], given[1:]):
            row = jnp.where(source == peer_of(me, k, inst_count), answer, row)
        last.append(row)
    store_rows(last, rows)
    project_far(rows, weight, keep, send, stacked=True)


def near_rows_kernel(weight, rows, keep, send):
    core = lax.rem(lax.axis_index("tp"), 2)
    pair = lax.axis_index("tp") // 2 * 2
    columns = keep.shape[1]
    for target, side in ((send, 1 - core), (keep, core)):
        project(rows, weight, (pair + side) * columns, columns, target)


def own_kernel(weight, first, second, after, keep, *refs):
    sends, rows = refs[:-1], refs[-1]
    core = lax.rem(lax.axis_index("tp"), 2)
    pair = lax.axis_index("tp") // 2 * 2
    columns = keep.shape[1]
    rows[: first.shape[0], :] = first[...]
    rows[first.shape[0] :, :] = second[...]
    at = 0
    for send in sends:
        project(rows, weight, (pair + 1 - core) * columns + at, send.shape[1], send)
        at += send.shape[1]
    project(rows, weight, (pair + core) * columns, columns, keep)


def sum_kernel(inst_count, chunks, piece_count, migration, keep, *refs):
    mates, parts, (out, staged, sem) = refs[:piece_count], refs[piece_count:-3], refs[-3:]
    slot_count, step_count, _ = out.shape
    pair = 2 * step_count
    width = mates[0].shape[1]
    arrivals, _ = arrivals_of(migration, inst_count)
    share = len(parts) // len(chunks)
    at = 0
    for n, chunk in enumerate(chunks):
        for base in range(0, chunk, pair):
            for m, mate in enumerate(mates):
                columns = slice(m * width, (m + 1) * width)
                total = keep[at : at + pair, columns] + mate[at : at + pair, :].astype(jnp.float32)
                for part in parts[n * share : (n + 1) * share]:
                    total = total + part[base : base + pair, columns].astype(jnp.float32)
                total = total.astype(jnp.bfloat16)
                for half in range(2):
                    staged[at // step_count + half, :, columns] = total[
                        half * step_count : (half + 1) * step_count
                    ]
            at += pair
    scatter_rows(staged, out, arrivals, 0, sem)


def scatter_rows(staged, out, arrivals, first, sem):
    slot_count = out.shape[0]
    for i in range(staged.shape[0]):
        slot = slot_at(first + i, arrivals, slot_count)
        pltpu.make_async_copy(staged.at[i], out.at[slot], sem.at[0]).start()
    pltpu.make_async_copy(staged, out.at[pl.ds(0, staged.shape[0])], sem.at[0]).wait()


def last_kernel(inst_count, first, migration, keep, mate, *refs):
    parts, (out, staged, sem) = refs[:-4], refs[-3:]
    step_count = out.shape[1]
    pair = 2 * step_count
    size = parts[0].shape[0]
    arrivals, _ = arrivals_of(migration, inst_count)
    for at in range(0, size, pair):
        own = keep.shape[0] - size + at
        total = keep[own : own + pair, :] + mate[own : own + pair, :].astype(jnp.float32)
        for part in parts:
            total = total + part[at : at + pair, :].astype(jnp.float32)
        total = total.astype(jnp.bfloat16)
        for half in range(2):
            staged[at // step_count + half] = total[half * step_count : (half + 1) * step_count]
    scatter_rows(staged, out, arrivals, first, sem)


def in_hbm(value):
    return pltpu.with_memory_space_constraint(value, pltpu.HBM)


def in_vmem(value):
    return pltpu.with_memory_space_constraint(value, pltpu.VMEM)


def on_device(queries, new_kv, kv_pool, out_weight, lengths, page_table, migration):
    inst_count = lax.axis_size("inst")
    tp_count = lax.axis_size("tp")
    chips = tp_count // 2
    slot_count, page_count = page_table.shape
    row_count, width = queries.shape
    step_count = row_count // slot_count
    queries = in_hbm(queries.reshape(slot_count, step_count, width))
    new_tokens = in_hbm(new_kv[0].reshape(slot_count, step_count, new_kv.shape[2]))
    pool = kv_pool[0]
    columns = out_weight.shape[1] // tp_count
    incoming = migration.shape[0] // inst_count
    weight = in_vmem(out_weight)
    lengths = in_hbm(lengths)
    page_table = in_hbm(page_table.T)
    migration = in_hbm(migration.T)
    limit = pltpu.CompilerParams(vmem_limit_bytes=32 * 2**20)
    light = pl.CostEstimate(flops=1, bytes_accessed=1, transcendentals=0)
    bf16, f32 = jnp.bfloat16, jnp.float32
    shape = jax.ShapeDtypeStruct
    swap = [(t, t ^ 1) for t in range(tp_count)]
    far = (chips - 1) * columns

    def hold(values, until):
        return pl.pallas_call(
            lambda *refs: None,
            out_shape=[pltpu.VMEM(value.shape, value.dtype) for value in values],
            in_specs=[ANY] * (len(values) + len(until)),
            out_specs=[ANY] * len(values),
            input_output_aliases={i: i for i in range(len(values))},
            compiler_params=pltpu.CompilerParams(vmem_limit_bytes=2**20),
            cost_estimate=light,
            name="hold",
        )(*[in_vmem(value) for value in values], *until)

    def send_far(summed):
        return [
            lax.ppermute(
                part, "tp", [(t, (t + 2 * d) % tp_count) for t in range(tp_count)]
            )
            for d, part in enumerate(summed, 1)
        ]

    def split_far(summed):
        return [summed[:, d * columns : (d + 1) * columns] for d in range(chips - 1)]

    def chunk_shapes(count):
        rows = count * step_count
        return [pltpu.VMEM((rows, far), f32), pltpu.VMEM((rows, far), bf16)]

    def rows_shape(count):
        return pltpu.VMEM((count * step_count, width), bf16)

    last_count = incoming + incoming % 2
    extra_count = last_count - incoming
    first_count = slot_count // 4 * 2
    second_count = slot_count - first_count - last_count
    last_rows = last_count * step_count

    def page_shape(count):
        return pltpu.VMEM((count, page_count, *pool.shape[1:]), bf16)

    dma = pltpu.SemaphoreType.DMA
    rounds = [
        k
        for k in range(inst_count)
        if any(peer_of(i, k, inst_count) != i for i in range(inst_count))
    ]
    pairs = {k: [(i, peer_of(i, k, inst_count)) for i in range(inst_count)] for k in rounds}
    first, queries, new_tokens, *packs = pl.pallas_call(
        functools.partial(first_kernel, inst_count, rounds),
        out_shape=[
            rows_shape(first_count),
            pltpu.VMEM(queries.shape, bf16),
            pltpu.VMEM(new_tokens.shape, bf16),
        ]
        + [shape((step_count, width + new_tokens.shape[2]), bf16)] * len(rounds),
        in_specs=[SMEM, SMEM, SMEM, ANY, ANY, ANY],
        out_specs=[VMEM] * (3 + len(rounds)),
        scratch_shapes=[page_shape(first_count), dma((2,)), dma((first_count,))],
        compiler_params=limit,
        cost_estimate=light,
        name="attend_first",
    )(migration, lengths, page_table, queries, new_tokens, in_hbm(pool))
    first, queries, new_tokens = in_vmem(first), in_vmem(queries), in_vmem(new_tokens)
    keep, send = pl.pallas_call(
        far_kernel,
        out_shape=chunk_shapes(first_count),
        in_specs=[VMEM] * 2,
        out_specs=[VMEM] * 2,
        compiler_params=limit,
        cost_estimate=light,
        name="far_first",
    )(first, weight)
    mate = lax.ppermute(send, "tp", swap)
    summed = (keep + mate.astype(f32)).astype(bf16)
    arrived_first = send_far(split_far(summed))
    packs = hold(packs, [summed])
    received = [lax.ppermute(pack, "inst", pairs[k]) for k, pack in zip(rounds, packs)]

    second, extra = pl.pallas_call(
        functools.partial(second_kernel, inst_count, first_count),
        out_shape=[
            rows_shape(second_count),
            pltpu.VMEM((extra_count, step_count, width), bf16),
        ],
        in_specs=[SMEM, SMEM, SMEM, VMEM, VMEM, VMEM, ANY],
        out_specs=[VMEM] * 2,
        compiler_params=limit,
        cost_estimate=light,
        name="attend_second",
    )(migration, lengths, page_table, queries, new_tokens, in_vmem(pool), summed)
    second = in_vmem(second)
    *answers, keep, send = pl.pallas_call(
        functools.partial(away_kernel, inst_count, rounds),
        out_shape=[shape((step_count, width), bf16)] * len(rounds) + chunk_shapes(second_count),
        in_specs=[SMEM, SMEM, SMEM, ANY] + [VMEM] * (2 + len(rounds)),
        out_specs=[VMEM] * (2 + len(rounds)),
        scratch_shapes=[page_shape(len(rounds)), dma((len(rounds),))],
        compiler_params=limit,
        cost_estimate=light,
        name="attend_away",
    )(lengths, page_table, migration, in_hbm(pool), second, weight, *received)
    mate = lax.ppermute(send, "tp", swap)
    answers = [lax.ppermute(answer, "inst", pairs[k]) for k, answer in zip(rounds, answers)]
    (keep,) = hold([keep], arrived_first)
    summed = (keep + mate.astype(f32)).astype(bf16)
    arrived_second = send_far(split_far(summed))

    early_rows = (first_count + second_count) * step_count
    pieces = PIECES
    early_keep, *early_sends = pl.pallas_call(
        own_kernel,
        out_shape=[
            pltpu.VMEM((early_rows, columns), f32),
            *[pltpu.VMEM((early_rows, columns // pieces), bf16)] * pieces,
        ],
        in_specs=[VMEM, VMEM, VMEM, ANY],
        out_specs=[VMEM] * (1 + pieces),
        scratch_shapes=[pltpu.VMEM((early_rows, width), bf16)],
        compiler_params=limit,
        cost_estimate=light,
        name="own_columns",
    )(weight, first, second, summed)
    early_mates = [lax.ppermute(early_send, "tp", swap) for early_send in early_sends]

    last, keep, send = pl.pallas_call(
        functools.partial(last_rows_kernel, inst_count, rounds),
        out_shape=[
            rows_shape(last_count),
            pltpu.VMEM((last_rows * (chips - 1), columns), f32),
            pltpu.VMEM((last_rows * (chips - 1), columns), bf16),
        ],
        in_specs=[SMEM] + [VMEM] * 2 + [ANY] + [VMEM] * len(rounds),
        out_specs=[VMEM] * 3,
        compiler_params=limit,
        cost_estimate=light,
        name="last_rows",
    )(migration, weight, in_vmem(extra), early_keep, *answers)
    mate = lax.ppermute(send, "tp", swap)
    near_keep, near_send = pl.pallas_call(
        near_rows_kernel,
        out_shape=[
            pltpu.VMEM((last_rows, columns), f32),
            pltpu.VMEM((last_rows, columns), bf16),
        ],
        in_specs=[VMEM] * 2,
        out_specs=[VMEM] * 2,
        compiler_params=limit,
        cost_estimate=light,
        name="near_rows",
    )(weight, in_vmem(last))
    near_mate = lax.ppermute(near_send, "tp", swap)
    (keep,) = hold([keep], arrived_second)
    summed = (keep + mate.astype(f32)).astype(bf16)
    arrived_last = send_far([summed[d * last_rows : (d + 1) * last_rows] for d in range(chips - 1)])

    early = slot_count - last_count
    out_shape = (slot_count, step_count, columns)
    out = pl.pallas_call(
        functools.partial(
            sum_kernel, inst_count, [first_count * step_count, second_count * step_count], pieces
        ),
        out_shape=pltpu.HBM(out_shape, bf16),
        in_specs=[SMEM] + [VMEM] * (1 + pieces + 2 * (chips - 1)),
        out_specs=ANY,
        scratch_shapes=[
            pltpu.VMEM((early, step_count, columns), bf16),
            pltpu.SemaphoreType.DMA((1,)),
        ],
        compiler_params=limit,
        cost_estimate=light,
        name="sum_early",
    )(migration, in_vmem(early_keep), *early_mates, *arrived_first, *arrived_second)
    out = pl.pallas_call(
        functools.partial(last_kernel, inst_count, early),
        out_shape=pltpu.HBM(out_shape, bf16),
        in_specs=[SMEM] + [VMEM] * (chips + 1) + [ANY],
        out_specs=ANY,
        scratch_shapes=[
            pltpu.VMEM((last_count, step_count, columns), bf16),
            pltpu.SemaphoreType.DMA((1,)),
        ],
        input_output_aliases={2 + chips: 0},
        compiler_params=limit,
        cost_estimate=light,
        name="sum_last",
    )(migration, in_vmem(near_keep), near_mate, *arrived_last, out)
    return out.reshape(row_count, columns)


def solution(mesh):
    placed = (
        P(("group", "inst"), "tp"),
        P("tp", ("group", "inst"), None),
        P("tp", ("group", "inst"), None, None),
        P("tp", None),
        P("group"),
        P(("group", "inst"), None),
        P("group", None),
    )
    return jax.shard_map(
        on_device, mesh=mesh, in_specs=placed, out_specs=P(("group", "inst"), "tp"), check_vma=False
    )
```
